32 devices in a mesh: req: 4 (over y, x), blk: 8 (over z, core).
Axes of the slice: x: 2, y: 2, z: 4, core: 2. Of those that a mesh axis runs over, the one named last changes fastest.
Arguments:
- new_states: bfloat16 [2048, 1024], P('req'), may hold values from -50 to 50
- encoder_out: bfloat16 [2048, 1024], P('req'), may hold values from -90 to 90
- cache_in: bfloat16 [4, 4096, 2048], P(None, 'blk', 'req'), may hold values from -90 to 90
- slot_order: int32 [4], replicated, may hold values from 0 to 3, each once
- new_lengths: int32 [4], replicated, may hold values from 1 to 512, 1280 in all
- cache_lengths: int32 [4], replicated, may hold values from 1 to 4096, 8192 in all
- enc_lengths: int32 [4], replicated, may hold values from 1 to 512, 1536 in all
- bucket_of: int32 [4608], replicated, may hold values from 0 to 31, as said below
- rel_bias: float32 [32, 16], replicated, may hold values from -4 to 4
- norm_gain: float32 [3, 1024], replicated, may hold values from 0.25 to 1.75
- self_q: bfloat16 [1024, 1024], P('req', 'blk'), may hold values from -0.09375 to 0.09375
- self_kv: bfloat16 [1024, 2, 1024], P('req', None, 'blk'), may hold values from -0.1875 to 0.1875
- self_out: bfloat16 [1024, 1024], P('blk', 'req'), may hold values from -0.1875 to 0.1875
- cross_q: bfloat16 [1024, 1024], P('req', 'blk'), may hold values from -0.09375 to 0.09375
- cross_kv: bfloat16 [1024, 2, 1024], P('req', None, 'blk'), may hold values from -0.1875 to 0.1875
- cross_out: bfloat16 [1024, 1024], P('blk', 'req'), may hold values from -0.1875 to 0.1875
- ff_in: bfloat16 [1024, 2, 2816], P('req', None, 'blk'), may hold values from -0.1875 to 0.1875
- ff_out: bfloat16 [2816, 1024], P('blk', 'req'), may hold values from -0.109375 to 0.109375
Outputs:
- layer_out: bfloat16 [2048, 1024], P('req')
- cache_out: bfloat16 [4, 4096, 2048], P('req', None, 'blk')
The draws below stay inside these ranges and needn't reach their ends.
Inputs may be any that keep to these rules, and one draw needn't show every extreme that they name: Slot s holds request slot_order[s]; every request is held once. `new_lengths`: they sum to 1280 and the most is 512. `cache_lengths`: they sum to 8192 and the most is 4096. `enc_lengths`: they sum to 1536 and the most is 512. `bucket_of`: non-decreasing in the distance, 0 at distance 0 and 31 at distance 4608 - 1.
All inputs are finite; a program needn't handle non-finite values.
Results may differ from the reference program's by a relative error of at most 0.035.
Values may be sent and summed in bfloat16 or wider, within the bound.
No kernel may reach another device: no remote copies, remote signals or barrier semaphores. Data moves between devices by JAX's collectives and lax.ppermute only.
A program may use at most 128 MiB of HBM per device.

```python
import math
import jax
import jax.numpy as jnp
import numpy as np
from jax import lax

D = 1024
H = 16
HD = 64
FF = 2816
NBUCKET = 32
Q = 512
CTX = 4096
ENC = 512
REQUESTS = 4
ROWS = 2048
ENC_ROWS = 2048
SPAN = 4608
N_BLK = 8


def draw_new_states(key, part):
    first, second, third = jax.random.split(key, 3)
    col_scale = jnp.exp(jax.random.uniform(third, (1, D), jnp.float32, -1.15, 1.15))
    base = jnp.clip(jax.random.normal(first, (ROWS, D), jnp.float32), -5.0, 5.0)
    row_scale = jnp.exp(jax.random.uniform(second, (ROWS, 1), jnp.float32, -1.15, 1.15))
    return (base * row_scale * col_scale).astype(jnp.bfloat16)


def draw_encoder_out(key, part):
    first = jax.random.fold_in(key, 0)
    third = jax.random.fold_in(key, 2)
    col_scale = jnp.exp(jax.random.uniform(third, (1, D), jnp.float32, -0.7, 0.7))
    base = jnp.clip(jax.random.normal(first, (ENC_ROWS, D), jnp.float32), -5.0, 5.0) * col_scale
    return base.astype(jnp.bfloat16)


def draw_cache_in(key, part):
    first = jax.random.fold_in(key, 0)
    base = jnp.clip(jax.random.normal(first, (REQUESTS, CTX, H, 2, HD), jnp.float32), -5.0, 5.0)
    return base.reshape(REQUESTS, CTX, H * 2 * HD).astype(jnp.bfloat16)


def draw_bucket_of(key, part):
    distance = jnp.arange(SPAN, dtype=jnp.int32)
    rolled = jax.random.randint(key, (SPAN,), 0, jnp.maximum(distance, 1))
    stepped = jnp.where(distance < 8, jnp.where(distance > 0, 1, 0), jnp.where(rolled < 4, 1, 0)).astype(jnp.int32)
    counted = jnp.cumsum(stepped).astype(jnp.int32)
    counted = jnp.where(distance == SPAN - 1, NBUCKET - 1, counted)
    return jnp.minimum(counted, NBUCKET - 1).astype(jnp.int32)


def shard_levels(stream_key, dims, shards, least, top_value):
    level, own = 1.0, jax.random.fold_in(stream_key, 6)
    for dim, blocks in shards:
        steps = jnp.exp(jax.random.uniform(jax.random.fold_in(own, dim), (blocks,), jnp.float32, least / len(shards), top_value / len(shards)))
        level = level * jnp.repeat(steps, dims[dim] // blocks).reshape([-1 if axis == dim else 1 for axis in range(len(dims))])
    return level


def length_profile(count, total, most, lean):
    loads = [(1 << 20) // math.isqrt(rank ** lean) + 1 for rank in range(2, count + 1)]
    rest, given = total - most - (count - 1), [1] * (count - 1)
    while rest > 0:
        movable = [i for i in range(count - 1) if given[i] < most]
        pool, left = sum([loads[i] for i in movable]), rest
        for i in movable:
            extra = min(most - given[i], max(1, left * loads[i] // pool), rest)
            given[i] = given[i] + extra
            rest = rest - extra
    return np.array([most] + given)


def ragged_sizes(key, amount, total, bound, slope):
    if amount == 2:
        one = jax.random.randint(key, (), max(1, total - bound), min(bound, total - 1) + 1)
        return jnp.stack([one, total - one])
    sizes = jnp.asarray(length_profile(amount, total, bound, slope), jnp.int32)
    twos = (amount - 1) // 2
    giver, sink = sizes[1:1 + 2 * twos:2], sizes[2:2 + 2 * twos:2]
    slack = jnp.minimum(giver - 1, bound - sink)
    shifted = jax.random.randint(jax.random.fold_in(key, 1), (twos,), 0, 1 << 20) % (slack + 1)
    sizes = sizes.at[1:1 + 2 * twos:2].set(giver - shifted).at[2:2 + 2 * twos:2].set(sink + shifted)
    return sizes[jax.random.permutation(jax.random.fold_in(key, 2), amount)]


def normal_values(stream_key, extent, scale, limit, pieces=(), held_as=jnp.bfloat16):
    result = scale * jax.random.normal(stream_key, extent, jnp.float32)
    if pieces:
        result = result * shard_levels(stream_key, extent, pieces, -0.22, 0.18)
    return jnp.clip(result, -limit, limit).astype(held_as)


def setup_inputs(seed: int = 0) -> dict:
    seeds = jax.random.split(jax.random.key(seed), 19)
    return {
        "new_states": draw_new_states(jax.random.fold_in(seeds[18], 71), 0),
        "encoder_out": draw_encoder_out(jax.random.fold_in(seeds[18], 71), 0),
        "cache_in": draw_cache_in(jax.random.fold_in(seeds[18], 71), 0),
        "slot_order": jax.random.permutation(seeds[3], REQUESTS).astype(jnp.int32),
        "new_lengths": ragged_sizes(seeds[4], REQUESTS, 5 * REQUESTS * Q // 8, Q, 2).astype(jnp.int32),
        "cache_lengths": ragged_sizes(seeds[5], REQUESTS, REQUESTS * CTX // 2, CTX, 2).astype(jnp.int32),
        "enc_lengths": ragged_sizes(seeds[6], REQUESTS, 3 * REQUESTS * ENC // 4, ENC, 1).astype(jnp.int32),
        "bucket_of": draw_bucket_of(jax.random.fold_in(seeds[18], 71), 0),
        "rel_bias": normal_values(seeds[8], (NBUCKET, H), 1.0, 4.0, (), jnp.float32),
        "norm_gain": jnp.clip(1.0 + 0.15 * jax.random.normal(seeds[9], (3, D), jnp.float32), 0.25, 1.75),
        "self_q": normal_values(seeds[10], (D, H * HD), (4 * D) ** -0.5, 0.09375, ((0, 4), (1, 8))),
        "self_kv": normal_values(seeds[11], (D, 2, H * HD), D ** -0.5, 0.1875, ((0, 4), (2, 8))),
        "self_out": normal_values(seeds[12], (H * HD, D), (H * HD) ** -0.5, 0.1875, ((0, 8), (1, 4))),
        "cross_q": normal_values(seeds[13], (D, H * HD), (4 * D) ** -0.5, 0.09375, ((0, 4), (1, 8))),
        "cross_kv": normal_values(seeds[14], (D, 2, H * HD), D ** -0.5, 0.1875, ((0, 4), (2, 8))),
        "cross_out": normal_values(seeds[15], (H * HD, D), (H * HD) ** -0.5, 0.1875, ((0, 8), (1, 4))),
        "ff_in": normal_values(seeds[16], (D, 2, FF), D ** -0.5, 0.1875, ((0, 4), (2, 8))),
        "ff_out": normal_values(seeds[17], (FF, D), FF ** -0.5, 0.109375, ((0, 8), (1, 4))),
    }


EPSILON = 1e-06
NEG_FILL = -1e+30

def rms_rows(row_block, gain):
    mean_square = lax.optimization_barrier(jnp.mean(row_block * row_block, axis=-1, keepdims=True))
    return (row_block * lax.rsqrt(mean_square + EPSILON) * gain).astype(jnp.bfloat16)

def softmax_rows(scores):
    row_top = lax.optimization_barrier(jnp.max(scores, axis=-1, keepdims=True))
    weights = jnp.exp(scores - row_top)
    return (weights / lax.optimization_barrier(jnp.sum(weights, axis=-1, keepdims=True))).astype(jnp.bfloat16)

def group_product(left_side, right_side, groups):
    row_count = left_side.shape[0]
    left_groups = left_side.reshape(row_count, groups, -1).astype(jnp.float32)
    right_groups = right_side.reshape(groups, -1, right_side.shape[1]).astype(jnp.float32)
    partials = jnp.einsum('tgk,gkd->tgd', left_groups, right_groups)
    rounded = lax.optimization_barrier(partials.astype(jnp.bfloat16))
    return lax.optimization_barrier(jnp.sum(rounded.astype(jnp.float32), axis=1))

def reference(new_states, encoder_out, cache_in, slot_order, new_lengths, cache_lengths, enc_lengths, bucket_of, rel_bias, norm_gain, self_q, self_kv, self_out, cross_q, cross_kv, cross_out, ff_in, ff_out):
    cache_out = jnp.take(cache_in, slot_order, axis=0)
    onehot = (bucket_of[:, None] == jnp.arange(NBUCKET, dtype=jnp.int32)[None, :]).astype(jnp.float32)
    bias_dist = jnp.dot(onehot, rel_bias, precision=lax.Precision.HIGHEST).T
    slot_new = jnp.take(new_lengths, slot_order)
    slot_old = jnp.take(cache_lengths, slot_order)
    slot_enc = jnp.take(enc_lengths, slot_order)
    positions = jnp.arange(Q, dtype=jnp.int32)
    cached_ids = jnp.arange(CTX, dtype=jnp.int32)
    encoder_ids = jnp.arange(ENC, dtype=jnp.int32)

    def one_slot(request):
        slot_id, fresh_len, old_len, enc_len = request
        states = lax.dynamic_slice_in_dim(new_states, (slot_id * Q).astype(jnp.int32), Q, 0).astype(jnp.float32)
        encoder_rows = lax.dynamic_slice_in_dim(encoder_out, (slot_id * ENC).astype(jnp.int32), ENC, 0)
        cache_rows = lax.dynamic_index_in_dim(cache_out, slot_id, 0, keepdims=False).reshape(CTX, H, 2, HD)
        normed = rms_rows(states, norm_gain[0])
        queries = jnp.dot(normed, self_q, preferred_element_type=jnp.float32).astype(jnp.bfloat16).reshape(Q, H, HD)
        key_value = jnp.einsum('td,dcn->tcn', normed.astype(jnp.float32), self_kv.astype(jnp.float32)).astype(jnp.bfloat16).reshape(Q, 2, H, HD)
        old_dist = jnp.clip(old_len + positions[:, None] - cached_ids[None, :], 0, SPAN - 1)
        old_scores = jnp.einsum('qhe,khe->hqk', queries.astype(jnp.float32), cache_rows[:, :, 0].astype(jnp.float32))
        old_scores = old_scores + bias_dist[:, old_dist]
        old_scores = jnp.where((cached_ids < old_len)[None, None, :], old_scores, NEG_FILL)
        fresh_dist = jnp.clip(positions[:, None] - positions[None, :], 0, SPAN - 1)
        fresh_scores = jnp.einsum('qhe,khe->hqk', queries.astype(jnp.float32), key_value[:, 0].astype(jnp.float32))
        fresh_scores = fresh_scores + bias_dist[:, fresh_dist]
        admitted = (positions[None, :] <= positions[:, None]) & (positions[None, :] < fresh_len)
        fresh_scores = jnp.where(admitted[None], fresh_scores, NEG_FILL)
        weights = softmax_rows(jnp.concatenate([old_scores, fresh_scores], axis=2))
        value_all = jnp.concatenate([cache_rows[:, :, 1], key_value[:, 1]], axis=0)
        context = jnp.einsum('hqk,khe->qhe', weights.astype(jnp.float32), value_all.astype(jnp.float32)).astype(jnp.bfloat16)
        states = states + group_product(context.reshape(Q, H * HD), self_out, N_BLK)
        normed = rms_rows(states, norm_gain[1])
        queries = jnp.dot(normed, cross_q, preferred_element_type=jnp.float32).astype(jnp.bfloat16).reshape(Q, H, HD)
        enc_pair = jnp.einsum('td,dcn->tcn', encoder_rows.astype(jnp.float32), cross_kv.astype(jnp.float32)).astype(jnp.bfloat16).reshape(ENC, 2, H, HD)
        scores = jnp.einsum('qhe,khe->hqk', queries.astype(jnp.float32), enc_pair[:, 0].astype(jnp.float32))
        scores = jnp.where((encoder_ids < enc_len)[None, None, :], scores, NEG_FILL)
        weights = softmax_rows(scores)
        context = jnp.einsum('hqk,khe->qhe', weights.astype(jnp.float32), enc_pair[:, 1].astype(jnp.float32)).astype(jnp.bfloat16)
        states = states + group_product(context.reshape(Q, H * HD), cross_out, N_BLK)
        normed = rms_rows(states, norm_gain[2])
        gate_up = jnp.einsum('td,dcf->tcf', normed.astype(jnp.float32), ff_in.astype(jnp.float32))
        hidden = (jax.nn.gelu(gate_up[:, 0], approximate=True) * gate_up[:, 1]).astype(jnp.bfloat16)
        states = states + group_product(hidden, ff_out, N_BLK)
        return states.astype(jnp.bfloat16)
    outputs = lax.map(one_slot, (jnp.arange(REQUESTS, dtype=jnp.int32), slot_new, slot_old, slot_enc))
    return (outputs.reshape(REQUESTS * Q, D), cache_out)
```

```python
import functools

import jax
import jax.numpy as jnp
from jax import lax
from jax.experimental import pallas as pl
from jax.experimental.pallas import tpu as pltpu
from jax.sharding import PartitionSpec as P

H = 16
HD = 64
EPSILON = 1e-06
NEG_FILL = -1e30
TILE = 128
F32 = jnp.float32
BF16 = jnp.bfloat16


def pick(table, place):
    matches = place == jnp.arange(table.shape[0], dtype=jnp.int32)
    return jnp.sum(jnp.where(matches, table, 0))


def xor_send(value, axis, step):
    size = lax.axis_size(axis)
    return lax.ppermute(value, axis, [(i, i ^ step) for i in range(size)])


def far_first(count):
    return [0, *range(count // 2, count), *range(1, count // 2)]


def chip_sends(parts):
    moved = [parts[0]] + [None] * (len(parts) - 1)
    for k in far_first(len(parts))[1:]:
        moved[k] = xor_send(parts[k], "blk", 2 * k)
    return moved


def reordered(parts):
    return [parts[k] for k in far_first(len(parts))]


def restored(parts):
    found = [None] * len(parts)
    for part, k in zip(parts, far_first(len(parts))):
        found[k] = part
    return found


VMEM = pl.BlockSpec(memory_space=pltpu.VMEM)
SMEM = pl.BlockSpec(memory_space=pltpu.SMEM)


def local_call(kernel, operands, outs, smem=0, scratch=(), flops=0, transcendentals=0):
    moved = sum(x.size * x.dtype.itemsize for x in list(operands) + list(outs))
    return pl.pallas_call(
        kernel,
        out_shape=list(outs),
        in_specs=[SMEM] * smem + [VMEM] * (len(operands) - smem),
        out_specs=[VMEM] * len(outs),
        scratch_shapes=list(scratch),
        compiler_params=pltpu.CompilerParams(vmem_limit_bytes=32 << 20),
        cost_estimate=pl.CostEstimate(
            flops=flops, bytes_accessed=moved, transcendentals=transcendentals
        ),
    )(*operands)


def shaped(shape, dtype=BF16):
    return jax.ShapeDtypeStruct(tuple(shape), dtype)


def after(value, *others):
    return lax.optimization_barrier((value,) + others)[0]


def place_kernel(order, *refs):
    parts, out = refs[:-1], refs[-1]
    for k, part in enumerate(parts):
        size = part.shape[0]
        out[pl.ds(pl.multiple_of(order(k) * size, size), size), :] = part[...]


def place(parts, order):
    rows, cols = parts[0].shape
    out = shaped((len(parts) * rows, cols))
    return local_call(functools.partial(place_kernel, order), parts, [out])[0]


def req_stack(value, moved, stride):
    def order(k):
        return (lax.axis_index("req") // stride) % 2 ^ k

    return place([value, moved], order)


def part_owner(part, strides):
    owner = 0
    for i, stride in enumerate(strides):
        owner += stride * ((part >> i) & 1)
    return owner


def pack_projection(query, pair, out, at):
    depth = query.shape[0]
    value = pair[1]
    out[at : at + depth, :] = jnp.concatenate([query[...], pair[0]], axis=1)
    tail = jnp.concatenate([value[: depth // 2], value[depth // 2 :]], axis=1)
    out[at + depth : at + depth + depth // 2, :] = tail


def packed_projection(ref, at, depth, width):
    head = ref[at : at + depth, :]
    tail = ref[at + depth : at + depth + depth // 2, :]
    value = jnp.concatenate([tail[:, :width], tail[:, width:]], axis=0)
    return head[:, :width], head[:, width:], value


def pack_kernel(*refs):
    q1, kv1, q2, kv2, ff, o1, o2, o3, first, mid, wide, wide_ref = refs
    depth = q1.shape[0]
    done = depth + depth // 2
    pack_projection(q1, kv1, first, 0)
    first[done:, :] = o1[...]
    pack_projection(q2, kv2, mid, 0)
    mid[done:, :] = o2[...]
    span = wide_ref.shape[1] // 2
    wide_ref[...] = jnp.zeros(wide_ref.shape, wide_ref.dtype)
    wide_ref[:, : ff.shape[2]] = ff[0]
    wide_ref[:, span : span + ff.shape[2]] = ff[1]
    lanes = wide.shape[1]
    for block in range(wide_ref.shape[1] // lanes):
        wide[block * depth : (block + 1) * depth, :] = wide_ref[
            :, block * lanes : (block + 1) * lanes
        ]
    wide[wide.shape[0] - o3.shape[0] :, :] = o3[...]


def join_kernel(taken, first, *outs):
    tokens = outs[0].shape[0]
    outs[0][...] = taken[:tokens, :]
    for k, out in enumerate(outs[1:], 1):
        out[:tokens, :] = taken[k * tokens : (k + 1) * tokens, :]
        out[tokens:, :] = first[...]


def project_kernel(tokens, heads_dev, states_ref, gain_ref, first, *refs):
    parts, (query_ref, fresh_ref, share_ref, normed_ref) = refs[:-4], refs[-4:]
    states = states_ref[...].astype(F32)
    mean_square = jnp.mean(states * states, axis=-1, keepdims=True)
    normed = states * lax.rsqrt(mean_square + EPSILON) * gain_ref[0:1, :]
    normed_ref[...] = normed.astype(BF16)
    size = share_ref.shape[0]
    blk = lax.axis_index("blk")
    spot = lax.rem(blk, 2) * (states.shape[0] // (2 * size)) + blk // 2
    share_ref[...] = states_ref[pl.ds(pl.multiple_of(spot * size, size), size), :]
    width = heads_dev * HD
    depth = normed_ref.shape[1] // (1 + len(parts))
    query, key, value = 0.0, 0.0, 0.0
    for k, part in enumerate([first, *parts]):
        at = 0 if k == 0 else tokens
        owner = lax.axis_index("req") ^ k
        rows = normed_ref[:, pl.ds(pl.multiple_of(owner * depth, depth), depth)]
        w_query, w_key, w_value = packed_projection(part, at, depth, width)
        query = query + lax.dot_general(
            w_query, rows, (((0,), (1,)), ((), ())), preferred_element_type=F32
        )
        key = key + jnp.dot(rows, w_key, preferred_element_type=F32)
        value = value + jnp.dot(rows, w_value, preferred_element_type=F32)
    pieces = []
    for head in range(heads_dev):
        own = slice(head * HD, (head + 1) * HD)
        query_ref[head, :HD, :] = query[own, :].astype(BF16)
        query_ref[head, HD:, :] = jnp.zeros((HD, query.shape[1]), BF16)
        pieces += [key[:, own], value[:, own]]
    fresh_ref[...] = jnp.concatenate(pieces, axis=1).astype(BF16)


def cut_kernel(order_ref, cache_ref, *outs):
    kept, given = outs[:-1], outs[-1]
    tokens, cols = kept[0].shape
    core = lax.rem(lax.axis_index("blk"), 2)
    own = pl.ds(pl.multiple_of(core * cols, cols), cols)
    other = pl.ds(pl.multiple_of((1 - core) * cols, cols), cols)
    for k, out in enumerate(kept):
        slot = order_ref[lax.axis_index("req") ^ k]
        out[...] = cache_ref[slot, :, own]
        given[k * tokens : (k + 1) * tokens, :] = cache_ref[slot, :, other]


def cut_cache(cache_in, slot_order):
    count, tokens, cols = cache_in.shape[0], cache_in.shape[1], cache_in.shape[2] // 2
    outs = [shaped((tokens, cols))] * count + [shaped((count * tokens, cols))]
    return local_call(cut_kernel, [slot_order, cache_in], outs, smem=1)


def turn_kernel(count, *refs):
    parts, outs = refs[:count], refs[count:]
    shift = lax.axis_index("req") ^ (lax.axis_index("blk") // 2)
    for case in range(count):

        @pl.when(shift == case)
        def _(case=case):
            for k in range(count):
                outs[k][...] = parts[k ^ case][: outs[k].shape[0], :]


def turn(parts):
    outs = [shaped(parts[0].shape)] * len(parts)
    return local_call(functools.partial(turn_kernel, len(parts)), parts, outs)


def band_kernel(heads_dev, widths, bias_ref, line_ref, out_ref, row_ref):
    head = lax.axis_index("blk") * heads_dev + pl.program_id(0)
    buckets = line_ref[...]
    row = jnp.zeros(buckets.shape, F32)
    for bucket in range(bias_ref.shape[0]):
        row = jnp.where(buckets == bucket, bias_ref[bucket, head], row)
    row_ref[...] = row
    start = 0
    done = 0
    for width in widths:
        for u in range(0, width, TILE):
            window = row_ref[:, start + u : start + u + 2 * TILE]
            wide = jnp.broadcast_to(window, (TILE, 2 * TILE))
            turned = pltpu.roll(wide, TILE + 1, 1, stride=1, stride_axis=0)
            out_ref[0, :, done + u : done + u + TILE] = turned[:, :TILE]
        start += width + TILE
        done += width


def make_band(bucket_of, rel_bias, old_len, heads_dev, cache_len, rows):
    wide_old, wide_new = cache_len - TILE + rows, 2 * rows - TILE
    low = jnp.broadcast_to(bucket_of[:1], (cache_len - 1,))
    padded = jnp.concatenate([low, bucket_of, bucket_of[-1:]])
    line_old = lax.dynamic_slice(padded, (old_len,), (wide_old + TILE,))
    begin = cache_len - rows
    line_new = padded[begin : begin + wide_new + TILE]
    line = jnp.concatenate([line_old, line_new])[None, :]
    total = wide_old + wide_new
    return pl.pallas_call(
        functools.partial(band_kernel, heads_dev, (wide_old, wide_new)),
        grid=(heads_dev,),
        out_shape=jax.ShapeDtypeStruct((heads_dev, TILE, total), F32),
        in_specs=[
            pl.BlockSpec(memory_space=pltpu.SMEM),
            pl.BlockSpec(memory_space=pltpu.VMEM),
        ],
        out_specs=pl.BlockSpec((1, TILE, total), lambda h: (h, 0, 0)),
        scratch_shapes=[pltpu.VMEM(line.shape, F32)],
        compiler_params=pltpu.CompilerParams(vmem_limit_bytes=32 << 20),
        cost_estimate=pl.CostEstimate(
            flops=8 * heads_dev * TILE * total,
            bytes_accessed=4 * heads_dev * TILE * total,
            transcendentals=0,
        ),
    )(rel_bias, line)


def self_kernel(cache_len, places, first_call, *refs):
    order_ref, old_ref, new_ref, query_ref, band_ref = refs[:5]
    count = len(places)
    blocks, refs = refs[5 : 5 + count], refs[5 + count :]
    if first_call:
        fresh_ref, total_ref, top_ref, norm_ref, score_ref = refs
    else:
        total_in, top_in, norm_in, out_ref, total_ref, top_ref, norm_ref, score_ref = refs
    slot = order_ref[lax.axis_index("req")]
    old_len, new_len = old_ref[slot], new_ref[slot]
    rows = query_ref.shape[2]
    wide_old = cache_len - TILE + rows
    blk = lax.axis_index("blk")

    def attend(keys_values, begin, admit):
        size = keys_values.shape[0]
        top = top_ref[0]
        score_ref[:size, :] = jnp.dot(
            keys_values, query_ref[0], preferred_element_type=F32
        )
        for t in range(0, size, TILE):
            bias = band_ref[0, :, pl.ds(pl.multiple_of(begin - t, TILE), rows)]
            scores = score_ref[t : t + TILE, :] + bias
            scores = jnp.where(admit(t), scores, NEG_FILL)
            score_ref[t : t + TILE, :] = scores
            top = jnp.maximum(top, jnp.max(scores, axis=0, keepdims=True))
        weights = jnp.exp(score_ref[:size, :] - top)
        keep = jnp.exp(top_ref[0] - top)
        norm_ref[0] = norm_ref[0] * keep + jnp.sum(weights, axis=0, keepdims=True)
        term = lax.dot_general(
            keys_values, weights.astype(BF16), (((0,), (0,)), ((), ())),
            preferred_element_type=F32,
        )
        total_ref[0] = total_ref[0] * keep + term
        top_ref[0] = top

    if first_call:
        top_ref[...] = jnp.full(top_ref.shape, NEG_FILL, F32)
        norm_ref[...] = jnp.zeros(norm_ref.shape, F32)
        total_ref[...] = jnp.zeros(total_ref.shape, F32)

        def admit_fresh(t):
            keys = t + lax.broadcasted_iota(jnp.int32, (TILE, rows), 0)
            ids = lax.broadcasted_iota(jnp.int32, (TILE, rows), 1)
            return (keys <= ids) & (keys < new_len)

        attend(fresh_ref[...], wide_old + rows - TILE, admit_fresh)
    else:
        top_ref[...] = top_in[...]
        norm_ref[...] = norm_in[...]
        total_ref[...] = total_in[...]

    for block, place_of in zip(blocks, places):
        first = (blk ^ place_of) * block.shape[0]

        @pl.when(first < old_len)
        def _(block=block, first=first):
            def admit(t):
                keys = first + t + lax.broadcasted_iota(jnp.int32, (TILE, rows), 0)
                return keys < old_len

            attend(block[...], cache_len - TILE - first, admit)

    if not first_call:
        out_ref[0] = (total_ref[0, HD:, :] / norm_ref[0]).astype(BF16)


def self_attend(lens, query_t, band, blocks, places, cache_len, fresh=None, state=None):
    heads_dev, pair, rows = query_t.shape
    count, tokens = len(blocks), blocks[0].shape[0]
    first_call = state is None
    head_block = lambda *tail: pl.BlockSpec((1,) + tail, lambda h: (h, 0, 0))
    in_specs = [SMEM] * 3 + [
        head_block(pair, rows),
        head_block(TILE, band.shape[2]),
    ] + [pl.BlockSpec((tokens, pair), lambda h: (0, h))] * count
    held = [(pair, rows), (1, rows), (1, rows)]
    score = pltpu.VMEM((max(tokens, rows), rows), F32)
    if first_call:
        in_specs.append(pl.BlockSpec((rows, pair), lambda h: (0, h)))
        more = [fresh]
        out_specs = [head_block(*shape) for shape in held]
        out_shape = [jax.ShapeDtypeStruct((heads_dev,) + shape, F32) for shape in held]
        scratch = [score]
    else:
        in_specs += [head_block(*shape) for shape in held]
        more = list(state)
        out_specs = head_block(HD, rows)
        out_shape = jax.ShapeDtypeStruct((heads_dev, HD, rows), BF16)
        scratch = [pltpu.VMEM((1,) + shape, F32) for shape in held] + [score]
    keys_all = count * tokens + (rows if first_call else 0)
    return pl.pallas_call(
        functools.partial(self_kernel, cache_len, places, first_call),
        grid=(heads_dev,),
        in_specs=in_specs,
        out_specs=out_specs,
        out_shape=out_shape,
        scratch_shapes=scratch,
        compiler_params=pltpu.CompilerParams(vmem_limit_bytes=40 << 20),
        cost_estimate=pl.CostEstimate(
            flops=4 * heads_dev * pair * rows * keys_all,
            bytes_accessed=2 * heads_dev * pair * keys_all + 4 * band.size,
            transcendentals=heads_dev * rows * keys_all,
        ),
    )(*lens, query_t, band, *blocks, *more)


def project_out(lefts, weights, skip, depth, owners, partial_ref):
    stride = weights[0].shape[0] // len(owners)
    width = weights[0].shape[1]
    for part, owner in enumerate(owners):
        total = 0.0
        for left, weight in zip(lefts, weights):
            block = weight[part * stride + skip : part * stride + skip + depth, :]
            total = total + lax.dot_general(
                left, block, (((0,), (0,)), ((), ())), preferred_element_type=F32
            )
        partial_ref[:, owner * width : (owner + 1) * width] = total.astype(BF16)


def tail_kernel(skip, *refs):
    parts, out = refs[:-1], refs[-1]
    size = out.shape[0] // len(parts)
    for k, part in enumerate(parts):
        at = skip[0] if k == 0 else skip[1]
        spot = (lax.axis_index("req") ^ k) * size
        out[pl.ds(pl.multiple_of(spot, size), size), :] = part[at : at + size, :]


def self_out_kernel(owners, *refs):
    kept, taken, w_own, w_other = refs[:4]
    outs, partial_ref = refs[4:-1], refs[-1]
    lefts = [kept[...], taken[...]]
    project_out(lefts, (w_own, w_other), 0, kept.shape[0], owners, partial_ref)
    chip = lax.axis_index("blk") // 2
    for k, out in enumerate(outs):
        size = out.shape[0]
        out[...] = partial_ref[pl.ds(pl.multiple_of((chip ^ k) * size, size), size), :]


def sum_rows(parts, residual_ref):
    total = residual_ref[...].astype(F32)
    moved = parts[0][...].astype(F32)
    for part in parts[1:]:
        moved = moved + part[...].astype(F32)
    return total + moved


def norm_kernel(which, count, *refs):
    gain_ref, residual_ref = refs[:2]
    parts, (total_ref, normed_ref) = refs[2 : 2 + count], refs[2 + count :]
    total = sum_rows(parts, residual_ref)
    total_ref[...] = total
    mean_square = jnp.mean(total * total, axis=-1, keepdims=True)
    normed = total * lax.rsqrt(mean_square + EPSILON) * gain_ref[which : which + 1, :]
    normed_ref[...] = normed.astype(BF16)


def sum_kernel(*refs):
    residual_ref, parts, out_ref = refs[0], refs[1:-1], refs[-1]
    out_ref[...] = sum_rows(parts, residual_ref).astype(BF16)


def fill_rows(blocks, rows_ref):
    for k, block in enumerate(blocks):
        size = block.shape[0]
        rows_ref[k * size : (k + 1) * size, :] = block[...]


def hand_rows(outs, partial_ref):
    for k, out in enumerate(outs):
        size = out.shape[0]
        out[...] = partial_ref[k * size : (k + 1) * size, :]


def pair_kernel(owners, rows_ref, *refs):
    weights, outs = refs[:2], refs[2:]
    width = outs[0].shape[1]
    depth = rows_ref.shape[1] // len(owners)
    for i, weight in enumerate(weights):
        stride = weight.shape[0] // len(owners)
        key, value = 0.0, 0.0
        for part, owner in enumerate(owners):
            rows = rows_ref[:, owner * depth : (owner + 1) * depth]
            _, w_key, w_value = packed_projection(weight, part * stride, depth, width)
            key = key + jnp.dot(rows, w_key, preferred_element_type=F32)
            value = value + jnp.dot(rows, w_value, preferred_element_type=F32)
        outs[i][...] = key.astype(BF16)
        outs[2 + i][...] = value.astype(BF16)


def cross_kernel(owners, count, heads_dev, order_ref, enc_ref, *refs):
    blocks, refs = refs[:count], refs[count:]
    w_mid, keys, values = refs[0:2], refs[2:4], refs[4:6]
    outs, (rows_ref, partial_ref) = refs[6:-2], refs[-2:]
    fill_rows(blocks, rows_ref)
    width = heads_dev * HD
    depth = rows_ref.shape[1] // len(owners)
    stride = w_mid[0].shape[0] // len(owners)
    enc_len = enc_ref[order_ref[lax.axis_index("req")]]
    contexts = []
    for w, key_ref, value_ref in zip(w_mid, keys, values):
        query = 0.0
        for part, owner in enumerate(owners):
            query = query + lax.dot_general(
                w[part * stride : part * stride + depth, :width],
                rows_ref[:, owner * depth : (owner + 1) * depth],
                (((0,), (1,)), ((), ())),
                preferred_element_type=F32,
            )
        query = query.astype(BF16)
        head_of = lax.broadcasted_iota(jnp.int32, query.shape, 0) // HD
        pieces = []
        for head in range(heads_dev):
            own_query = jnp.where(head_of == head, query, jnp.zeros_like(query))
            scores = jnp.dot(key_ref[...], own_query, preferred_element_type=F32)
            admitted = lax.broadcasted_iota(jnp.int32, scores.shape, 0) < enc_len
            scores = jnp.where(admitted, scores, NEG_FILL)
            weights = jnp.exp(scores - jnp.max(scores, axis=0, keepdims=True))
            norm = jnp.sum(weights, axis=0, keepdims=True)
            context = lax.dot_general(
                value_ref[...], weights.astype(BF16), (((0,), (0,)), ((), ())),
                preferred_element_type=F32,
            )
            pieces.append((context[head * HD : (head + 1) * HD, :] / norm).astype(BF16))
        contexts.append(jnp.concatenate(pieces, axis=0))
    project_out(contexts, w_mid, depth + depth // 2, width, owners, partial_ref)
    hand_rows(outs, partial_ref)


def ffn_kernel(owners, count, hidden_dev, *refs):
    blocks, weights = refs[:count], refs[count : count + 2]
    outs, (rows_ref, partial_ref) = refs[count + 2 : -2], refs[-2:]
    fill_rows(blocks, rows_ref)
    depth = rows_ref.shape[1] // len(owners)
    stride = weights[0].shape[0] // len(owners)
    blocks_in = (stride - hidden_dev) // depth
    hiddens = []
    for w in weights:
        totals = [0.0] * blocks_in
        for part, owner in enumerate(owners):
            rows = rows_ref[:, owner * depth : (owner + 1) * depth]
            for block in range(blocks_in):
                at = part * stride + block * depth
                totals[block] = totals[block] + jnp.dot(
                    rows, w[at : at + depth, :], preferred_element_type=F32
                )
        both = jnp.concatenate(totals, axis=1)
        span = both.shape[1] // 2
        hidden = jax.nn.gelu(both[:, :span], approximate=True) * both[:, span:]
        hiddens.append(hidden[:, :hidden_dev].astype(BF16))
    width = weights[0].shape[1]
    for part, owner in enumerate(owners):
        total = 0.0
        for hidden, w in zip(hiddens, weights):
            at = (part + 1) * stride - hidden_dev
            total = total + jnp.dot(
                hidden, w[at : at + hidden_dev, :], preferred_element_type=F32
            )
        partial_ref[:, owner * width : (owner + 1) * width] = total.astype(BF16)
    hand_rows(outs, partial_ref)


def per_device(
    new_states,
    encoder_out,
    cache_in,
    slot_order,
    new_lengths,
    cache_lengths,
    enc_lengths,
    bucket_of,
    rel_bias,
    norm_gain,
    self_q,
    self_kv,
    self_out,
    cross_q,
    cross_kv,
    cross_out,
    ff_in,
    ff_out,
):
    req_count, blk_count = lax.axis_size("req"), lax.axis_size("blk")
    chips = blk_count // 2
    core = lax.axis_index("blk") % 2
    heads_dev = H // blk_count
    width_dev = heads_dev * HD
    rows, width = new_states.shape
    half, share = rows // 2, rows // blk_count
    depth, hidden_dev = self_q.shape[0], ff_in.shape[2]
    up_strides = [1 << i for i in range(req_count.bit_length() - 1)]
    down_strides = up_strides[::-1]
    down_owners = [part_owner(p, down_strides) for p in range(req_count)]

    tokens = cache_in.shape[1]
    *kept, given = cut_cache(cache_in, slot_order)
    near_req = [kept[0]] + [xor_send(kept[k], "req", k) for k in range(1, req_count)]
    taken = xor_send(given, "blk", 1)
    lanes = 2 * width_dev
    skip = depth + depth // 2
    packed_in = [self_q, self_kv, cross_q, cross_kv, ff_in, self_out, cross_out, ff_out]
    packed_in = [jnp.moveaxis(w, 1, 0) if w.ndim == 3 else w for w in packed_in]
    packed_in[0] = after(packed_in[0], kept[0])
    wide_cols = 2 * TILE * -(-hidden_dev // TILE)
    first, mid, wide = local_call(
        pack_kernel,
        packed_in,
        [
            shaped((skip + width_dev, lanes)),
            shaped((skip + width_dev, lanes)),
            shaped((depth * (wide_cols // lanes) + hidden_dev, lanes)),
        ],
        scratch=[pltpu.VMEM((depth, wide_cols), BF16)],
    )

    joined = shaped((tokens + first.shape[0], taken.shape[1]))
    joined = local_call(
        join_kernel,
        [taken, first],
        [shaped((tokens, taken.shape[1]))] + [joined] * (req_count - 1),
    )
    near = list(turn([after(near_req[0], joined[0]), *near_req[1:]]))
    far_req = [joined[0]]
    far_req += [xor_send(after(joined[k], near[0]), "req", k) for k in range(1, req_count)]
    near[1] = after(near[1], far_req[1])
    near = chip_sends(near)
    far = turn([after(far_req[0], *near[1:]), *far_req[1:]])
    far = chip_sends(far)

    def token_order(i):
        here = lax.axis_index("blk")
        return 2 * ((here // 2) ^ (i % chips)) + (lax.rem(here, 2) ^ (i // chips))

    cache_own = place(near + far, token_order)

    w_self_out = local_call(
        functools.partial(tail_kernel, (skip, tokens + skip)),
        [first, *far_req[1:]],
        [shaped((req_count * width_dev, self_out.shape[1]))],
    )[0]
    w_self_out = (w_self_out, xor_send(w_self_out, "blk", 1))

    old_len = pick(cache_lengths, pick(slot_order, lax.axis_index("req")))
    band = make_band(bucket_of, rel_bias, old_len, heads_dev, tokens * blk_count, rows)
    query_t, fresh, residual = local_call(
        functools.partial(project_kernel, tokens, heads_dev),
        [new_states, norm_gain, first, *far_req[1:]],
        [
            shaped((heads_dev, 2 * HD, rows)),
            shaped((rows, 2 * width_dev)),
            shaped((share, width)),
        ],
        scratch=[pltpu.VMEM((rows, width), BF16)],
        flops=6 * rows * width * width_dev,
    )
    lens = (slot_order, cache_lengths, new_lengths)
    near_places = [2 * k for k in range(chips)]
    far_places = [2 * k + 1 for k in range(chips)]
    cache_len = tokens * blk_count
    state = self_attend(
        lens,
        query_t,
        band,
        [far[0], *reordered(near)],
        [far_places[0], *reordered(near_places)],
        cache_len,
        fresh=fresh,
    )

    moved_mid = xor_send(after(mid, state[0], *far[1:]), "req", up_strides[0])
    moved_wide = xor_send(after(wide, state[0], *far[1:]), "req", down_strides[0])

    def gather_on(value, moved, strides, *hold):
        value = req_stack(after(value, *hold), moved, strides[0])
        for stride in strides[1:-1]:
            value = req_stack(value, xor_send(value, "req", stride), stride)
        return value, xor_send(value, "req", strides[-1])

    context = self_attend(
        lens,
        query_t,
        band,
        reordered(far)[1:],
        reordered(far_places)[1:],
        cache_len,
        state=state,
    )
    context = context.reshape(width_dev, rows)

    kept = lax.dynamic_slice_in_dim(context, core * half, half, 1)
    given = lax.dynamic_slice_in_dim(context, (1 - core) * half, half, 1)
    parts_out = [shaped((share, width))] * chips
    partial_ref = pltpu.VMEM((half, width), BF16)
    parts = local_call(
        functools.partial(self_out_kernel, range(req_count)),
        [kept, xor_send(given, "blk", 1), *w_self_out],
        parts_out,
        scratch=[partial_ref],
        flops=4 * half * width * width_dev,
    )


    mid, moved_mid = gather_on(mid, moved_mid, up_strides, parts[0])

    def add_and_norm(which, residual, parts):
        total, normed = local_call(
            functools.partial(norm_kernel, which, chips),
            [norm_gain, residual, *reordered(parts)],
            [shaped((share, width), F32), shaped((share, width))],
        )
        return total, normed, chip_sends([normed] * chips)

    parts = chip_sends(parts)
    residual, normed, blocks = add_and_norm(1, residual, parts)
    w_mid = req_stack(after(mid, normed), moved_mid, up_strides[-1])
    w_mid = (w_mid, xor_send(w_mid, "blk", 1))
    wide, moved_wide = gather_on(wide, moved_wide, down_strides, normed)

    enc_rows = encoder_out.shape[0]
    pairs = local_call(
        functools.partial(pair_kernel, range(req_count)),
        [encoder_out, *w_mid],
        [shaped((enc_rows, width_dev))] * 4,
        flops=8 * enc_rows * width * width_dev,
    )
    parts = local_call(
        functools.partial(cross_kernel, range(req_count), chips, heads_dev),
        [slot_order, enc_lengths, *reordered(blocks), *w_mid, *pairs],
        parts_out,
        smem=2,
        scratch=[partial_ref, partial_ref],
        flops=8 * half * width_dev * (width + heads_dev * enc_rows),
        transcendentals=2 * heads_dev * half * enc_rows,
    )
    parts = chip_sends(restored(parts))
    w_wide = req_stack(after(wide, *parts[1:]), moved_wide, down_strides[-1])
    w_wide = (w_wide, xor_send(w_wide, "blk", 1))
    residual, _, blocks = add_and_norm(2, residual, parts)

    parts = local_call(
        functools.partial(ffn_kernel, down_owners, chips, hidden_dev),
        [*reordered(blocks), *w_wide],
        parts_out,
        scratch=[partial_ref, partial_ref],
        flops=12 * half * width * hidden_dev,
        transcendentals=2 * half * hidden_dev,
    )
    final = local_call(sum_kernel, [residual, *reordered(chip_sends(restored(parts)))], [shaped((share, width))])[0]

    same = chip_sends([after(final, cache_own)] * chips)
    both = same + [xor_send(part, "blk", 1) for part in same]

    def row_order(i):
        here = lax.axis_index("blk")
        core_at = lax.rem(here, 2) ^ (i // chips)
        return core_at * chips + ((here // 2) ^ (i % chips))

    layer_out = place(both, row_order)
    return (layer_out, cache_own[None])


def solution(mesh):
    in_specs = (
        P("req", None),
        P("req", None),
        P(None, "blk", "req"),
        P(),
        P(),
        P(),
        P(),
        P(),
        P(),
        P(),
        P("req", "blk"),
        P("req", None, "blk"),
        P("blk", "req"),
        P("req", "blk"),
        P("req", None, "blk"),
        P("blk", "req"),
        P("req", None, "blk"),
        P("blk", "req"),
    )
    out_specs = (P("req", None), P("req", None, "blk"))
    return jax.shard_map(
        per_device, mesh=mesh, in_specs=in_specs, out_specs=out_specs, check_vma=False
    )
```

```python
import functools

import jax
import jax.numpy as jnp
from jax import lax
from jax.experimental import pallas as pl
from jax.experimental.pallas import tpu as pltpu
from jax.sharding import PartitionSpec as P

H = 16
HD = 64
EPSILON = 1e-06
NEG_FILL = -1e30
TILE = 128
F32 = jnp.float32
BF16 = jnp.bfloat16


def pick(table, place):
    matches = place == jnp.arange(table.shape[0], dtype=jnp.int32)
    return jnp.sum(jnp.where(matches, table, 0))


def xor_send(value, axis, step):
    size = lax.axis_size(axis)
    return lax.ppermute(value, axis, [(i, i ^ step) for i in range(size)])


def far_first(count):
    return [0, *range(count // 2, count), *range(1, count // 2)]


def chip_sends(parts):
    moved = [parts[0]] + [None] * (len(parts) - 1)
    for k in far_first(len(parts))[1:]:
        moved[k] = xor_send(parts[k], "blk", 2 * k)
    return moved


def reordered(parts):
    return [parts[k] for k in far_first(len(parts))]


def restored(parts):
    found = [None] * len(parts)
    for part, k in zip(parts, far_first(len(parts))):
        found[k] = part
    return found


VMEM = pl.BlockSpec(memory_space=pltpu.VMEM)
SMEM = pl.BlockSpec(memory_space=pltpu.SMEM)


def local_call(kernel, operands, outs, smem=0, scratch=(), flops=0, transcendentals=0):
    moved = sum(x.size * x.dtype.itemsize for x in list(operands) + list(outs))
    return pl.pallas_call(
        kernel,
        out_shape=list(outs),
        in_specs=[SMEM] * smem + [VMEM] * (len(operands) - smem),
        out_specs=[VMEM] * len(outs),
        scratch_shapes=list(scratch),
        compiler_params=pltpu.CompilerParams(vmem_limit_bytes=8 << 20),
        cost_estimate=pl.CostEstimate(
            flops=flops, bytes_accessed=moved, transcendentals=transcendentals
        ),
    )(*operands)


def shaped(shape, dtype=BF16):
    return jax.ShapeDtypeStruct(tuple(shape), dtype)


def after(value, *others):
    return lax.optimization_barrier((value,) + others)[0]


def place_kernel(order, *refs):
    parts, out = refs[:-1], refs[-1]
    for k, part in enumerate(parts):
        size = part.shape[0]
        out[pl.ds(pl.multiple_of(order(k) * size, size), size), :] = part[...]


def place(parts, order):
    rows, cols = parts[0].shape
    out = shaped((len(parts) * rows, cols))
    return local_call(functools.partial(place_kernel, order), parts, [out])[0]


def stack_order(stride):
    return lambda k: (lax.axis_index("req") // stride) % 2 ^ k


def req_stack(value, moved, stride):
    return place([value, moved], stack_order(stride))


def req_split(values, moved, strides, rows):
    ins, outs = [], []
    for value, other, size in zip(values, moved, rows):
        ins += [value, other]
        outs += [shaped((2 * n, value.shape[1])) for n in (size, value.shape[0] - size)]
    orders = [stack_order(stride) for stride in strides]
    return local_call(functools.partial(split_kernel, orders), ins, outs)


def double_place_kernel(orders, *refs):
    ins, outs = refs[: 2 * len(orders)], refs[2 * len(orders) :]
    for i, order in enumerate(orders):
        place_kernel(order, *ins[2 * i : 2 * i + 2], outs[i])


def req_stack_two(values, moved, strides):
    ins, outs = [], []
    for value, other in zip(values, moved):
        ins += [value, other]
        outs.append(shaped((2 * value.shape[0], value.shape[1])))
    orders = [stack_order(stride) for stride in strides]
    return local_call(functools.partial(double_place_kernel, orders), ins, outs)


def gather_on(value, strides):
    for stride in strides[1:-1]:
        value = req_stack(value, xor_send(value, "req", stride), stride)
    return value, xor_send(value, "req", strides[-1])


def part_owner(part, strides):
    owner = 0
    for i, stride in enumerate(strides):
        owner += stride * ((part >> i) & 1)
    return owner


def pack_projection(query, pair, out, at):
    depth = query.shape[0]
    value = pair[1]
    out[at : at + depth, :] = jnp.concatenate([query[...], pair[0]], axis=1)
    tail = jnp.concatenate([value[: depth // 2], value[depth // 2 :]], axis=1)
    out[at + depth : at + depth + depth // 2, :] = tail


def packed_projection(ref, at, depth, width):
    head = ref[at : at + depth, :]
    tail = ref[at + depth : at + depth + depth // 2, :]
    value = jnp.concatenate([tail[:, :width], tail[:, width:]], axis=0)
    return head[:, :width], head[:, width:], value


def beside(block, width):
    return jnp.concatenate([block[:width], block[width:]], axis=1)


def stacked(block, width):
    return jnp.concatenate([block[:, :width], block[:, width:]], axis=0)


def pack_cross_kernel(query, out, packed):
    depth = query.shape[0]
    packed[: depth // 2, :] = beside(query[...], depth // 2)
    packed[depth // 2 :, :] = out[...]


def pack_kernel(*refs):
    q1, kv1, kv2, ff, o1, o3, first, rest_a, rest_b, wide_ref = refs
    depth, lanes = q1.shape[0], first.shape[1]
    done = depth + depth // 2
    pack_projection(q1, kv1, first, 0)
    first[done:, :] = o1[...]
    rest_a[: depth // 2, :] = beside(kv2[0], depth // 2)
    rest_a[depth // 2 : depth, :] = beside(kv2[1], depth // 2)
    span = wide_ref.shape[1] // 2
    wide_ref[...] = jnp.zeros(wide_ref.shape, wide_ref.dtype)
    wide_ref[:, : ff.shape[2]] = ff[0]
    wide_ref[:, span : span + ff.shape[2]] = ff[1]
    blocks = [wide_ref[:, at : at + lanes] for at in range(0, wide_ref.shape[1], lanes)]
    count_a = rest_a.shape[0] // depth - 1
    for i, block in enumerate(blocks):
        out, at = (rest_a, i + 1) if i < count_a else (rest_b, i - count_a)
        out[at * depth : (at + 1) * depth, :] = block
    rest_b[rest_b.shape[0] - o3.shape[0] :, :] = o3[...]


def weave_kernel(count, *refs):
    parts, (rest_a, rest_b, out_a, out_b) = refs[:count], refs[count:]
    width = parts[0].shape[1] // 2
    half_depth = parts[0].shape[0] - width
    for k in range(0, count, 2):
        pair = [stacked(part[:half_depth, :], width) for part in parts[k : k + 2]]
        out_a[k * half_depth : (k + 2) * half_depth, :] = jnp.concatenate(pair, axis=1)
    for k, part in enumerate(parts):
        out_b[k * width : (k + 1) * width, :] = part[half_depth:, :]
    out_a[count * half_depth :, :] = rest_a[...]
    out_b[count * width :, :] = rest_b[...]


def split_kernel(orders, *refs):
    ins, outs = refs[: 2 * len(orders)], refs[2 * len(orders) :]
    for i, order in enumerate(orders):
        head, tail = outs[2 * i : 2 * i + 2]
        at = head.shape[0] // 2
        for k, part in enumerate(ins[2 * i : 2 * i + 2]):
            for out, rows in ((head, part[:at, :]), (tail, part[at:, :])):
                size = rows.shape[0]
                out[pl.ds(pl.multiple_of(order(k) * size, size), size), :] = rows


def join_kernel(taken, first, *outs):
    tokens = outs[0].shape[0]
    outs[0][...] = taken[:tokens, :]
    for k, out in enumerate(outs[1:], 1):
        out[:tokens, :] = taken[k * tokens : (k + 1) * tokens, :]
        out[tokens:, :] = first[...]


def project_kernel(tokens, heads_dev, states_ref, gain_ref, first, *refs):
    parts, (query_ref, fresh_ref, share_ref, normed_ref) = refs[:-4], refs[-4:]
    states = states_ref[...].astype(F32)
    mean_square = jnp.mean(states * states, axis=-1, keepdims=True)
    normed = states * lax.rsqrt(mean_square + EPSILON) * gain_ref[0:1, :]
    normed_ref[...] = normed.astype(BF16)
    size = share_ref.shape[0]
    blk = lax.axis_index("blk")
    spot = lax.rem(blk, 2) * (states.shape[0] // (2 * size)) + blk // 2
    share_ref[...] = states_ref[pl.ds(pl.multiple_of(spot * size, size), size), :]
    width = heads_dev * HD
    depth = normed_ref.shape[1] // (1 + len(parts))
    query, key, value = 0.0, 0.0, 0.0
    for k, part in enumerate([first, *parts]):
        at = 0 if k == 0 else tokens
        owner = lax.axis_index("req") ^ k
        rows = normed_ref[:, pl.ds(pl.multiple_of(owner * depth, depth), depth)]
        w_query, w_key, w_value = packed_projection(part, at, depth, width)
        query = query + lax.dot_general(
            w_query, rows, (((0,), (1,)), ((), ())), preferred_element_type=F32
        )
        key = key + jnp.dot(rows, w_key, preferred_element_type=F32)
        value = value + jnp.dot(rows, w_value, preferred_element_type=F32)
    pieces = []
    for head in range(heads_dev):
        own = slice(head * HD, (head + 1) * HD)
        query_ref[head, :HD, :] = query[own, :].astype(BF16)
        query_ref[head, HD:, :] = jnp.zeros((HD, query.shape[1]), BF16)
        pieces += [key[:, own], value[:, own]]
    fresh_ref[...] = jnp.concatenate(pieces, axis=1).astype(BF16)


def cut_kernel(order_ref, cache_ref, *outs):
    kept, given = outs[:-1], outs[-1]
    tokens, cols = kept[0].shape
    core = lax.rem(lax.axis_index("blk"), 2)
    own = pl.ds(pl.multiple_of(core * cols, cols), cols)
    other = pl.ds(pl.multiple_of((1 - core) * cols, cols), cols)
    for k, out in enumerate(kept):
        slot = order_ref[lax.axis_index("req") ^ k]
        out[...] = cache_ref[slot, :, own]
        given[k * tokens : (k + 1) * tokens, :] = cache_ref[slot, :, other]


def cut_cache(cache_in, slot_order):
    count, tokens, cols = cache_in.shape[0], cache_in.shape[1], cache_in.shape[2] // 2
    outs = [shaped((tokens, cols))] * count + [shaped((count * tokens, cols))]
    return local_call(cut_kernel, [slot_order, cache_in], outs, smem=1)


def turn_kernel(count, *refs):
    parts, outs = refs[:count], refs[count:]
    shift = lax.axis_index("req") ^ (lax.axis_index("blk") // 2)
    for case in range(count):

        @pl.when(shift == case)
        def _(case=case):
            for k in range(count):
                outs[k][...] = parts[k ^ case][: outs[k].shape[0], :]


def turn(parts):
    outs = [shaped(parts[0].shape)] * len(parts)
    return local_call(functools.partial(turn_kernel, len(parts)), parts, outs)


def band_kernel(heads_dev, widths, bias_ref, line_ref, out_ref, row_ref):
    head = lax.axis_index("blk") * heads_dev + pl.program_id(0)
    buckets = line_ref[...]
    row = jnp.zeros(buckets.shape, F32)
    for bucket in range(bias_ref.shape[0]):
        row = jnp.where(buckets == bucket, bias_ref[bucket, head], row)
    row_ref[...] = row
    start = 0
    done = 0
    for width in widths:
        for u in range(0, width, TILE):
            window = row_ref[:, start + u : start + u + 2 * TILE]
            wide = jnp.broadcast_to(window, (TILE, 2 * TILE))
            turned = pltpu.roll(wide, TILE + 1, 1, stride=1, stride_axis=0)
            out_ref[0, :, done + u : done + u + TILE] = turned[:, :TILE]
        start += width + TILE
        done += width


def make_band(bucket_of, rel_bias, old_len, heads_dev, cache_len, rows):
    wide_old, wide_new = cache_len - TILE + rows, 2 * rows - TILE
    low = jnp.broadcast_to(bucket_of[:1], (cache_len - 1,))
    padded = jnp.concatenate([low, bucket_of, bucket_of[-1:]])
    line_old = lax.dynamic_slice(padded, (old_len,), (wide_old + TILE,))
    begin = cache_len - rows
    line_new = padded[begin : begin + wide_new + TILE]
    line = jnp.concatenate([line_old, line_new])[None, :]
    total = wide_old + wide_new
    return pl.pallas_call(
        functools.partial(band_kernel, heads_dev, (wide_old, wide_new)),
        grid=(heads_dev,),
        out_shape=jax.ShapeDtypeStruct((heads_dev, TILE, total), F32),
        in_specs=[
            pl.BlockSpec(memory_space=pltpu.SMEM),
            pl.BlockSpec(memory_space=pltpu.VMEM),
        ],
        out_specs=pl.BlockSpec((1, TILE, total), lambda h: (h, 0, 0)),
        scratch_shapes=[pltpu.VMEM(line.shape, F32)],
        compiler_params=pltpu.CompilerParams(vmem_limit_bytes=8 << 20),
        cost_estimate=pl.CostEstimate(
            flops=8 * heads_dev * TILE * total,
            bytes_accessed=4 * heads_dev * TILE * total,
            transcendentals=0,
        ),
    )(rel_bias, line)


def self_kernel(cache_len, places, first_call, *refs):
    order_ref, old_ref, new_ref, query_ref, band_ref = refs[:5]
    count = len(places)
    blocks, refs = refs[5 : 5 + count], refs[5 + count :]
    if first_call:
        fresh_ref, total_ref, top_ref, norm_ref, score_ref = refs
    else:
        total_in, top_in, norm_in, out_ref, total_ref, top_ref, norm_ref, score_ref = refs
    slot = order_ref[lax.axis_index("req")]
    old_len, new_len = old_ref[slot], new_ref[slot]
    rows = query_ref.shape[2]
    wide_old = cache_len - TILE + rows
    blk = lax.axis_index("blk")

    def attend(keys_values, begin, admit):
        size = keys_values.shape[0]
        top = top_ref[0]
        score_ref[:size, :] = jnp.dot(
            keys_values, query_ref[0], preferred_element_type=F32
        )
        for t in range(0, size, TILE):
            bias = band_ref[0, :, pl.ds(pl.multiple_of(begin - t, TILE), rows)]
            scores = score_ref[t : t + TILE, :] + bias
            scores = jnp.where(admit(t), scores, NEG_FILL)
            score_ref[t : t + TILE, :] = scores
            top = jnp.maximum(top, jnp.max(scores, axis=0, keepdims=True))
        weights = jnp.exp(score_ref[:size, :] - top)
        keep = jnp.exp(top_ref[0] - top)
        norm_ref[0] = norm_ref[0] * keep + jnp.sum(weights, axis=0, keepdims=True)
        term = lax.dot_general(
            keys_values, weights.astype(BF16), (((0,), (0,)), ((), ())),
            preferred_element_type=F32,
        )
        total_ref[0] = total_ref[0] * keep + term
        top_ref[0] = top

    if first_call:
        top_ref[...] = jnp.full(top_ref.shape, NEG_FILL, F32)
        norm_ref[...] = jnp.zeros(norm_ref.shape, F32)
        total_ref[...] = jnp.zeros(total_ref.shape, F32)

        def admit_fresh(t):
            keys = t + lax.broadcasted_iota(jnp.int32, (TILE, rows), 0)
            ids = lax.broadcasted_iota(jnp.int32, (TILE, rows), 1)
            return (keys <= ids) & (keys < new_len)

        attend(fresh_ref[...], wide_old + rows - TILE, admit_fresh)
    else:
        top_ref[...] = top_in[...]
        norm_ref[...] = norm_in[...]
        total_ref[...] = total_in[...]

    for block, place_of in zip(blocks, places):
        first = (blk ^ place_of) * block.shape[0]

        @pl.when(first < old_len)
        def _(block=block, first=first):
            def admit(t):
                keys = first + t + lax.broadcasted_iota(jnp.int32, (TILE, rows), 0)
                return keys < old_len

            attend(block[...], cache_len - TILE - first, admit)

    if not first_call:
        out_ref[0] = (total_ref[0, HD:, :] / norm_ref[0]).astype(BF16)


def self_attend(lens, query_t, band, blocks, places, cache_len, fresh=None, state=None):
    heads_dev, pair, rows = query_t.shape
    count, tokens = len(blocks), blocks[0].shape[0]
    first_call = state is None
    head_block = lambda *tail: pl.BlockSpec((1,) + tail, lambda h: (h, 0, 0))
    in_specs = [SMEM] * 3 + [
        head_block(pair, rows),
        head_block(TILE, band.shape[2]),
    ] + [pl.BlockSpec((tokens, pair), lambda h: (0, h))] * count
    held = [(pair, rows), (1, rows), (1, rows)]
    score = pltpu.VMEM((max(tokens, rows), rows), F32)
    if first_call:
        in_specs.append(pl.BlockSpec((rows, pair), lambda h: (0, h)))
        more = [fresh]
        out_specs = [head_block(*shape) for shape in held]
        out_shape = [jax.ShapeDtypeStruct((heads_dev,) + shape, F32) for shape in held]
        scratch = [score]
    else:
        in_specs += [head_block(*shape) for shape in held]
        more = list(state)
        out_specs = head_block(HD, rows)
        out_shape = jax.ShapeDtypeStruct((heads_dev, HD, rows), BF16)
        scratch = [pltpu.VMEM((1,) + shape, F32) for shape in held] + [score]
    keys_all = count * tokens + (rows if first_call else 0)
    return pl.pallas_call(
        functools.partial(self_kernel, cache_len, places, first_call),
        grid=(heads_dev,),
        in_specs=in_specs,
        out_specs=out_specs,
        out_shape=out_shape,
        scratch_shapes=scratch,
        compiler_params=pltpu.CompilerParams(vmem_limit_bytes=16 << 20),
        cost_estimate=pl.CostEstimate(
            flops=4 * heads_dev * pair * rows * keys_all,
            bytes_accessed=2 * heads_dev * pair * keys_all + 4 * band.size,
            transcendentals=heads_dev * rows * keys_all,
        ),
    )(*lens, query_t, band, *blocks, *more)


def project_out(lefts, weights, skip, depth, owners, partial_ref):
    stride = weights[0].shape[0] // len(owners)
    width = weights[0].shape[1]
    for part, owner in enumerate(owners):
        total = 0.0
        for left, weight in zip(lefts, weights):
            block = weight[part * stride + skip : part * stride + skip + depth, :]
            total = total + lax.dot_general(
                left, block, (((0,), (0,)), ((), ())), preferred_element_type=F32
            )
        partial_ref[:, owner * width : (owner + 1) * width] = total.astype(BF16)


def tail_kernel(skip, *refs):
    parts, out = refs[:-1], refs[-1]
    size = out.shape[0] // len(parts)
    for k, part in enumerate(parts):
        at = skip[0] if k == 0 else skip[1]
        spot = (lax.axis_index("req") ^ k) * size
        out[pl.ds(pl.multiple_of(spot, size), size), :] = part[at : at + size, :]


def self_out_kernel(owners, *refs):
    kept, taken, w_own, w_other = refs[:4]
    outs, partial_ref = refs[4:-1], refs[-1]
    lefts = [kept[...], taken[...]]
    project_out(lefts, (w_own, w_other), 0, kept.shape[0], owners, partial_ref)
    chip = lax.axis_index("blk") // 2
    for k, out in enumerate(outs):
        size = out.shape[0]
        out[...] = partial_ref[pl.ds(pl.multiple_of((chip ^ k) * size, size), size), :]


def sum_rows(parts, residual_ref):
    total = residual_ref[...].astype(F32)
    moved = parts[0][...].astype(F32)
    for part in parts[1:]:
        moved = moved + part[...].astype(F32)
    return total + moved


def norm_rows(total, gain):
    mean_square = jnp.mean(total * total, axis=-1, keepdims=True)
    return (total * lax.rsqrt(mean_square + EPSILON) * gain).astype(BF16)


def query_kernel(owners, count, *refs):
    gain_ref, residual_ref, refs = refs[0], refs[1], refs[2:]
    parts, weights, (total_ref, *outs) = refs[:count], refs[count : count + 2], refs[count + 2 :]
    total = sum_rows(parts, residual_ref)
    total_ref[...] = total
    normed = norm_rows(total, gain_ref[1:2, :])
    depth = normed.shape[1] // len(owners)
    stride = weights[0].shape[0] // len(owners)
    width = outs[0].shape[1] // 2
    for pair in range(count // 2):
        found = []
        for w in weights:
            query = 0.0
            for part, owner in enumerate(owners):
                at = part * stride + pair * depth
                query = query + jnp.dot(
                    normed[:, owner * depth : (owner + 1) * depth],
                    w[at : at + depth, :],
                    preferred_element_type=F32,
                )
            found.append(query)
        for k in range(2):
            own = slice(k * width, (k + 1) * width)
            both = jnp.concatenate([query[:, own] for query in found], axis=1)
            outs[2 * pair + k][...] = both.astype(BF16)


def cross_out_kernel(owners, count, *refs):
    gain_ref, residual_ref, refs = refs[0], refs[1], refs[2:]
    blocks, weights, (total_ref, normed_ref) = (
        refs[:count], refs[count : count + 2], refs[count + 2 :],
    )
    width = blocks[0].shape[1] // 2
    stride = weights[0].shape[0] // len(owners)
    lanes = weights[0].shape[1]
    for part, owner in enumerate(owners):
        total = 0.0
        for i, w in enumerate(weights):
            left = [block[:, i * width : (i + 1) * width] for block in blocks]
            total = total + jnp.dot(
                jnp.concatenate(left, axis=1),
                w[part * stride : part * stride + count * width, :],
                preferred_element_type=F32,
            )
        cols = slice(owner * lanes, (owner + 1) * lanes)
        total_ref[:, cols] = residual_ref[:, cols] + total
    normed_ref[...] = norm_rows(total_ref[...], gain_ref[2:3, :])


def sum_kernel(*refs):
    residual_ref, parts, out_ref = refs[0], refs[1:-1], refs[-1]
    out_ref[...] = sum_rows(parts, residual_ref).astype(BF16)


def fill_rows(blocks, rows_ref):
    for k, block in enumerate(blocks):
        size = block.shape[0]
        rows_ref[k * size : (k + 1) * size, :] = block[...]


def hand_rows(outs, partial_ref):
    for k, out in enumerate(outs):
        size = out.shape[0]
        out[...] = partial_ref[k * size : (k + 1) * size, :]


def pair_kernel(owners, rows_ref, *refs):
    weights, outs = refs[:2], refs[2:]
    width = outs[0].shape[1]
    depth = rows_ref.shape[1] // len(owners)
    for core, weight in enumerate(weights):
        stride = weight.shape[0] // len(owners)
        for i in range(2):
            total = 0.0
            for part, owner in enumerate(owners):
                rows = rows_ref[:, owner * depth : (owner + 1) * depth]
                at = (part + 1) * stride - depth + i * (depth // 2)
                block = stacked(weight[at : at + depth // 2, :], width)
                total = total + jnp.dot(rows, block, preferred_element_type=F32)
            outs[2 * i + core][...] = total.astype(BF16)


def cross_kernel(count, heads_dev, order_ref, enc_ref, *refs):
    blocks, keys, values = refs[:count], refs[count : count + 2], refs[count + 2 : count + 4]
    outs, rows_ref = refs[count + 4 : -1], refs[-1]
    fill_rows(blocks, rows_ref)
    width = heads_dev * HD
    enc_len = enc_ref[order_ref[lax.axis_index("req")]]
    contexts = []
    for core, (key_ref, value_ref) in enumerate(zip(keys, values)):
        query = rows_ref[:, core * width : (core + 1) * width]
        head_of = lax.broadcasted_iota(jnp.int32, query.shape, 1) // HD
        for head in range(heads_dev):
            own_query = jnp.where(head_of == head, query, jnp.zeros_like(query))
            scores = lax.dot_general(
                key_ref[...], own_query, (((1,), (1,)), ((), ())), preferred_element_type=F32
            )
            admitted = lax.broadcasted_iota(jnp.int32, scores.shape, 0) < enc_len
            scores = jnp.where(admitted, scores, NEG_FILL)
            weights = jnp.exp(scores - jnp.max(scores, axis=0, keepdims=True))
            norm = jnp.sum(weights, axis=0, keepdims=True)
            context = lax.dot_general(
                value_ref[...], weights.astype(BF16), (((0,), (0,)), ((), ())),
                preferred_element_type=F32,
            )
            contexts.append(context[head * HD : (head + 1) * HD, :] / norm)
    context = jnp.concatenate(contexts, axis=0).T.astype(BF16)
    for k, out in enumerate(outs):
        size = out.shape[0]
        out[...] = context[k * size : (k + 1) * size, :]


def ffn_kernel(owners_a, owners_b, count, hidden_dev, *refs):
    blocks, weights_a, weights_b = refs[:count], refs[count : count + 2], refs[count + 2 : count + 4]
    outs, (rows_ref, partial_ref) = refs[count + 4 : -2], refs[-2:]
    fill_rows(blocks, rows_ref)
    depth = rows_ref.shape[1] // len(owners_a)
    stride_a = weights_a[0].shape[0] // len(owners_a)
    stride_b = weights_b[0].shape[0] // len(owners_b)
    hiddens = []
    for w_a, w_b in zip(weights_a, weights_b):
        totals = []
        for w, owners, stride, last in (
            (w_a, owners_a, stride_a, stride_a),
            (w_b, owners_b, stride_b, stride_b - hidden_dev),
        ):
            for block in range(last // depth):
                total = 0.0
                for part, owner in enumerate(owners):
                    at = part * stride + block * depth
                    total = total + jnp.dot(
                        rows_ref[:, owner * depth : (owner + 1) * depth],
                        w[at : at + depth, :],
                        preferred_element_type=F32,
                    )
                totals.append(total)
        both = jnp.concatenate(totals, axis=1)
        span = both.shape[1] // 2
        hidden = jax.nn.gelu(both[:, :span], approximate=True) * both[:, span:]
        hiddens.append(hidden[:, :hidden_dev].astype(BF16))
    lanes = weights_b[0].shape[1]
    for part, owner in enumerate(owners_b):
        total = 0.0
        for hidden, w in zip(hiddens, weights_b):
            at = (part + 1) * stride_b - hidden_dev
            total = total + jnp.dot(
                hidden, w[at : at + hidden_dev, :], preferred_element_type=F32
            )
        partial_ref[:, owner * lanes : (owner + 1) * lanes] = total.astype(BF16)
    hand_rows(outs, partial_ref)


def per_device(
    new_states,
    encoder_out,
    cache_in,
    slot_order,
    new_lengths,
    cache_lengths,
    enc_lengths,
    bucket_of,
    rel_bias,
    norm_gain,
    self_q,
    self_kv,
    self_out,
    cross_q,
    cross_kv,
    cross_out,
    ff_in,
    ff_out,
):
    req_count, blk_count = lax.axis_size("req"), lax.axis_size("blk")
    chips = blk_count // 2
    core = lax.axis_index("blk") % 2
    heads_dev = H // blk_count
    width_dev = heads_dev * HD
    rows, width = new_states.shape
    half, share = rows // 2, rows // blk_count
    depth, hidden_dev = self_q.shape[0], ff_in.shape[2]
    up_strides = [1 << i for i in range(req_count.bit_length() - 1)]
    down_strides = up_strides[::-1]
    down_owners = [part_owner(p, down_strides) for p in range(req_count)]

    lanes = 2 * width_dev
    cross = local_call(
        pack_cross_kernel,
        [cross_q, cross_out],
        [shaped((depth // 2 + width_dev, lanes))],
    )[0]
    cross_parts = chip_sends([cross] * chips)
    tokens = cache_in.shape[1]
    *kept, given = cut_cache(cache_in, slot_order)
    old_len = pick(cache_lengths, pick(slot_order, lax.axis_index("req")))
    band = make_band(bucket_of, rel_bias, old_len, heads_dev, tokens * blk_count, rows)
    near_req = [kept[0]] + [xor_send(kept[k], "req", k) for k in range(1, req_count)]
    taken = xor_send(after(given, cross_parts[1]), "blk", 1)
    skip = depth + depth // 2
    packed_in = [self_q, self_kv, cross_kv, ff_in, self_out, ff_out]
    packed_in = [jnp.moveaxis(w, 1, 0) if w.ndim == 3 else w for w in packed_in]
    packed_in[0] = after(packed_in[0], kept[0])
    wide_cols = 2 * TILE * -(-hidden_dev // TILE)
    blocks_in = wide_cols // lanes
    blocks_a = -(-blocks_in // 2)
    first, rest_a, rest_b = local_call(
        pack_kernel,
        packed_in,
        [
            shaped((skip + width_dev, lanes)),
            shaped((depth + blocks_a * depth, lanes)),
            shaped(((blocks_in - blocks_a) * depth + hidden_dev, lanes)),
        ],
        scratch=[pltpu.VMEM((depth, wide_cols), BF16)],
    )

    all_depth = chips * (depth // 2)
    later_a, later_b = local_call(
        functools.partial(weave_kernel, chips),
        [*cross_parts, rest_a, rest_b],
        [
            shaped((all_depth + rest_a.shape[0], lanes)),
            shaped((chips * width_dev + rest_b.shape[0], lanes)),
        ],
    )

    joined = shaped((tokens + first.shape[0], taken.shape[1]))
    joined = local_call(
        join_kernel,
        [taken, first],
        [shaped((tokens, taken.shape[1]))] + [joined] * (req_count - 1),
    )
    near = list(turn([after(near_req[0], joined[0], later_a), *near_req[1:]]))
    far_req = [joined[0]]
    far_req += [
        xor_send(after(joined[k], near[0]), "req", k) for k in range(1, req_count)
    ]
    near[1] = after(near[1], far_req[1])
    near = chip_sends(near)
    far = turn([after(far_req[0], band, *near[1:]), *far_req[1:]])
    far = chip_sends(far)

    def token_order(i):
        here = lax.axis_index("blk")
        return 2 * ((here // 2) ^ (i % chips)) + (lax.rem(here, 2) ^ (i // chips))

    cache_own = place(near + far, token_order)

    w_self_out = local_call(
        functools.partial(tail_kernel, (skip, tokens + skip)),
        [first, *far_req[1:]],
        [shaped((req_count * width_dev, self_out.shape[1]))],
    )[0]
    w_self_out = (w_self_out, xor_send(w_self_out, "blk", 1))

    query_t, fresh, residual = local_call(
        functools.partial(project_kernel, tokens, heads_dev),
        [new_states, norm_gain, first, *far_req[1:]],
        [
            shaped((heads_dev, 2 * HD, rows)),
            shaped((rows, 2 * width_dev)),
            shaped((share, width)),
        ],
        scratch=[pltpu.VMEM((rows, width), BF16)],
        flops=6 * rows * width * width_dev,
    )
    lens = (slot_order, cache_lengths, new_lengths)
    near_places = [2 * k for k in range(chips)]
    far_places = [2 * k + 1 for k in range(chips)]
    cache_len = tokens * blk_count
    state = self_attend(
        lens,
        query_t,
        band,
        [far[0], *reordered(near)],
        [far_places[0], *reordered(near_places)],
        cache_len,
        fresh=fresh,
    )

    moved_a = xor_send(after(later_a, far[0]), "req", up_strides[0])
    moved_b = xor_send(after(later_b, far[0]), "req", down_strides[0])
    w_query, w_wide, w_cross, w_down = req_split(
        [after(later_a, state[0], *far[1:]), later_b],
        [moved_a, moved_b],
        [up_strides[0], down_strides[0]],
        [all_depth + depth, chips * width_dev],
    )
    w_query, moved_a = gather_on(w_query, up_strides)
    w_cross, moved_b = gather_on(w_cross, down_strides)
    context = self_attend(
        lens,
        query_t,
        band,
        reordered(far)[1:],
        reordered(far_places)[1:],
        cache_len,
        state=state,
    )
    context = context.reshape(width_dev, rows)

    kept = lax.dynamic_slice_in_dim(context, core * half, half, 1)
    given = lax.dynamic_slice_in_dim(context, (1 - core) * half, half, 1)
    parts_out = [shaped((share, width))] * chips
    partial_ref = pltpu.VMEM((half, width), BF16)
    parts = local_call(
        functools.partial(self_out_kernel, range(req_count)),
        [kept, xor_send(given, "blk", 1), *w_self_out],
        parts_out,
        scratch=[partial_ref],
        flops=4 * half * width * width_dev,
    )


    parts = chip_sends(parts)
    last = [up_strides[-1], down_strides[-1]]
    w_query, w_cross = req_stack_two(
        [after(w_query, *parts[1:]), w_cross], [moved_a, moved_b], last
    )
    w_query = (w_query, xor_send(w_query, "blk", 1))
    w_wide, moved_a = gather_on(after(w_wide, *parts[1:]), up_strides)
    w_down, moved_b = gather_on(after(w_down, *parts[1:]), down_strides)
    total, *queries = local_call(
        functools.partial(query_kernel, range(req_count), chips),
        [norm_gain, residual, *reordered(parts), *w_query],
        [shaped((share, width), F32)] + [shaped((share, lanes))] * chips,
        flops=2 * share * width * width,
    )
    residual = total
    w_cross = (w_cross, xor_send(w_cross, "blk", 1))
    enc_rows = encoder_out.shape[0]
    pairs = local_call(
        functools.partial(pair_kernel, range(req_count)),
        [encoder_out, *w_query],
        [shaped((enc_rows, width_dev))] * 4,
        flops=8 * enc_rows * width * width_dev,
    )
    contexts = local_call(
        functools.partial(cross_kernel, chips, heads_dev),
        [slot_order, enc_lengths, *reordered(chip_sends(queries)), *pairs],
        [shaped((share, lanes))] * chips,
        smem=2,
        scratch=[pltpu.VMEM((half, lanes), BF16)],
        flops=8 * half * width_dev * heads_dev * enc_rows,
        transcendentals=2 * heads_dev * half * enc_rows,
    )
    contexts = chip_sends(restored(contexts))

    residual, normed = local_call(
        functools.partial(cross_out_kernel, down_owners, chips),
        [norm_gain, residual, *contexts, *w_cross],
        [shaped((share, width), F32), shaped((share, width))],
        flops=2 * share * width * width,
    )
    blocks = chip_sends([normed] * chips)
    w_wide, w_down = req_stack_two([after(w_wide, normed), w_down], [moved_a, moved_b], last)
    w_wide = (w_wide, xor_send(w_wide, "blk", 1))
    w_down = (w_down, xor_send(w_down, "blk", 1))

    parts = local_call(
        functools.partial(ffn_kernel, range(req_count), down_owners, chips, hidden_dev),
        [*reordered(blocks), *w_wide, *w_down],
        parts_out,
        scratch=[partial_ref, partial_ref],
        flops=12 * half * width * hidden_dev,
        transcendentals=2 * half * hidden_dev,
    )
    final = local_call(
        sum_kernel,
        [residual, *reordered(chip_sends(restored(parts)))],
        [shaped((share, width))],
    )[0]

    same = chip_sends([after(final, cache_own)] * chips)
    both = same + [xor_send(part, "blk", 1) for part in same]

    def row_order(i):
        here = lax.axis_index("blk")
        core_at = lax.rem(here, 2) ^ (i // chips)
        return core_at * chips + ((here // 2) ^ (i % chips))

    layer_out = place(both, row_order)
    return (layer_out, cache_own[None])


def solution(mesh):
    in_specs = (
        P("req", None),
        P("req", None),
        P(None, "blk", "req"),
        P(),
        P(),
        P(),
        P(),
        P(),
        P(),
        P(),
        P("req", "blk"),
        P("req", None, "blk"),
        P("blk", "req"),
        P("req", "blk"),
        P("req", None, "blk"),
        P("blk", "req"),
        P("req", None, "blk"),
        P("blk", "req"),
    )
    out_specs = (P("req", None), P("req", None, "blk"))
    return jax.shard_map(
        per_device, mesh=mesh, in_specs=in_specs, out_specs=out_specs, check_vma=False
    )
```

```python
import functools

import jax
import jax.numpy as jnp
from jax import lax
from jax.experimental import pallas as pl
from jax.experimental.pallas import tpu as pltpu
from jax.sharding import PartitionSpec as P

H = 16
HD = 64
EPSILON = 1e-06
NEG_FILL = -1e30
TILE = 128
F32 = jnp.float32
BF16 = jnp.bfloat16


def xor_send(value, axis, step):
    size = lax.axis_size(axis)
    return lax.ppermute(value, axis, [(i, i ^ step) for i in range(size)])


def far_first(count):
    return [0, *range(count // 2, count), *range(1, count // 2)]


def chip_sends(parts):
    moved = [parts[0]] + [None] * (len(parts) - 1)
    for k in far_first(len(parts))[1:]:
        moved[k] = xor_send(parts[k], "blk", 2 * k)
    return moved


def reordered(parts):
    return [parts[k] for k in far_first(len(parts))]


def restored(parts):
    found = [None] * len(parts)
    for part, k in zip(parts, far_first(len(parts))):
        found[k] = part
    return found


VMEM = pl.BlockSpec(memory_space=pltpu.VMEM)
SMEM = pl.BlockSpec(memory_space=pltpu.SMEM)


def local_call(kernel, operands, outs, smem=0, scratch=(), flops=0, transcendentals=0):
    moved = sum(x.size * x.dtype.itemsize for x in list(operands) + list(outs))
    return pl.pallas_call(
        kernel,
        out_shape=list(outs),
        in_specs=[SMEM] * smem + [VMEM] * (len(operands) - smem),
        out_specs=[VMEM] * len(outs),
        scratch_shapes=list(scratch),
        compiler_params=pltpu.CompilerParams(vmem_limit_bytes=8 << 20),
        cost_estimate=pl.CostEstimate(
            flops=flops, bytes_accessed=moved, transcendentals=transcendentals
        ),
    )(*operands)


def shaped(shape, dtype=BF16):
    return jax.ShapeDtypeStruct(tuple(shape), dtype)


def after(value, *others):
    return lax.optimization_barrier((value,) + others)[0]


def place_kernel(order, *refs):
    parts, out = refs[:-1], refs[-1]
    for k, part in enumerate(parts):
        size = part.shape[0]
        out[pl.ds(pl.multiple_of(order(k) * size, size), size), :] = part[...]


def place(parts, order):
    rows, cols = parts[0].shape
    out = shaped((len(parts) * rows, cols))
    return local_call(functools.partial(place_kernel, order), parts, [out])[0]


def stack_order(stride):
    return lambda k: (lax.axis_index("req") // stride) % 2 ^ k


def req_stack(value, moved, stride):
    return place([value, moved], stack_order(stride))


def req_split(values, moved, strides, rows):
    ins, outs = [], []
    for value, other, size in zip(values, moved, rows):
        ins += [value, other]
        outs += [shaped((2 * n, value.shape[1])) for n in (size, value.shape[0] - size)]
    orders = [stack_order(stride) for stride in strides]
    return local_call(functools.partial(split_kernel, orders), ins, outs)


def double_place_kernel(orders, *refs):
    ins, outs = refs[: 2 * len(orders)], refs[2 * len(orders) :]
    for i, order in enumerate(orders):
        place_kernel(order, *ins[2 * i : 2 * i + 2], outs[i])


def req_stack_two(values, moved, strides):
    ins, outs = [], []
    for value, other in zip(values, moved):
        ins += [value, other]
        outs.append(shaped((2 * value.shape[0], value.shape[1])))
    orders = [stack_order(stride) for stride in strides]
    return local_call(functools.partial(double_place_kernel, orders), ins, outs)


def gather_on(value, strides):
    for stride in strides[1:-1]:
        value = req_stack(value, xor_send(value, "req", stride), stride)
    return value, xor_send(value, "req", strides[-1])


def part_owner(part, strides):
    owner = 0
    for i, stride in enumerate(strides):
        owner += stride * ((part >> i) & 1)
    return owner


def pack_projection(query, pair, out, at):
    depth = query.shape[0]
    value = pair[1]
    out[at : at + depth, :] = jnp.concatenate([query[...], pair[0]], axis=1)
    tail = jnp.concatenate([value[: depth // 2], value[depth // 2 :]], axis=1)
    out[at + depth : at + depth + depth // 2, :] = tail


def packed_projection(ref, at, depth, width):
    head = ref[at : at + depth, :]
    tail = ref[at + depth : at + depth + depth // 2, :]
    value = jnp.concatenate([tail[:, :width], tail[:, width:]], axis=0)
    return head[:, :width], head[:, width:], value


def beside(block, width):
    return jnp.concatenate([block[:width], block[width:]], axis=1)


def stacked(block, width):
    return jnp.concatenate([block[:, :width], block[:, width:]], axis=0)


def pack_cross_kernel(query, out, packed):
    depth = query.shape[0]
    packed[: depth // 2, :] = beside(query[...], depth // 2)
    packed[depth // 2 :, :] = out[...]


def pack_kernel(*refs):
    q1, kv1, kv2, ff, o1, o3, first, rest_a, rest_b, wide_ref = refs
    depth, lanes = q1.shape[0], first.shape[1]
    done = depth + depth // 2
    pack_projection(q1, kv1, first, 0)
    first[done:, :] = o1[...]
    rest_a[: depth // 2, :] = beside(kv2[0], depth // 2)
    rest_a[depth // 2 : depth, :] = beside(kv2[1], depth // 2)
    span = wide_ref.shape[1] // 2
    wide_ref[...] = jnp.zeros(wide_ref.shape, wide_ref.dtype)
    for i in range(2):
        block = ff[i].astype(F32).T.astype(BF16)
        wide_ref[:, i * span : i * span + block.shape[1]] = block
    blocks = [wide_ref[:, at : at + lanes] for at in range(0, wide_ref.shape[1], lanes)]
    count_a = rest_a.shape[0] // depth - 1
    for i, block in enumerate(blocks):
        out, at = (rest_a, i + 1) if i < count_a else (rest_b, i - count_a)
        out[at * depth : (at + 1) * depth, :] = block
    rest_b[rest_b.shape[0] - o3.shape[0] :, :] = o3[...]


def weave_kernel(count, *refs):
    parts, (rest_a, rest_b, out_a, out_b) = refs[:count], refs[count:]
    width = parts[0].shape[1] // 2
    half_depth = parts[0].shape[0] - width
    for k in range(0, count, 2):
        pair = [stacked(part[:half_depth, :], width) for part in parts[k : k + 2]]
        out_a[k * half_depth : (k + 2) * half_depth, :] = jnp.concatenate(pair, axis=1)
    for k, part in enumerate(parts):
        out_b[k * width : (k + 1) * width, :] = part[half_depth:, :]
    out_a[count * half_depth :, :] = rest_a[...]
    out_b[count * width :, :] = rest_b[...]


def split_kernel(orders, *refs):
    ins, outs = refs[: 2 * len(orders)], refs[2 * len(orders) :]
    for i, order in enumerate(orders):
        head, tail = outs[2 * i : 2 * i + 2]
        at = head.shape[0] // 2
        for k, part in enumerate(ins[2 * i : 2 * i + 2]):
            for out, rows in ((head, part[:at, :]), (tail, part[at:, :])):
                size = rows.shape[0]
                out[pl.ds(pl.multiple_of(order(k) * size, size), size), :] = rows


def join_kernel(taken, first, *outs):
    tokens = outs[0].shape[0]
    outs[0][...] = taken[:tokens, :]
    for k, out in enumerate(outs[1:], 1):
        out[:tokens, :] = taken[k * tokens : (k + 1) * tokens, :]
        out[tokens:, :] = first[...]


def project_kernel(tokens, heads_dev, states_ref, gain_ref, first, *refs):
    parts, (query_ref, fresh_ref, share_ref, normed_ref) = refs[:-4], refs[-4:]
    states = states_ref[...].astype(F32)
    mean_square = jnp.mean(states * states, axis=-1, keepdims=True)
    normed = states * lax.rsqrt(mean_square + EPSILON) * gain_ref[0:1, :]
    normed_ref[...] = normed.astype(BF16)
    size = share_ref.shape[0]
    blk = lax.axis_index("blk")
    spot = lax.rem(blk, 2) * (states.shape[0] // (2 * size)) + blk // 2
    share_ref[...] = states_ref[pl.ds(pl.multiple_of(spot * size, size), size), :]
    width = heads_dev * HD
    depth = normed_ref.shape[1] // (1 + len(parts))
    query, key, value = 0.0, 0.0, 0.0
    for k, part in enumerate([first, *parts]):
        at = 0 if k == 0 else tokens
        owner = lax.axis_index("req") ^ k
        rows = normed_ref[:, pl.ds(pl.multiple_of(owner * depth, depth), depth)]
        w_query, w_key, w_value = packed_projection(part, at, depth, width)
        query = query + lax.dot_general(
            w_query, rows, (((0,), (1,)), ((), ())), preferred_element_type=F32
        )
        key = key + jnp.dot(rows, w_key, preferred_element_type=F32)
        value = value + jnp.dot(rows, w_value, preferred_element_type=F32)
    pieces = []
    for head in range(heads_dev):
        own = slice(head * HD, (head + 1) * HD)
        query_ref[head, :HD, :] = query[own, :].astype(BF16)
        query_ref[head, HD:, :] = jnp.zeros((HD, query.shape[1]), BF16)
        pieces += [key[:, own], value[:, own]]
    fresh_ref[...] = jnp.concatenate(pieces, axis=1).astype(BF16)


def cut_kernel(order_ref, cache_ref, *outs):
    kept, given = outs[:-1], outs[-1]
    tokens, cols = kept[0].shape
    core = lax.rem(lax.axis_index("blk"), 2)
    own = pl.ds(pl.multiple_of(core * cols, cols), cols)
    other = pl.ds(pl.multiple_of((1 - core) * cols, cols), cols)
    for k, out in enumerate(kept):
        slot = order_ref[lax.axis_index("req") ^ k]
        out[...] = cache_ref[slot, :, own]
        given[k * tokens : (k + 1) * tokens, :] = cache_ref[slot, :, other]


def cut_cache(cache_in, slot_order):
    count, tokens, cols = cache_in.shape[0], cache_in.shape[1], cache_in.shape[2] // 2
    outs = [shaped((tokens, cols))] * count + [shaped((count * tokens, cols))]
    return local_call(cut_kernel, [slot_order, cache_in], outs, smem=1)


def turn_kernel(count, *refs):
    parts, outs = refs[:count], refs[count:]
    shift = lax.axis_index("req") ^ (lax.axis_index("blk") // 2)
    for case in range(count):

        @pl.when(shift == case)
        def _(case=case):
            for k in range(count):
                outs[k][...] = parts[k ^ case][: outs[k].shape[0], :]


def turn(parts):
    outs = [shaped(parts[0].shape)] * len(parts)
    return local_call(functools.partial(turn_kernel, len(parts)), parts, outs)


def band_kernel(heads_dev, cache_len, widths, order_ref, old_ref, bias_ref, bucket_ref, *refs):
    out_ref, line_ref, row_ref = refs
    head = lax.axis_index("blk") * heads_dev + pl.program_id(0)
    old_len = old_ref[order_ref[lax.axis_index("req")]]
    heads = lax.broadcasted_iota(jnp.int32, bias_ref.shape, 0)
    bias = jnp.sum(jnp.where(heads == head, bias_ref[...], 0.0), axis=0, keepdims=True)
    buckets = bucket_ref[...]
    copies, size = line_ref.shape
    line_ref[:, :cache_len] = jnp.broadcast_to(buckets[:, :1], (copies, cache_len))
    line_ref[:, cache_len:] = jnp.broadcast_to(buckets, (copies, size - cache_len))
    start = 0
    done = 0
    rows = (widths[1] + TILE) // 2
    for width, first in zip(widths, (old_len + 1, cache_len - rows + 1)):
        turned = pltpu.roll(line_ref[...], size - first, 1)[:, : width + TILE]
        row = jnp.zeros(turned.shape, F32)
        for bucket in range(bias_ref.shape[1]):
            row = jnp.where(turned == bucket, bias[:, bucket : bucket + 1], row)
        row_ref[:, start : start + width + TILE] = row
        for u in range(0, width, TILE):
            window = row_ref[0:1, start + u : start + u + 2 * TILE]
            wide = jnp.broadcast_to(window, (TILE, 2 * TILE))
            skewed = pltpu.roll(wide, TILE + 1, 1, stride=1, stride_axis=0)
            out_ref[0, :, done + u : done + u + TILE] = skewed[:, :TILE]
        start += width + TILE
        done += width


def make_band(bucket_of, rel_bias, slot_order, cache_lengths, heads_dev, cache_len, rows):
    widths = (cache_len - TILE + rows, 2 * rows - TILE)
    total = sum(widths)
    return pl.pallas_call(
        functools.partial(band_kernel, heads_dev, cache_len, widths),
        grid=(heads_dev,),
        out_shape=jax.ShapeDtypeStruct((heads_dev, TILE, total), F32),
        in_specs=[SMEM, SMEM, VMEM, VMEM],
        out_specs=pl.BlockSpec((1, TILE, total), lambda h: (h, 0, 0)),
        scratch_shapes=[
            pltpu.VMEM((8, cache_len + bucket_of.shape[0]), jnp.int32),
            pltpu.VMEM((8, total + 2 * TILE), F32),
        ],
        compiler_params=pltpu.CompilerParams(vmem_limit_bytes=12 << 20),
        cost_estimate=pl.CostEstimate(
            flops=8 * heads_dev * TILE * total,
            bytes_accessed=4 * heads_dev * TILE * total,
            transcendentals=0,
        ),
    )(slot_order, cache_lengths, rel_bias.T, bucket_of[None, :])


def self_kernel(cache_len, places, first_call, *refs):
    order_ref, old_ref, new_ref, query_ref, band_ref = refs[:5]
    count = len(places)
    blocks, refs = refs[5 : 5 + count], refs[5 + count :]
    if first_call:
        fresh_ref, total_ref, top_ref, norm_ref, score_ref = refs
    else:
        total_in, top_in, norm_in, kept_ref, given_ref = refs[:5]
        total_ref, top_ref, norm_ref, score_ref = refs[5:]
    slot = order_ref[lax.axis_index("req")]
    old_len, new_len = old_ref[slot], new_ref[slot]
    rows = query_ref.shape[2]
    wide_old = cache_len - TILE + rows
    blk = lax.axis_index("blk")

    def attend(keys_values, begin, admit):
        size = keys_values.shape[0]
        top = top_ref[0]
        score_ref[:size, :] = jnp.dot(
            keys_values, query_ref[0], preferred_element_type=F32
        )
        for t in range(0, size, TILE):
            bias = band_ref[0, :, pl.ds(pl.multiple_of(begin - t, TILE), rows)]
            scores = score_ref[t : t + TILE, :] + bias
            scores = jnp.where(admit(t), scores, NEG_FILL)
            score_ref[t : t + TILE, :] = scores
            top = jnp.maximum(top, jnp.max(scores, axis=0, keepdims=True))
        weights = jnp.exp(score_ref[:size, :] - top)
        keep = jnp.exp(top_ref[0] - top)
        norm_ref[0] = norm_ref[0] * keep + jnp.sum(weights, axis=0, keepdims=True)
        term = lax.dot_general(
            keys_values, weights.astype(BF16), (((0,), (0,)), ((), ())),
            preferred_element_type=F32,
        )
        total_ref[0] = total_ref[0] * keep + term
        top_ref[0] = top

    if first_call:
        top_ref[...] = jnp.full(top_ref.shape, NEG_FILL, F32)
        norm_ref[...] = jnp.zeros(norm_ref.shape, F32)
        total_ref[...] = jnp.zeros(total_ref.shape, F32)

        def admit_fresh(t):
            keys = t + lax.broadcasted_iota(jnp.int32, (TILE, rows), 0)
            ids = lax.broadcasted_iota(jnp.int32, (TILE, rows), 1)
            return (keys <= ids) & (keys < new_len)

        attend(fresh_ref[...], wide_old + rows - TILE, admit_fresh)
    else:
        top_ref[...] = top_in[...]
        norm_ref[...] = norm_in[...]
        total_ref[...] = total_in[...]

    for block, place_of in zip(blocks, places):
        first = (blk ^ place_of) * block.shape[0]

        @pl.when(first < old_len)
        def _(block=block, first=first):
            def admit(t):
                keys = first + t + lax.broadcasted_iota(jnp.int32, (TILE, rows), 0)
                return keys < old_len

            attend(block[...], cache_len - TILE - first, admit)

    if not first_call:
        total_ref[0, :HD, :] = total_ref[0, HD:, :] / norm_ref[0]
        half = rows // 2
        for out_ref, core in ((kept_ref, lax.rem(blk, 2)), (given_ref, 1 - lax.rem(blk, 2))):
            spot = pl.ds(pl.multiple_of(core * half, half), half)
            out_ref[0] = total_ref[0, :HD, spot].astype(BF16)


def self_attend(lens, query_t, band, blocks, places, cache_len, fresh=None, state=None):
    heads_dev, pair, rows = query_t.shape
    count, tokens = len(blocks), blocks[0].shape[0]
    first_call = state is None
    head_block = lambda *tail: pl.BlockSpec((1,) + tail, lambda h: (h, 0, 0))
    in_specs = [SMEM] * 3 + [
        head_block(pair, rows),
        head_block(TILE, band.shape[2]),
    ] + [pl.BlockSpec((tokens, pair), lambda h: (0, h))] * count
    held = [(pair, rows), (1, rows), (1, rows)]
    score = pltpu.VMEM((max(tokens, rows), rows), F32)
    if first_call:
        in_specs.append(pl.BlockSpec((rows, pair), lambda h: (0, h)))
        more = [fresh]
        out_specs = [head_block(*shape) for shape in held]
        out_shape = [jax.ShapeDtypeStruct((heads_dev,) + shape, F32) for shape in held]
        scratch = [score]
    else:
        in_specs += [head_block(*shape) for shape in held]
        more = list(state)
        out_specs = [head_block(HD, rows // 2)] * 2
        out_shape = [shaped((heads_dev, HD, rows // 2))] * 2
        scratch = [pltpu.VMEM((1,) + shape, F32) for shape in held] + [score]
    keys_all = count * tokens + (rows if first_call else 0)
    return pl.pallas_call(
        functools.partial(self_kernel, cache_len, places, first_call),
        grid=(heads_dev,),
        in_specs=in_specs,
        out_specs=out_specs,
        out_shape=out_shape,
        scratch_shapes=scratch,
        compiler_params=pltpu.CompilerParams(vmem_limit_bytes=16 << 20),
        cost_estimate=pl.CostEstimate(
            flops=4 * heads_dev * pair * rows * keys_all,
            bytes_accessed=2 * heads_dev * pair * keys_all + 4 * band.size,
            transcendentals=heads_dev * rows * keys_all,
        ),
    )(*lens, query_t, band, *blocks, *more)


def project_out(lefts, weights, skip, depth, owners, partial_ref):
    stride = weights[0].shape[0] // len(owners)
    width = weights[0].shape[1]
    for part, owner in enumerate(owners):
        total = 0.0
        for left, weight in zip(lefts, weights):
            block = weight[part * stride + skip : part * stride + skip + depth, :]
            total = total + lax.dot_general(
                left, block, (((0,), (0,)), ((), ())), preferred_element_type=F32
            )
        partial_ref[:, owner * width : (owner + 1) * width] = total.astype(BF16)


def tail_kernel(skip, *refs):
    parts, out = refs[:-1], refs[-1]
    size = out.shape[0] // len(parts)
    for k, part in enumerate(parts):
        at = skip[0] if k == 0 else skip[1]
        spot = (lax.axis_index("req") ^ k) * size
        out[pl.ds(pl.multiple_of(spot, size), size), :] = part[at : at + size, :]


def self_out_kernel(owners, *refs):
    kept, taken, w_own, w_other = refs[:4]
    outs, partial_ref = refs[4:-1], refs[-1]
    lefts = [kept[...], taken[...]]
    project_out(lefts, (w_own, w_other), 0, kept.shape[0], owners, partial_ref)
    chip = lax.axis_index("blk") // 2
    for k, out in enumerate(outs):
        size = out.shape[0]
        out[...] = partial_ref[pl.ds(pl.multiple_of((chip ^ k) * size, size), size), :]


def sum_rows(parts, residual_ref):
    total = residual_ref[...].astype(F32)
    moved = parts[0][...].astype(F32)
    for part in parts[1:]:
        moved = moved + part[...].astype(F32)
    return total + moved


def norm_rows(total, gain):
    mean_square = jnp.mean(total * total, axis=-1, keepdims=True)
    return (total * lax.rsqrt(mean_square + EPSILON) * gain).astype(BF16)


def query_kernel(owners, count, *refs):
    gain_ref, residual_ref, refs = refs[0], refs[1], refs[2:]
    parts, weights, (total_ref, *outs) = refs[:count], refs[count : count + 2], refs[count + 2 :]
    total = sum_rows(parts, residual_ref)
    total_ref[...] = total
    normed = norm_rows(total, gain_ref[1:2, :])
    depth = normed.shape[1] // len(owners)
    stride = weights[0].shape[0] // len(owners)
    width = outs[0].shape[1] // 2
    for pair in range(count // 2):
        found = []
        for w in weights:
            query = 0.0
            for part, owner in enumerate(owners):
                at = part * stride + pair * depth
                query = query + jnp.dot(
                    normed[:, owner * depth : (owner + 1) * depth],
                    w[at : at + depth, :],
                    preferred_element_type=F32,
                )
            found.append(query)
        for k in range(2):
            own = slice(k * width, (k + 1) * width)
            both = jnp.concatenate([query[:, own] for query in found], axis=1)
            outs[2 * pair + k][...] = both.astype(BF16)


def cross_out_kernel(owners, count, *refs):
    gain_ref, residual_ref, refs = refs[0], refs[1], refs[2:]
    blocks, weights, (total_ref, normed_ref) = (
        refs[:count], refs[count : count + 2], refs[count + 2 :],
    )
    width = blocks[0].shape[1] // 2
    stride = weights[0].shape[0] // len(owners)
    lanes = weights[0].shape[1]
    for part, owner in enumerate(owners):
        total = 0.0
        for i, w in enumerate(weights):
            left = [block[:, i * width : (i + 1) * width] for block in blocks]
            total = total + jnp.dot(
                jnp.concatenate(left, axis=1),
                w[part * stride : part * stride + count * width, :],
                preferred_element_type=F32,
            )
        cols = slice(owner * lanes, (owner + 1) * lanes)
        total_ref[:, cols] = residual_ref[:, cols] + total
    normed_ref[...] = norm_rows(total_ref[...], gain_ref[2:3, :])


def sum_kernel(*refs):
    residual_ref, parts, out_ref = refs[0], refs[1:-1], refs[-1]
    out_ref[...] = sum_rows(parts, residual_ref).astype(BF16)


def fill_rows(blocks, rows_ref):
    for k, block in enumerate(blocks):
        size = block.shape[0]
        rows_ref[k * size : (k + 1) * size, :] = block[...]


def hand_rows(outs, partial_ref):
    for k, out in enumerate(outs):
        size = out.shape[0]
        out[...] = partial_ref[k * size : (k + 1) * size, :]


def pair_kernel(owners, rows_ref, *refs):
    weights, outs = refs[:2], refs[2:]
    width = outs[0].shape[1]
    depth = rows_ref.shape[1] // len(owners)
    for core, weight in enumerate(weights):
        stride = weight.shape[0] // len(owners)
        for i in range(2):
            total = 0.0
            for part, owner in enumerate(owners):
                rows = rows_ref[:, owner * depth : (owner + 1) * depth]
                at = (part + 1) * stride - depth + i * (depth // 2)
                block = stacked(weight[at : at + depth // 2, :], width)
                total = total + jnp.dot(rows, block, preferred_element_type=F32)
            outs[2 * i + core][...] = total.astype(BF16)


def cross_kernel(count, heads_dev, order_ref, enc_ref, *refs):
    blocks, keys, values = refs[:count], refs[count : count + 2], refs[count + 2 : count + 4]
    outs, rows_ref = refs[count + 4 : -1], refs[-1]
    fill_rows(blocks, rows_ref)
    width = heads_dev * HD
    enc_len = enc_ref[order_ref[lax.axis_index("req")]]
    contexts = []
    for core, (key_ref, value_ref) in enumerate(zip(keys, values)):
        query = rows_ref[:, core * width : (core + 1) * width]
        head_of = lax.broadcasted_iota(jnp.int32, query.shape, 1) // HD
        for head in range(heads_dev):
            own_query = jnp.where(head_of == head, query, jnp.zeros_like(query))
            scores = lax.dot_general(
                key_ref[...], own_query, (((1,), (1,)), ((), ())), preferred_element_type=F32
            )
            admitted = lax.broadcasted_iota(jnp.int32, scores.shape, 0) < enc_len
            scores = jnp.where(admitted, scores, NEG_FILL)
            weights = jnp.exp(scores - jnp.max(scores, axis=0, keepdims=True))
            norm = jnp.sum(weights, axis=0, keepdims=True)
            context = lax.dot_general(
                value_ref[...], weights.astype(BF16), (((0,), (0,)), ((), ())),
                preferred_element_type=F32,
            )
            contexts.append(context[head * HD : (head + 1) * HD, :] / norm)
    context = jnp.concatenate(contexts, axis=0).T.astype(BF16)
    for k, out in enumerate(outs):
        size = out.shape[0]
        out[...] = context[k * size : (k + 1) * size, :]


def ffn_kernel(owners_a, owners_b, count, hidden_dev, *refs):
    blocks, weights_a, weights_b = refs[:count], refs[count : count + 2], refs[count + 2 : count + 4]
    outs, (rows_ref, partial_ref) = refs[count + 4 : -2], refs[-2:]
    fill_rows(blocks, rows_ref)
    depth = rows_ref.shape[1] // len(owners_a)
    stride_a = weights_a[0].shape[0] // len(owners_a)
    stride_b = weights_b[0].shape[0] // len(owners_b)
    hiddens = []
    for w_a, w_b in zip(weights_a, weights_b):
        totals = []
        for w, owners, stride, last in (
            (w_a, owners_a, stride_a, stride_a),
            (w_b, owners_b, stride_b, stride_b - hidden_dev),
        ):
            for block in range(last // depth):
                total = 0.0
                for part, owner in enumerate(owners):
                    at = part * stride + block * depth
                    total = total + jnp.dot(
                        rows_ref[:, owner * depth : (owner + 1) * depth],
                        w[at : at + depth, :],
                        preferred_element_type=F32,
                    )
                totals.append(total)
        both = jnp.concatenate(totals, axis=1)
        span = both.shape[1] // 2
        hidden = jax.nn.gelu(both[:, :span], approximate=True) * both[:, span:]
        hiddens.append(hidden[:, :hidden_dev].astype(BF16))
    lanes = weights_b[0].shape[1]
    for part, owner in enumerate(owners_b):
        total = 0.0
        for hidden, w in zip(hiddens, weights_b):
            at = (part + 1) * stride_b - hidden_dev
            total = total + jnp.dot(
                hidden, w[at : at + hidden_dev, :], preferred_element_type=F32
            )
        partial_ref[:, owner * lanes : (owner + 1) * lanes] = total.astype(BF16)
    hand_rows(outs, partial_ref)


def per_device(
    new_states,
    encoder_out,
    cache_in,
    slot_order,
    new_lengths,
    cache_lengths,
    enc_lengths,
    bucket_of,
    rel_bias,
    norm_gain,
    self_q,
    self_kv,
    self_out,
    cross_q,
    cross_kv,
    cross_out,
    ff_in,
    ff_out,
):
    req_count, blk_count = lax.axis_size("req"), lax.axis_size("blk")
    chips = blk_count // 2
    heads_dev = H // blk_count
    width_dev = heads_dev * HD
    rows, width = new_states.shape
    half, share = rows // 2, rows // blk_count
    depth, hidden_dev = self_q.shape[0], ff_in.shape[2]
    up_strides = [1 << i for i in range(req_count.bit_length() - 1)]
    down_strides = up_strides[::-1]
    down_owners = [part_owner(p, down_strides) for p in range(req_count)]

    lanes = 2 * width_dev
    cross = local_call(
        pack_cross_kernel,
        [cross_q, cross_out],
        [shaped((depth // 2 + width_dev, lanes))],
    )[0]
    cross_parts = chip_sends([cross] * chips)
    tokens = cache_in.shape[1]
    *kept, given = cut_cache(cache_in, slot_order)
    band = make_band(
        bucket_of, rel_bias, slot_order, cache_lengths, heads_dev, tokens * blk_count, rows
    )
    near_req = [kept[0]] + [xor_send(kept[k], "req", k) for k in range(1, req_count)]
    taken = xor_send(after(given, cross_parts[1]), "blk", 1)
    skip = depth + depth // 2
    packed_in = [self_q, self_kv, cross_kv, ff_in, self_out, ff_out]
    packed_in[1], packed_in[2] = jnp.moveaxis(self_kv, 1, 0), jnp.moveaxis(cross_kv, 1, 0)
    packed_in[3] = ff_in.transpose(1, 2, 0)
    packed_in[0] = after(packed_in[0], kept[0])
    wide_cols = 2 * TILE * -(-hidden_dev // TILE)
    blocks_in = wide_cols // lanes
    blocks_a = -(-blocks_in // 2)
    first, rest_a, rest_b = local_call(
        pack_kernel,
        packed_in,
        [
            shaped((skip + width_dev, lanes)),
            shaped((depth + blocks_a * depth, lanes)),
            shaped(((blocks_in - blocks_a) * depth + hidden_dev, lanes)),
        ],
        scratch=[pltpu.VMEM((depth, wide_cols), BF16)],
    )

    all_depth = chips * (depth // 2)
    later_a, later_b = local_call(
        functools.partial(weave_kernel, chips),
        [*cross_parts, rest_a, rest_b],
        [
            shaped((all_depth + rest_a.shape[0], lanes)),
            shaped((chips * width_dev + rest_b.shape[0], lanes)),
        ],
    )

    joined = shaped((tokens + first.shape[0], taken.shape[1]))
    joined = local_call(
        join_kernel,
        [taken, first],
        [shaped((tokens, taken.shape[1]))] + [joined] * (req_count - 1),
    )
    near = list(turn([after(near_req[0], joined[0], later_a), *near_req[1:]]))
    far_req = [joined[0]]
    far_req += [
        xor_send(after(joined[k], near[0]), "req", k) for k in range(1, req_count)
    ]
    near[1] = after(near[1], far_req[1])
    near = chip_sends(near)
    far = turn([after(far_req[0], band, *near[1:]), *far_req[1:]])
    far = chip_sends(far)

    def token_order(i):
        here = lax.axis_index("blk")
        return 2 * ((here // 2) ^ (i % chips)) + (lax.rem(here, 2) ^ (i // chips))

    cache_own = place(near + far, token_order)

    w_self_out = local_call(
        functools.partial(tail_kernel, (skip, tokens + skip)),
        [first, *far_req[1:]],
        [shaped((req_count * width_dev, self_out.shape[1]))],
    )[0]
    w_self_out = (w_self_out, xor_send(w_self_out, "blk", 1))

    query_t, fresh, residual = local_call(
        functools.partial(project_kernel, tokens, heads_dev),
        [new_states, norm_gain, first, *far_req[1:]],
        [
            shaped((heads_dev, 2 * HD, rows)),
            shaped((rows, 2 * width_dev)),
            shaped((share, width)),
        ],
        scratch=[pltpu.VMEM((rows, width), BF16)],
        flops=6 * rows * width * width_dev,
    )
    lens = (slot_order, cache_lengths, new_lengths)
    near_places = [2 * k for k in range(chips)]
    far_places = [2 * k + 1 for k in range(chips)]
    cache_len = tokens * blk_count
    state = self_attend(
        lens,
        query_t,
        band,
        [far[0], *reordered(near)],
        [far_places[0], *reordered(near_places)],
        cache_len,
        fresh=fresh,
    )

    moved_a = xor_send(after(later_a, far[0]), "req", up_strides[0])
    moved_b = xor_send(after(later_b, far[0]), "req", down_strides[0])
    w_query, w_wide, w_cross, w_down = req_split(
        [after(later_a, state[0], *far[1:]), later_b],
        [moved_a, moved_b],
        [up_strides[0], down_strides[0]],
        [all_depth + depth, chips * width_dev],
    )
    w_query, moved_a = gather_on(w_query, up_strides)
    w_cross, moved_b = gather_on(w_cross, down_strides)
    kept, given = self_attend(
        lens,
        query_t,
        band,
        reordered(far)[1:],
        reordered(far_places)[1:],
        cache_len,
        state=state,
    )
    kept, given = kept.reshape(width_dev, half), given.reshape(width_dev, half)

    parts_out = [shaped((share, width))] * chips
    partial_ref = pltpu.VMEM((half, width), BF16)
    parts = local_call(
        functools.partial(self_out_kernel, range(req_count)),
        [kept, xor_send(given, "blk", 1), *w_self_out],
        parts_out,
        scratch=[partial_ref],
        flops=4 * half * width * width_dev,
    )


    parts = chip_sends(parts)
    last = [up_strides[-1], down_strides[-1]]
    w_query, w_cross = req_stack_two(
        [after(w_query, *parts[1:]), w_cross], [moved_a, moved_b], last
    )
    w_query = (w_query, xor_send(w_query, "blk", 1))
    w_wide, moved_a = gather_on(after(w_wide, *parts[1:]), up_strides)
    w_down, moved_b = gather_on(after(w_down, *parts[1:]), down_strides)
    total, *queries = local_call(
        functools.partial(query_kernel, range(req_count), chips),
        [norm_gain, residual, *reordered(parts), *w_query],
        [shaped((share, width), F32)] + [shaped((share, lanes))] * chips,
        flops=2 * share * width * width,
    )
    residual = total
    w_cross = (w_cross, xor_send(w_cross, "blk", 1))
    enc_rows = encoder_out.shape[0]
    pairs = local_call(
        functools.partial(pair_kernel, range(req_count)),
        [encoder_out, *w_query],
        [shaped((enc_rows, width_dev))] * 4,
        flops=8 * enc_rows * width * width_dev,
    )
    contexts = local_call(
        functools.partial(cross_kernel, chips, heads_dev),
        [slot_order, enc_lengths, *reordered(chip_sends(queries)), *pairs],
        [shaped((share, lanes))] * chips,
        smem=2,
        scratch=[pltpu.VMEM((half, lanes), BF16)],
        flops=8 * half * width_dev * heads_dev * enc_rows,
        transcendentals=2 * heads_dev * half * enc_rows,
    )
    contexts = chip_sends(restored(contexts))

    residual, normed = local_call(
        functools.partial(cross_out_kernel, down_owners, chips),
        [norm_gain, residual, *contexts, *w_cross],
        [shaped((share, width), F32), shaped((share, width))],
        flops=2 * share * width * width,
    )
    blocks = chip_sends([normed] * chips)
    w_wide, w_down = req_stack_two([after(w_wide, normed), w_down], [moved_a, moved_b], last)
    w_wide = (w_wide, xor_send(w_wide, "blk", 1))
    w_down = (w_down, xor_send(w_down, "blk", 1))

    parts = local_call(
        functools.partial(ffn_kernel, range(req_count), down_owners, chips, hidden_dev),
        [*reordered(blocks), *w_wide, *w_down],
        parts_out,
        scratch=[partial_ref, partial_ref],
        flops=12 * half * width * hidden_dev,
        transcendentals=2 * half * hidden_dev,
    )
    final = local_call(
        sum_kernel,
        [residual, *reordered(chip_sends(restored(parts)))],
        [shaped((share, width))],
    )[0]

    same = chip_sends([after(final, cache_own)] * chips)
    both = same + [xor_send(part, "blk", 1) for part in same]

    def row_order(i):
        here = lax.axis_index("blk")
        core_at = lax.rem(here, 2) ^ (i // chips)
        return core_at * chips + ((here // 2) ^ (i % chips))

    layer_out = place(both, row_order)
    return (layer_out, cache_own[None])


def solution(mesh):
    in_specs = (
        P("req", None),
        P("req", None),
        P(None, "blk", "req"),
        P(),
        P(),
        P(),
        P(),
        P(),
        P(),
        P(),
        P("req", "blk"),
        P("req", None, "blk"),
        P("blk", "req"),
        P("req", "blk"),
        P("req", None, "blk"),
        P("blk", "req"),
        P("req", None, "blk"),
        P("blk", "req"),
    )
    out_specs = (P("req", None), P("req", None, "blk"))
    return jax.shard_map(
        per_device, mesh=mesh, in_specs=in_specs, out_specs=out_specs, check_vma=False
    )
```

```python
import functools

import jax
import jax.numpy as jnp
from jax import lax
from jax.experimental import pallas as pl
from jax.experimental.pallas import tpu as pltpu
from jax.sharding import PartitionSpec as P

H = 16
HD = 64
EPSILON = 1e-06
NEG_FILL = -1e30
TILE = 128
F32 = jnp.float32
BF16 = jnp.bfloat16


def xor_send(value, axis, step):
    size = lax.axis_size(axis)
    return lax.ppermute(value, axis, [(i, i ^ step) for i in range(size)])


def far_first(count):
    return [0, *range(count // 2, count), *range(1, count // 2)]


def chip_sends(parts):
    moved = [parts[0]] + [None] * (len(parts) - 1)
    for k in far_first(len(parts))[1:]:
        moved[k] = xor_send(parts[k], "blk", 2 * k)
    return moved


def reordered(parts):
    return [parts[k] for k in far_first(len(parts))]


def restored(parts):
    found = [None] * len(parts)
    for part, k in zip(parts, far_first(len(parts))):
        found[k] = part
    return found


VMEM = pl.BlockSpec(memory_space=pltpu.VMEM)
SMEM = pl.BlockSpec(memory_space=pltpu.SMEM)


def local_call(kernel, operands, outs, smem=0, scratch=(), flops=0, transcendentals=0):
    moved = sum(x.size * x.dtype.itemsize for x in list(operands) + list(outs))
    return pl.pallas_call(
        kernel,
        out_shape=list(outs),
        in_specs=[SMEM] * smem + [VMEM] * (len(operands) - smem),
        out_specs=[VMEM] * len(outs),
        scratch_shapes=list(scratch),
        compiler_params=pltpu.CompilerParams(vmem_limit_bytes=8 << 20),
        cost_estimate=pl.CostEstimate(
            flops=flops, bytes_accessed=moved, transcendentals=transcendentals
        ),
    )(*operands)


def shaped(shape, dtype=BF16):
    return jax.ShapeDtypeStruct(tuple(shape), dtype)


def after(value, *others):
    return lax.optimization_barrier((value,) + others)[0]


def place_kernel(order, *refs):
    parts, out = refs[:-1], refs[-1]
    for k, part in enumerate(parts):
        size = part.shape[0]
        out[pl.ds(pl.multiple_of(order(k) * size, size), size), :] = part[...]


def place(parts, order):
    rows, cols = parts[0].shape
    out = shaped((len(parts) * rows, cols))
    return local_call(functools.partial(place_kernel, order), parts, [out])[0]


def stack_order(stride):
    return lambda k: (lax.axis_index("req") // stride) % 2 ^ k


def req_stack(value, moved, stride):
    return place([value, moved], stack_order(stride))


def req_split(values, moved, strides, rows):
    ins, outs = [], []
    for value, other, size in zip(values, moved, rows):
        ins += [value, other]
        outs += [shaped((2 * n, value.shape[1])) for n in (size, value.shape[0] - size)]
    orders = [stack_order(stride) for stride in strides]
    return local_call(functools.partial(split_kernel, orders), ins, outs)


def double_place_kernel(orders, *refs):
    ins, outs = refs[: 2 * len(orders)], refs[2 * len(orders) :]
    for i, order in enumerate(orders):
        place_kernel(order, *ins[2 * i : 2 * i + 2], outs[i])


def req_stack_two(values, moved, strides):
    ins, outs = [], []
    for value, other in zip(values, moved):
        ins += [value, other]
        outs.append(shaped((2 * value.shape[0], value.shape[1])))
    orders = [stack_order(stride) for stride in strides]
    return local_call(functools.partial(double_place_kernel, orders), ins, outs)


def gather_on(value, strides):
    for stride in strides[1:-1]:
        value = req_stack(value, xor_send(value, "req", stride), stride)
    return value, xor_send(value, "req", strides[-1])


def part_owner(part, strides):
    owner = 0
    for i, stride in enumerate(strides):
        owner += stride * ((part >> i) & 1)
    return owner


def pack_projection(query, pair, out, at):
    depth = query.shape[0]
    value = pair[1]
    out[at : at + depth, :] = jnp.concatenate([query[...], pair[0]], axis=1)
    tail = jnp.concatenate([value[: depth // 2], value[depth // 2 :]], axis=1)
    out[at + depth : at + depth + depth // 2, :] = tail


def packed_projection(ref, at, depth, width):
    head = ref[at : at + depth, :]
    tail = ref[at + depth : at + depth + depth // 2, :]
    value = jnp.concatenate([tail[:, :width], tail[:, width:]], axis=0)
    return head[:, :width], head[:, width:], value


def beside(block, width):
    return jnp.concatenate([block[:width], block[width:]], axis=1)


def stacked(block, width):
    return jnp.concatenate([block[:, :width], block[:, width:]], axis=0)


def pack_cross_kernel(query, out, packed):
    depth = query.shape[0]
    packed[: depth // 2, :] = beside(query[...], depth // 2)
    packed[depth // 2 :, :] = out[...]


def pack_kernel(*refs):
    q1, kv1, kv2, ff, o1, o3, first, rest_a, rest_b, wide_ref = refs
    depth, lanes = q1.shape[0], first.shape[1]
    done = depth + depth // 2
    pack_projection(q1, kv1, first, 0)
    first[done:, :] = o1[...]
    rest_a[: depth // 2, :] = beside(kv2[0], depth // 2)
    rest_a[depth // 2 : depth, :] = beside(kv2[1], depth // 2)
    span = wide_ref.shape[1] // 2
    wide_ref[...] = jnp.zeros(wide_ref.shape, wide_ref.dtype)
    for i in range(2):
        block = ff[i].astype(F32).T.astype(BF16)
        wide_ref[:, i * span : i * span + block.shape[1]] = block
    blocks = [wide_ref[:, at : at + lanes] for at in range(0, wide_ref.shape[1], lanes)]
    count_a = rest_a.shape[0] // depth - 1
    for i, block in enumerate(blocks):
        out, at = (rest_a, i + 1) if i < count_a else (rest_b, i - count_a)
        out[at * depth : (at + 1) * depth, :] = block
    rest_b[rest_b.shape[0] - o3.shape[0] :, :] = o3[...]


def weave_kernel(count, all_parts, rest_a, rest_b, out_a, out_b):
    size, width = all_parts.shape[0] // count, all_parts.shape[1] // 2
    parts = [all_parts[k * size : (k + 1) * size, :] for k in range(count)]
    half_depth = size - width
    for k in range(0, count, 2):
        pair = [stacked(part[:half_depth, :], width) for part in parts[k : k + 2]]
        out_a[k * half_depth : (k + 2) * half_depth, :] = jnp.concatenate(pair, axis=1)
    for k, part in enumerate(parts):
        out_b[k * width : (k + 1) * width, :] = part[half_depth:, :]
    out_a[count * half_depth :, :] = rest_a[...]
    out_b[count * width :, :] = rest_b[...]


def split_kernel(orders, *refs):
    ins, outs = refs[: 2 * len(orders)], refs[2 * len(orders) :]
    for i, order in enumerate(orders):
        head, tail = outs[2 * i : 2 * i + 2]
        at = head.shape[0] // 2
        for k, part in enumerate(ins[2 * i : 2 * i + 2]):
            for out, rows in ((head, part[:at, :]), (tail, part[at:, :])):
                size = rows.shape[0]
                out[pl.ds(pl.multiple_of(order(k) * size, size), size), :] = rows


def join_kernel(taken, first, *outs):
    tokens = outs[0].shape[0]
    outs[0][...] = taken[:tokens, :]
    for k, out in enumerate(outs[1:], 1):
        out[:tokens, :] = taken[k * tokens : (k + 1) * tokens, :]
        out[tokens:, :] = first[...]


def project_kernel(tokens, heads_dev, states_ref, gain_ref, first, *refs):
    parts, (query_ref, fresh_ref, share_ref, normed_ref) = refs[:-4], refs[-4:]
    states = states_ref[...].astype(F32)
    mean_square = jnp.mean(states * states, axis=-1, keepdims=True)
    normed = states * lax.rsqrt(mean_square + EPSILON) * gain_ref[0:1, :]
    normed_ref[...] = normed.astype(BF16)
    size = share_ref.shape[0]
    blk = lax.axis_index("blk")
    spot = lax.rem(blk, 2) * (states.shape[0] // (2 * size)) + blk // 2
    share_ref[...] = states_ref[pl.ds(pl.multiple_of(spot * size, size), size), :]
    width = heads_dev * HD
    depth = normed_ref.shape[1] // (1 + len(parts))
    query, key, value = 0.0, 0.0, 0.0
    for k, part in enumerate([first, *parts]):
        at = 0 if k == 0 else tokens
        owner = lax.axis_index("req") ^ k
        rows = normed_ref[:, pl.ds(pl.multiple_of(owner * depth, depth), depth)]
        w_query, w_key, w_value = packed_projection(part, at, depth, width)
        query = query + lax.dot_general(
            w_query, rows, (((0,), (1,)), ((), ())), preferred_element_type=F32
        )
        key = key + jnp.dot(rows, w_key, preferred_element_type=F32)
        value = value + jnp.dot(rows, w_value, preferred_element_type=F32)
    pieces = []
    for head in range(heads_dev):
        own = slice(head * HD, (head + 1) * HD)
        query_ref[head, :HD, :] = query[own, :].astype(BF16)
        query_ref[head, HD:, :] = jnp.zeros((HD, query.shape[1]), BF16)
        pieces += [key[:, own], value[:, own]]
    fresh_ref[...] = jnp.concatenate(pieces, axis=1).astype(BF16)


def cut_kernel(order_ref, cache_ref, *outs):
    kept, given = outs[:-1], outs[-1]
    tokens, cols = kept[0].shape
    core = lax.rem(lax.axis_index("blk"), 2)
    own = pl.ds(pl.multiple_of(core * cols, cols), cols)
    other = pl.ds(pl.multiple_of((1 - core) * cols, cols), cols)
    for k, out in enumerate(kept):
        slot = order_ref[lax.axis_index("req") ^ k]
        out[...] = cache_ref[slot, :, own]
        given[k * tokens : (k + 1) * tokens, :] = cache_ref[slot, :, other]


def cut_cache(cache_in, slot_order):
    count, tokens, cols = cache_in.shape[0], cache_in.shape[1], cache_in.shape[2] // 2
    outs = [shaped((tokens, cols))] * count + [shaped((count * tokens, cols))]
    return local_call(cut_kernel, [slot_order, cache_in], outs, smem=1)


def turn_kernel(count, *refs):
    parts, outs = refs[:count], refs[count:]
    shift = lax.axis_index("req") ^ (lax.axis_index("blk") // 2)
    for case in range(count):

        @pl.when(shift == case)
        def _(case=case):
            for k in range(count):
                outs[k][...] = parts[k ^ case][: outs[k].shape[0], :]


def turn(parts):
    outs = [shaped(parts[0].shape)] * len(parts)
    return local_call(functools.partial(turn_kernel, len(parts)), parts, outs)


def band_kernel(heads_dev, cache_len, widths, order_ref, old_ref, bias_ref, bucket_ref, *refs):
    out_ref, line_ref, row_ref = refs
    head = lax.axis_index("blk") * heads_dev + pl.program_id(0)
    old_len = old_ref[order_ref[lax.axis_index("req")]]
    heads = lax.broadcasted_iota(jnp.int32, bias_ref.shape, 0)
    bias = jnp.sum(jnp.where(heads == head, bias_ref[...], 0.0), axis=0, keepdims=True)
    buckets = bucket_ref[...]
    copies, size = line_ref.shape
    line_ref[:, :cache_len] = jnp.broadcast_to(buckets[:, :1], (copies, cache_len))
    line_ref[:, cache_len:] = jnp.broadcast_to(buckets, (copies, size - cache_len))
    start = 0
    done = 0
    rows = (widths[1] + TILE) // 2
    for width, first in zip(widths, (old_len + 1, cache_len - rows + 1)):
        turned = pltpu.roll(line_ref[...], size - first, 1)[:, : width + TILE]
        row = jnp.zeros(turned.shape, F32)
        for bucket in range(bias_ref.shape[1]):
            row = jnp.where(turned == bucket, bias[:, bucket : bucket + 1], row)
        row_ref[:, start : start + width + TILE] = row
        for u in range(0, width, TILE):
            window = row_ref[0:1, start + u : start + u + 2 * TILE]
            wide = jnp.broadcast_to(window, (TILE, 2 * TILE))
            skewed = pltpu.roll(wide, TILE + 1, 1, stride=1, stride_axis=0)
            out_ref[0, :, done + u : done + u + TILE] = skewed[:, :TILE]
        start += width + TILE
        done += width


def make_band(bucket_of, rel_bias, slot_order, cache_lengths, heads_dev, cache_len, rows):
    widths = (cache_len - TILE + rows, 2 * rows - TILE)
    total = sum(widths)
    return pl.pallas_call(
        functools.partial(band_kernel, heads_dev, cache_len, widths),
        grid=(heads_dev,),
        out_shape=jax.ShapeDtypeStruct((heads_dev, TILE, total), F32),
        in_specs=[SMEM, SMEM, VMEM, VMEM],
        out_specs=pl.BlockSpec((1, TILE, total), lambda h: (h, 0, 0)),
        scratch_shapes=[
            pltpu.VMEM((8, cache_len + bucket_of.shape[0]), jnp.int32),
            pltpu.VMEM((8, total + 2 * TILE), F32),
        ],
        compiler_params=pltpu.CompilerParams(vmem_limit_bytes=12 << 20),
        cost_estimate=pl.CostEstimate(
            flops=8 * heads_dev * TILE * total,
            bytes_accessed=4 * heads_dev * TILE * total,
            transcendentals=0,
        ),
    )(slot_order, cache_lengths, rel_bias.T, bucket_of[None, :])


def self_kernel(cache_len, places, first_call, last_call, *refs):
    order_ref, old_ref, new_ref, query_ref, band_ref = refs[:5]
    count = len(places)
    blocks, refs = refs[5 : 5 + count], refs[5 + count :]
    if first_call:
        fresh_ref, refs = refs[0], refs[1:]
    else:
        (total_in, top_in, norm_in), refs = refs[:3], refs[3:]
    if last_call:
        (kept_ref, given_ref), refs = refs[:2], refs[2:]
    total_ref, top_ref, norm_ref, score_ref = refs
    slot = order_ref[lax.axis_index("req")]
    old_len, new_len = old_ref[slot], new_ref[slot]
    rows = query_ref.shape[2]
    wide_old = cache_len - TILE + rows
    blk = lax.axis_index("blk")

    def attend(keys_values, begin, admit):
        size = keys_values.shape[0]
        top = top_ref[0]
        score_ref[:size, :] = jnp.dot(
            keys_values, query_ref[0], preferred_element_type=F32
        )
        for t in range(0, size, TILE):
            bias = band_ref[0, :, pl.ds(pl.multiple_of(begin - t, TILE), rows)]
            scores = score_ref[t : t + TILE, :] + bias
            scores = jnp.where(admit(t), scores, NEG_FILL)
            score_ref[t : t + TILE, :] = scores
            top = jnp.maximum(top, jnp.max(scores, axis=0, keepdims=True))
        weights = jnp.exp(score_ref[:size, :] - top)
        keep = jnp.exp(top_ref[0] - top)
        norm_ref[0] = norm_ref[0] * keep + jnp.sum(weights, axis=0, keepdims=True)
        term = lax.dot_general(
            keys_values, weights.astype(BF16), (((0,), (0,)), ((), ())),
            preferred_element_type=F32,
        )
        total_ref[0] = total_ref[0] * keep + term
        top_ref[0] = top

    if first_call:
        top_ref[...] = jnp.full(top_ref.shape, NEG_FILL, F32)
        norm_ref[...] = jnp.zeros(norm_ref.shape, F32)
        total_ref[...] = jnp.zeros(total_ref.shape, F32)

        def admit_fresh(t):
            keys = t + lax.broadcasted_iota(jnp.int32, (TILE, rows), 0)
            ids = lax.broadcasted_iota(jnp.int32, (TILE, rows), 1)
            return (keys <= ids) & (keys < new_len)

        attend(fresh_ref[...], wide_old + rows - TILE, admit_fresh)
    else:
        top_ref[...] = top_in[...]
        norm_ref[...] = norm_in[...]
        total_ref[...] = total_in[...]

    for block, place_of in zip(blocks, places):
        first = (blk ^ place_of) * block.shape[0]

        @pl.when(first < old_len)
        def _(block=block, first=first):
            def admit(t):
                keys = first + t + lax.broadcasted_iota(jnp.int32, (TILE, rows), 0)
                return keys < old_len

            attend(block[...], cache_len - TILE - first, admit)

    if last_call:
        total_ref[0, :HD, :] = total_ref[0, HD:, :] / norm_ref[0]
        half = rows // 2
        for out_ref, core in ((kept_ref, lax.rem(blk, 2)), (given_ref, 1 - lax.rem(blk, 2))):
            spot = pl.ds(pl.multiple_of(core * half, half), half)
            out_ref[0] = total_ref[0, :HD, spot].astype(BF16)


def self_attend(lens, query_t, band, blocks, places, cache_len, fresh=None, state=None, last_call=False):
    heads_dev, pair, rows = query_t.shape
    count, tokens = len(blocks), blocks[0].shape[0]
    first_call = state is None
    head_block = lambda *tail: pl.BlockSpec((1,) + tail, lambda h: (h, 0, 0))
    in_specs = [SMEM] * 3 + [
        head_block(pair, rows),
        head_block(TILE, band.shape[2]),
    ] + [pl.BlockSpec((tokens, pair), lambda h: (0, h))] * count
    held = [(pair, rows), (1, rows), (1, rows)]
    score = pltpu.VMEM((max(tokens, rows), rows), F32)
    if first_call:
        in_specs.append(pl.BlockSpec((rows, pair), lambda h: (0, h)))
        more = [fresh]
    else:
        in_specs += [head_block(*shape) for shape in held]
        more = list(state)
    if not last_call:
        out_specs = [head_block(*shape) for shape in held]
        out_shape = [jax.ShapeDtypeStruct((heads_dev,) + shape, F32) for shape in held]
        scratch = [score]
    else:
        out_specs = [head_block(HD, rows // 2)] * 2
        out_shape = [shaped((heads_dev, HD, rows // 2))] * 2
        scratch = [pltpu.VMEM((1,) + shape, F32) for shape in held] + [score]
    keys_all = count * tokens + (rows if first_call else 0)
    return pl.pallas_call(
        functools.partial(self_kernel, cache_len, places, first_call, last_call),
        grid=(heads_dev,),
        in_specs=in_specs,
        out_specs=out_specs,
        out_shape=out_shape,
        scratch_shapes=scratch,
        compiler_params=pltpu.CompilerParams(vmem_limit_bytes=16 << 20),
        cost_estimate=pl.CostEstimate(
            flops=4 * heads_dev * pair * rows * keys_all,
            bytes_accessed=2 * heads_dev * pair * keys_all + 4 * band.size,
            transcendentals=heads_dev * rows * keys_all,
        ),
    )(*lens, query_t, band, *blocks, *more)


def project_out(lefts, weights, skip, depth, owners, partial_ref):
    stride = weights[0].shape[0] // len(owners)
    width = weights[0].shape[1]
    for part, owner in enumerate(owners):
        total = 0.0
        for left, weight in zip(lefts, weights):
            block = weight[part * stride + skip : part * stride + skip + depth, :]
            total = total + lax.dot_general(
                left, block, (((0,), (0,)), ((), ())), preferred_element_type=F32
            )
        partial_ref[:, owner * width : (owner + 1) * width] = total.astype(BF16)


def tail_kernel(skip, *refs):
    parts, out = refs[:-1], refs[-1]
    size = out.shape[0] // len(parts)
    for k, part in enumerate(parts):
        at = skip[0] if k == 0 else skip[1]
        spot = (lax.axis_index("req") ^ k) * size
        out[pl.ds(pl.multiple_of(spot, size), size), :] = part[at : at + size, :]


def self_out_kernel(owners, *refs):
    kept, taken, w_own, w_other = refs[:4]
    outs, partial_ref = refs[4:-1], refs[-1]
    lefts = [kept[...], taken[...]]
    project_out(lefts, (w_own, w_other), 0, kept.shape[0], owners, partial_ref)
    chip = lax.axis_index("blk") // 2
    for k, out in enumerate(outs):
        size = out.shape[0]
        out[...] = partial_ref[pl.ds(pl.multiple_of((chip ^ k) * size, size), size), :]


def sum_rows(parts, residual_ref):
    total = residual_ref[...].astype(F32)
    moved = parts[0][...].astype(F32)
    for part in parts[1:]:
        moved = moved + part[...].astype(F32)
    return total + moved


def norm_rows(total, gain):
    mean_square = jnp.mean(total * total, axis=-1, keepdims=True)
    return (total * lax.rsqrt(mean_square + EPSILON) * gain).astype(BF16)


def query_kernel(owners, count, *refs):
    gain_ref, residual_ref, refs = refs[0], refs[1], refs[2:]
    parts, weights, (total_ref, *outs) = refs[:count], refs[count : count + 2], refs[count + 2 :]
    total = sum_rows(parts, residual_ref)
    total_ref[...] = total
    normed = norm_rows(total, gain_ref[1:2, :])
    depth = normed.shape[1] // len(owners)
    stride = weights[0].shape[0] // len(owners)
    width = outs[0].shape[1] // 2
    for pair in range(count // 2):
        found = []
        for w in weights:
            query = 0.0
            for part, owner in enumerate(owners):
                at = part * stride + pair * depth
                query = query + jnp.dot(
                    normed[:, owner * depth : (owner + 1) * depth],
                    w[at : at + depth, :],
                    preferred_element_type=F32,
                )
            found.append(query)
        for k in range(2):
            own = slice(k * width, (k + 1) * width)
            both = jnp.concatenate([query[:, own] for query in found], axis=1)
            outs[2 * pair + k][...] = both.astype(BF16)


def cross_out_kernel(owners, count, *refs):
    gain_ref, residual_ref, refs = refs[0], refs[1], refs[2:]
    blocks, weights, (total_ref, normed_ref) = (
        refs[:count], refs[count : count + 2], refs[count + 2 :],
    )
    width = blocks[0].shape[1] // 2
    stride = weights[0].shape[0] // len(owners)
    lanes = weights[0].shape[1]
    for part, owner in enumerate(owners):
        total = 0.0
        for i, w in enumerate(weights):
            left = [block[:, i * width : (i + 1) * width] for block in blocks]
            total = total + jnp.dot(
                jnp.concatenate(left, axis=1),
                w[part * stride : part * stride + count * width, :],
                preferred_element_type=F32,
            )
        cols = slice(owner * lanes, (owner + 1) * lanes)
        total_ref[:, cols] = residual_ref[:, cols] + total
    normed_ref[...] = norm_rows(total_ref[...], gain_ref[2:3, :])


def sum_kernel(*refs):
    residual_ref, parts, out_ref = refs[0], refs[1:-1], refs[-1]
    out_ref[...] = sum_rows(parts, residual_ref).astype(BF16)


def fill_rows(blocks, rows_ref):
    for k, block in enumerate(blocks):
        size = block.shape[0]
        rows_ref[k * size : (k + 1) * size, :] = block[...]


def hand_rows(outs, partial_ref):
    for k, out in enumerate(outs):
        size = out.shape[0]
        out[...] = partial_ref[k * size : (k + 1) * size, :]


def pair_kernel(owners, rows_ref, *refs):
    weights, outs = refs[:2], refs[2:]
    width = outs[0].shape[1]
    depth = rows_ref.shape[1] // len(owners)
    for core, weight in enumerate(weights):
        stride = weight.shape[0] // len(owners)
        for i in range(2):
            total = 0.0
            for part, owner in enumerate(owners):
                rows = rows_ref[:, owner * depth : (owner + 1) * depth]
                at = (part + 1) * stride - depth + i * (depth // 2)
                block = stacked(weight[at : at + depth // 2, :], width)
                total = total + jnp.dot(rows, block, preferred_element_type=F32)
            outs[2 * i + core][...] = total.astype(BF16)


def cross_kernel(count, heads_dev, order_ref, enc_ref, *refs):
    blocks, keys, values = refs[:count], refs[count : count + 2], refs[count + 2 : count + 4]
    outs, rows_ref = refs[count + 4 : -1], refs[-1]
    fill_rows(blocks, rows_ref)
    width = heads_dev * HD
    enc_len = enc_ref[order_ref[lax.axis_index("req")]]
    contexts = []
    for core, (key_ref, value_ref) in enumerate(zip(keys, values)):
        query = rows_ref[:, core * width : (core + 1) * width]
        head_of = lax.broadcasted_iota(jnp.int32, query.shape, 1) // HD
        for head in range(heads_dev):
            own_query = jnp.where(head_of == head, query, jnp.zeros_like(query))
            scores = lax.dot_general(
                key_ref[...], own_query, (((1,), (1,)), ((), ())), preferred_element_type=F32
            )
            admitted = lax.broadcasted_iota(jnp.int32, scores.shape, 0) < enc_len
            scores = jnp.where(admitted, scores, NEG_FILL)
            weights = jnp.exp(scores - jnp.max(scores, axis=0, keepdims=True))
            norm = jnp.sum(weights, axis=0, keepdims=True)
            context = lax.dot_general(
                value_ref[...], weights.astype(BF16), (((0,), (0,)), ((), ())),
                preferred_element_type=F32,
            )
            contexts.append(context[head * HD : (head + 1) * HD, :] / norm)
    context = jnp.concatenate(contexts, axis=0).T.astype(BF16)
    for k, out in enumerate(outs):
        size = out.shape[0]
        out[...] = context[k * size : (k + 1) * size, :]


def ffn_kernel(owners_a, owners_b, count, hidden_dev, *refs):
    blocks, weights_a, weights_b = refs[:count], refs[count : count + 2], refs[count + 2 : count + 4]
    outs, (rows_ref, partial_ref) = refs[count + 4 : -2], refs[-2:]
    fill_rows(blocks, rows_ref)
    depth = rows_ref.shape[1] // len(owners_a)
    stride_a = weights_a[0].shape[0] // len(owners_a)
    stride_b = weights_b[0].shape[0] // len(owners_b)
    hiddens = []
    for w_a, w_b in zip(weights_a, weights_b):
        totals = []
        for w, owners, stride, last in (
            (w_a, owners_a, stride_a, stride_a),
            (w_b, owners_b, stride_b, stride_b - hidden_dev),
        ):
            for block in range(last // depth):
                total = 0.0
                for part, owner in enumerate(owners):
                    at = part * stride + block * depth
                    total = total + jnp.dot(
                        rows_ref[:, owner * depth : (owner + 1) * depth],
                        w[at : at + depth, :],
                        preferred_element_type=F32,
                    )
                totals.append(total)
        both = jnp.concatenate(totals, axis=1)
        span = both.shape[1] // 2
        hidden = jax.nn.gelu(both[:, :span], approximate=True) * both[:, span:]
        hiddens.append(hidden[:, :hidden_dev].astype(BF16))
    lanes = weights_b[0].shape[1]
    for part, owner in enumerate(owners_b):
        total = 0.0
        for hidden, w in zip(hiddens, weights_b):
            at = (part + 1) * stride_b - hidden_dev
            total = total + jnp.dot(
                hidden, w[at : at + hidden_dev, :], preferred_element_type=F32
            )
        partial_ref[:, owner * lanes : (owner + 1) * lanes] = total.astype(BF16)
    hand_rows(outs, partial_ref)


def per_device(
    new_states,
    encoder_out,
    cache_in,
    slot_order,
    new_lengths,
    cache_lengths,
    enc_lengths,
    bucket_of,
    rel_bias,
    norm_gain,
    self_q,
    self_kv,
    self_out,
    cross_q,
    cross_kv,
    cross_out,
    ff_in,
    ff_out,
):
    req_count, blk_count = lax.axis_size("req"), lax.axis_size("blk")
    chips = blk_count // 2
    heads_dev = H // blk_count
    width_dev = heads_dev * HD
    rows, width = new_states.shape
    half, share = rows // 2, rows // blk_count
    depth, hidden_dev = self_q.shape[0], ff_in.shape[2]
    up_strides = [1 << i for i in range(req_count.bit_length() - 1)]
    down_strides = up_strides[::-1]
    down_owners = [part_owner(p, down_strides) for p in range(req_count)]

    lanes = 2 * width_dev
    tokens = cache_in.shape[1]
    *kept, given = cut_cache(cache_in, slot_order)
    band = make_band(
        bucket_of, rel_bias, slot_order, cache_lengths, heads_dev, tokens * blk_count, rows
    )
    near_req = [kept[0]] + [xor_send(kept[k], "req", k) for k in range(1, req_count)]
    cross = local_call(
        pack_cross_kernel,
        [after(cross_q, kept[0]), cross_out],
        [shaped((depth // 2 + width_dev, lanes))],
    )[0]
    for step in range(chips.bit_length() - 1):
        cross = place([cross, xor_send(cross, "blk", 2 << step)], lambda k: k)
        cross_first = cross if step == 0 else cross_first
    taken = xor_send(given, "blk", 1)
    skip = depth + depth // 2
    packed_in = [self_q, self_kv, cross_kv, ff_in, self_out, ff_out]
    packed_in[1], packed_in[2] = jnp.moveaxis(self_kv, 1, 0), jnp.moveaxis(cross_kv, 1, 0)
    packed_in[3] = ff_in.transpose(1, 2, 0)
    packed_in[0] = after(packed_in[0], kept[0])
    wide_cols = 2 * TILE * -(-hidden_dev // TILE)
    blocks_in = wide_cols // lanes
    blocks_a = -(-blocks_in // 2)
    first, rest_a, rest_b = local_call(
        pack_kernel,
        packed_in,
        [
            shaped((skip + width_dev, lanes)),
            shaped((depth + blocks_a * depth, lanes)),
            shaped(((blocks_in - blocks_a) * depth + hidden_dev, lanes)),
        ],
        scratch=[pltpu.VMEM((depth, wide_cols), BF16)],
    )

    all_depth = chips * (depth // 2)
    later_a, later_b = local_call(
        functools.partial(weave_kernel, chips),
        [cross, rest_a, rest_b],
        [
            shaped((all_depth + rest_a.shape[0], lanes)),
            shaped((chips * width_dev + rest_b.shape[0], lanes)),
        ],
    )

    joined = shaped((tokens + first.shape[0], taken.shape[1]))
    joined = local_call(
        join_kernel,
        [taken, first],
        [shaped((tokens, taken.shape[1]))] + [joined] * (req_count - 1),
    )
    near = list(turn([after(near_req[0], joined[0], cross_first), *near_req[1:]]))
    far_req = [joined[0]]
    far_req += [
        xor_send(after(joined[k], near[0]), "req", k) for k in range(1, req_count - 1)
    ]
    far_req.append(xor_send(after(joined[-1], near[0], cross), "req", req_count - 1))
    near[1] = after(near[1], far_req[1])
    near = chip_sends(near)
    far = turn([after(far_req[0], band, later_a, *near[1:]), *far_req[1:]])
    far = chip_sends(far)

    def token_order(i):
        here = lax.axis_index("blk")
        return 2 * ((here // 2) ^ (i % chips)) + (lax.rem(here, 2) ^ (i // chips))

    cache_own = place(near + far, token_order)

    w_self_out = local_call(
        functools.partial(tail_kernel, (skip, tokens + skip)),
        [first, *far_req[1:]],
        [shaped((req_count * width_dev, self_out.shape[1]))],
    )[0]
    w_self_out = (w_self_out, xor_send(w_self_out, "blk", 1))

    query_t, fresh, residual = local_call(
        functools.partial(project_kernel, tokens, heads_dev),
        [new_states, norm_gain, first, *far_req[1:]],
        [
            shaped((heads_dev, 2 * HD, rows)),
            shaped((rows, 2 * width_dev)),
            shaped((share, width)),
        ],
        scratch=[pltpu.VMEM((rows, width), BF16)],
        flops=6 * rows * width * width_dev,
    )
    lens = (slot_order, cache_lengths, new_lengths)
    near_places = [2 * k for k in range(chips)]
    far_places = [2 * k + 1 for k in range(chips)]
    cache_len = tokens * blk_count
    state = self_attend(
        lens,
        query_t,
        band,
        [far[0], *reordered(near)],
        [far_places[0], *reordered(near_places)],
        cache_len,
        fresh=fresh,
    )
    state = self_attend(
        lens, query_t, band, far[1 : chips // 2], far_places[1 : chips // 2], cache_len, state=state
    )

    moved_a = xor_send(after(later_a, far[0]), "req", up_strides[0])
    moved_b = xor_send(after(later_b, far[0]), "req", down_strides[0])
    w_query, w_wide, w_cross, w_down = req_split(
        [after(later_a, state[0], *far[1:]), later_b],
        [moved_a, moved_b],
        [up_strides[0], down_strides[0]],
        [all_depth + depth, chips * width_dev],
    )
    w_query, moved_a = gather_on(w_query, up_strides)
    w_cross, moved_b = gather_on(w_cross, down_strides)
    kept, given = self_attend(
        lens,
        query_t,
        band,
        far[chips // 2 :],
        far_places[chips // 2 :],
        cache_len,
        state=state,
        last_call=True,
    )
    kept, given = kept.reshape(width_dev, half), given.reshape(width_dev, half)

    parts_out = [shaped((share, width))] * chips
    partial_ref = pltpu.VMEM((half, width), BF16)
    parts = local_call(
        functools.partial(self_out_kernel, range(req_count)),
        [kept, xor_send(given, "blk", 1), *w_self_out],
        parts_out,
        scratch=[partial_ref],
        flops=4 * half * width * width_dev,
    )


    parts = chip_sends(parts)
    last = [up_strides[-1], down_strides[-1]]
    w_query, w_cross = req_stack_two(
        [after(w_query, *parts[1:]), w_cross], [moved_a, moved_b], last
    )
    w_query = (w_query, xor_send(w_query, "blk", 1))
    w_cross = (w_cross, xor_send(w_cross, "blk", 1))
    residual = after(residual, w_cross[1])
    w_wide, moved_a = gather_on(after(w_wide, *parts[1:]), up_strides)
    w_down, moved_b = gather_on(after(w_down, *parts[1:]), down_strides)
    total, *queries = local_call(
        functools.partial(query_kernel, range(req_count), chips),
        [norm_gain, residual, *reordered(parts), *w_query],
        [shaped((share, width), F32)] + [shaped((share, lanes))] * chips,
        flops=2 * share * width * width,
    )
    residual = total
    enc_rows = encoder_out.shape[0]
    pairs = local_call(
        functools.partial(pair_kernel, range(req_count)),
        [encoder_out, *w_query],
        [shaped((enc_rows, width_dev))] * 4,
        flops=8 * enc_rows * width * width_dev,
    )
    contexts = local_call(
        functools.partial(cross_kernel, chips, heads_dev),
        [slot_order, enc_lengths, *reordered(chip_sends(queries)), *pairs],
        [shaped((share, lanes))] * chips,
        smem=2,
        scratch=[pltpu.VMEM((half, lanes), BF16)],
        flops=8 * half * width_dev * heads_dev * enc_rows,
        transcendentals=2 * heads_dev * half * enc_rows,
    )
    contexts = chip_sends(restored(contexts))

    residual, normed = local_call(
        functools.partial(cross_out_kernel, down_owners, chips),
        [norm_gain, residual, *contexts, *w_cross],
        [shaped((share, width), F32), shaped((share, width))],
        flops=2 * share * width * width,
    )
    blocks = chip_sends([normed] * chips)
    w_wide, w_down = req_stack_two([after(w_wide, normed), w_down], [moved_a, moved_b], last)
    w_wide = (w_wide, xor_send(w_wide, "blk", 1))
    w_down = (w_down, xor_send(w_down, "blk", 1))

    parts = local_call(
        functools.partial(ffn_kernel, range(req_count), down_owners, chips, hidden_dev),
        [*reordered(blocks), *w_wide, *w_down],
        parts_out,
        scratch=[partial_ref, partial_ref],
        flops=12 * half * width * hidden_dev,
        transcendentals=2 * half * hidden_dev,
    )
    final = local_call(
        sum_kernel,
        [residual, *reordered(chip_sends(restored(parts)))],
        [shaped((share, width))],
    )[0]

    same = chip_sends([after(final, cache_own)] * chips)
    both = same + [xor_send(part, "blk", 1) for part in same]

    def row_order(i):
        here = lax.axis_index("blk")
        core_at = lax.rem(here, 2) ^ (i // chips)
        return core_at * chips + ((here // 2) ^ (i % chips))

    layer_out = place(both, row_order)
    return (layer_out, cache_own[None])


def solution(mesh):
    in_specs = (
        P("req", None),
        P("req", None),
        P(None, "blk", "req"),
        P(),
        P(),
        P(),
        P(),
        P(),
        P(),
        P(),
        P("req", "blk"),
        P("req", None, "blk"),
        P("blk", "req"),
        P("req", "blk"),
        P("req", None, "blk"),
        P("blk", "req"),
        P("req", None, "blk"),
        P("blk", "req"),
    )
    out_specs = (P("req", None), P("req", None, "blk"))
    return jax.shard_map(
        per_device, mesh=mesh, in_specs=in_specs, out_specs=out_specs, check_vma=False
    )
```

```python
import functools

import jax
import jax.numpy as jnp
from jax import lax
from jax.experimental import pallas as pl
from jax.experimental.pallas import tpu as pltpu
from jax.sharding import PartitionSpec as P

H = 16
HD = 64
EPSILON = 1e-06
NEG_FILL = -1e30
TILE = 128
F32 = jnp.float32
BF16 = jnp.bfloat16


def xor_send(value, axis, step):
    size = lax.axis_size(axis)
    return lax.ppermute(value, axis, [(i, i ^ step) for i in range(size)])


def far_first(count):
    return [0, *range(count // 2, count), *range(1, count // 2)]


def chip_sends(parts):
    moved = [parts[0]] + [None] * (len(parts) - 1)
    for k in far_first(len(parts))[1:]:
        moved[k] = xor_send(parts[k], "blk", 2 * k)
    return moved


def reordered(parts):
    return [parts[k] for k in far_first(len(parts))]


def restored(parts):
    found = [None] * len(parts)
    for part, k in zip(parts, far_first(len(parts))):
        found[k] = part
    return found


VMEM = pl.BlockSpec(memory_space=pltpu.VMEM)
SMEM = pl.BlockSpec(memory_space=pltpu.SMEM)


def local_call(kernel, operands, outs, smem=0, scratch=(), flops=0, transcendentals=0):
    moved = sum(x.size * x.dtype.itemsize for x in list(operands) + list(outs))
    return pl.pallas_call(
        kernel,
        out_shape=list(outs),
        in_specs=[SMEM] * smem + [VMEM] * (len(operands) - smem),
        out_specs=[VMEM] * len(outs),
        scratch_shapes=list(scratch),
        compiler_params=pltpu.CompilerParams(vmem_limit_bytes=8 << 20),
        cost_estimate=pl.CostEstimate(
            flops=flops, bytes_accessed=moved, transcendentals=transcendentals
        ),
    )(*operands)


def shaped(shape, dtype=BF16):
    return jax.ShapeDtypeStruct(tuple(shape), dtype)


def after(value, *others):
    return lax.optimization_barrier((value,) + others)[0]


def place_kernel(order, *refs):
    parts, out = refs[:-1], refs[-1]
    for k, part in enumerate(parts):
        size = part.shape[0]
        out[pl.ds(pl.multiple_of(order(k) * size, size), size), :] = part[...]


def place(parts, order):
    rows, cols = parts[0].shape
    out = shaped((len(parts) * rows, cols))
    return local_call(functools.partial(place_kernel, order), parts, [out])[0]


def stack_order(stride):
    return lambda k: (lax.axis_index("req") // stride) % 2 ^ k


def req_stack(value, moved, stride):
    return place([value, moved], stack_order(stride))


def req_split(values, moved, strides, rows):
    ins, outs = [], []
    for value, other, size in zip(values, moved, rows):
        ins += [value, other]
        outs += [shaped((2 * n, value.shape[1])) for n in (size, value.shape[0] - size)]
    orders = [stack_order(stride) for stride in strides]
    return local_call(functools.partial(split_kernel, orders), ins, outs)


def double_place_kernel(orders, *refs):
    ins, outs = refs[: 2 * len(orders)], refs[2 * len(orders) :]
    for i, order in enumerate(orders):
        place_kernel(order, *ins[2 * i : 2 * i + 2], outs[i])


def req_stack_two(values, moved, strides):
    ins, outs = [], []
    for value, other in zip(values, moved):
        ins += [value, other]
        outs.append(shaped((2 * value.shape[0], value.shape[1])))
    orders = [stack_order(stride) for stride in strides]
    return local_call(functools.partial(double_place_kernel, orders), ins, outs)


def gather_on(value, strides):
    for stride in strides[1:-1]:
        value = req_stack(value, xor_send(value, "req", stride), stride)
    return value, xor_send(value, "req", strides[-1])


def part_owner(part, strides):
    owner = 0
    for i, stride in enumerate(strides):
        owner += stride * ((part >> i) & 1)
    return owner


def pack_projection(query, pair, out, at):
    depth = query.shape[0]
    value = pair[1]
    out[at : at + depth, :] = jnp.concatenate([query[...], pair[0]], axis=1)
    tail = jnp.concatenate([value[: depth // 2], value[depth // 2 :]], axis=1)
    out[at + depth : at + depth + depth // 2, :] = tail


def packed_projection(ref, at, depth, width):
    head = ref[at : at + depth, :]
    tail = ref[at + depth : at + depth + depth // 2, :]
    value = jnp.concatenate([tail[:, :width], tail[:, width:]], axis=0)
    return head[:, :width], head[:, width:], value


def beside(block, width):
    return jnp.concatenate([block[:width], block[width:]], axis=1)


def stacked(block, width):
    return jnp.concatenate([block[:, :width], block[:, width:]], axis=0)


def pack_cross_kernel(query, out, packed):
    depth = query.shape[0]
    packed[: depth // 2, :] = beside(query[...], depth // 2)
    packed[depth // 2 :, :] = out[...]


def pack_kernel(*refs):
    q1, kv1, kv2, ff, o1, o3, first, rest_a, rest_b, wide_ref = refs
    depth, lanes = q1.shape[0], first.shape[1]
    done = depth + depth // 2
    pack_projection(q1, kv1, first, 0)
    first[done:, :] = o1[...]
    rest_a[: depth // 2, :] = beside(kv2[0], depth // 2)
    rest_a[depth // 2 : depth, :] = beside(kv2[1], depth // 2)
    span = wide_ref.shape[1] // 2
    wide_ref[...] = jnp.zeros(wide_ref.shape, wide_ref.dtype)
    for i in range(2):
        block = ff[i].astype(F32).T.astype(BF16)
        wide_ref[:, i * span : i * span + block.shape[1]] = block
    blocks = [wide_ref[:, at : at + lanes] for at in range(0, wide_ref.shape[1], lanes)]
    count_a = rest_a.shape[0] // depth - 1
    for i, block in enumerate(blocks):
        out, at = (rest_a, i + 1) if i < count_a else (rest_b, i - count_a)
        out[at * depth : (at + 1) * depth, :] = block
    rest_b[rest_b.shape[0] - o3.shape[0] :, :] = o3[...]


def weave_kernel(count, all_parts, rest_a, rest_b, out_a, out_b):
    size, width = all_parts.shape[0] // count, all_parts.shape[1] // 2
    parts = [all_parts[k * size : (k + 1) * size, :] for k in range(count)]
    half_depth = size - width
    for k in range(0, count, 2):
        pair = [stacked(part[:half_depth, :], width) for part in parts[k : k + 2]]
        out_a[k * half_depth : (k + 2) * half_depth, :] = jnp.concatenate(pair, axis=1)
    for k, part in enumerate(parts):
        out_b[k * width : (k + 1) * width, :] = part[half_depth:, :]
    out_a[count * half_depth :, :] = rest_a[...]
    out_b[count * width :, :] = rest_b[...]


def split_kernel(orders, *refs):
    ins, outs = refs[: 2 * len(orders)], refs[2 * len(orders) :]
    for i, order in enumerate(orders):
        head, tail = outs[2 * i : 2 * i + 2]
        at = head.shape[0] // 2
        for k, part in enumerate(ins[2 * i : 2 * i + 2]):
            for out, rows in ((head, part[:at, :]), (tail, part[at:, :])):
                size = rows.shape[0]
                out[pl.ds(pl.multiple_of(order(k) * size, size), size), :] = rows


def join_kernel(taken, first, *outs):
    tokens = outs[0].shape[0]
    outs[0][...] = taken[:tokens, :]
    for k, out in enumerate(outs[1:], 1):
        out[:tokens, :] = taken[k * tokens : (k + 1) * tokens, :]
        out[tokens:, :] = first[...]


def project_kernel(tokens, heads_dev, states_ref, gain_ref, first, *refs):
    parts, (query_ref, fresh_ref, share_ref, normed_ref) = refs[:-4], refs[-4:]
    states = states_ref[...].astype(F32)
    mean_square = jnp.mean(states * states, axis=-1, keepdims=True)
    normed = states * lax.rsqrt(mean_square + EPSILON) * gain_ref[0:1, :]
    normed_ref[...] = normed.astype(BF16)
    size = share_ref.shape[0]
    blk = lax.axis_index("blk")
    spot = lax.rem(blk, 2) * (states.shape[0] // (2 * size)) + blk // 2
    share_ref[...] = states_ref[pl.ds(pl.multiple_of(spot * size, size), size), :]
    width = heads_dev * HD
    depth = normed_ref.shape[1] // (1 + len(parts))
    query, key, value = 0.0, 0.0, 0.0
    for k, part in enumerate([first, *parts]):
        at = 0 if k == 0 else tokens
        owner = lax.axis_index("req") ^ k
        rows = normed_ref[:, pl.ds(pl.multiple_of(owner * depth, depth), depth)]
        w_query, w_key, w_value = packed_projection(part, at, depth, width)
        query = query + lax.dot_general(
            w_query, rows, (((0,), (1,)), ((), ())), preferred_element_type=F32
        )
        key = key + jnp.dot(rows, w_key, preferred_element_type=F32)
        value = value + jnp.dot(rows, w_value, preferred_element_type=F32)
    pieces = []
    for head in range(heads_dev):
        own = slice(head * HD, (head + 1) * HD)
        query_ref[head, :HD, :] = query[own, :].astype(BF16)
        query_ref[head, HD:, :] = jnp.zeros((HD, query.shape[1]), BF16)
        pieces += [key[:, own], value[:, own]]
    fresh_ref[...] = jnp.concatenate(pieces, axis=1).astype(BF16)


def cut_kernel(order_ref, cache_ref, *outs):
    kept, given = outs[:-1], outs[-1]
    tokens, cols = kept[0].shape
    core = lax.rem(lax.axis_index("blk"), 2)
    own = pl.ds(pl.multiple_of(core * cols, cols), cols)
    other = pl.ds(pl.multiple_of((1 - core) * cols, cols), cols)
    for k, out in enumerate(kept):
        slot = order_ref[lax.axis_index("req") ^ k]
        out[...] = cache_ref[slot, :, own]
        given[k * tokens : (k + 1) * tokens, :] = cache_ref[slot, :, other]


def cut_cache(cache_in, slot_order):
    count, tokens, cols = cache_in.shape[0], cache_in.shape[1], cache_in.shape[2] // 2
    outs = [shaped((tokens, cols))] * count + [shaped((count * tokens, cols))]
    return local_call(cut_kernel, [slot_order, cache_in], outs, smem=1)


def turn_kernel(count, *refs):
    parts, outs = refs[:count], refs[count:]
    shift = lax.axis_index("req") ^ (lax.axis_index("blk") // 2)
    for case in range(count):

        @pl.when(shift == case)
        def _(case=case):
            for k in range(count):
                outs[k][...] = parts[k ^ case][: outs[k].shape[0], :]


def turn(parts):
    outs = [shaped(parts[0].shape)] * len(parts)
    return local_call(functools.partial(turn_kernel, len(parts)), parts, outs)


def band_kernel(heads_dev, cache_len, widths, order_ref, old_ref, bias_ref, bucket_ref, *refs):
    out_ref, line_ref, row_ref = refs
    head = lax.axis_index("blk") * heads_dev + pl.program_id(0)
    old_len = old_ref[order_ref[lax.axis_index("req")]]
    heads = lax.broadcasted_iota(jnp.int32, bias_ref.shape, 0)
    bias = jnp.sum(jnp.where(heads == head, bias_ref[...], 0.0), axis=0, keepdims=True)
    buckets = bucket_ref[...]
    copies, size = line_ref.shape
    line_ref[:, :cache_len] = jnp.broadcast_to(buckets[:, :1], (copies, cache_len))
    line_ref[:, cache_len:] = jnp.broadcast_to(buckets, (copies, size - cache_len))
    start = 0
    done = 0
    rows = (widths[1] + TILE) // 2
    for width, first in zip(widths, (old_len + 1, cache_len - rows + 1)):
        turned = pltpu.roll(line_ref[...], size - first, 1)[:, : width + TILE]
        row = jnp.zeros(turned.shape, F32)
        for bucket in range(bias_ref.shape[1]):
            row = jnp.where(turned == bucket, bias[:, bucket : bucket + 1], row)
        row_ref[:, start : start + width + TILE] = row
        for u in range(0, width, TILE):
            window = row_ref[0:1, start + u : start + u + 2 * TILE]
            wide = jnp.broadcast_to(window, (TILE, 2 * TILE))
            skewed = pltpu.roll(wide, TILE + 1, 1, stride=1, stride_axis=0)
            out_ref[0, :, done + u : done + u + TILE] = skewed[:, :TILE]
        start += width + TILE
        done += width


def make_band(bucket_of, rel_bias, slot_order, cache_lengths, heads_dev, cache_len, rows):
    widths = (cache_len - TILE + rows, 2 * rows - TILE)
    total = sum(widths)
    return pl.pallas_call(
        functools.partial(band_kernel, heads_dev, cache_len, widths),
        grid=(heads_dev,),
        out_shape=jax.ShapeDtypeStruct((heads_dev, TILE, total), F32),
        in_specs=[SMEM, SMEM, VMEM, VMEM],
        out_specs=pl.BlockSpec((1, TILE, total), lambda h: (h, 0, 0)),
        scratch_shapes=[
            pltpu.VMEM((8, cache_len + bucket_of.shape[0]), jnp.int32),
            pltpu.VMEM((8, total + 2 * TILE), F32),
        ],
        compiler_params=pltpu.CompilerParams(vmem_limit_bytes=12 << 20),
        cost_estimate=pl.CostEstimate(
            flops=8 * heads_dev * TILE * total,
            bytes_accessed=4 * heads_dev * TILE * total,
            transcendentals=0,
        ),
    )(slot_order, cache_lengths, rel_bias.T, bucket_of[None, :])


def self_kernel(cache_len, places, first_call, last_call, *refs):
    order_ref, old_ref, new_ref, query_ref, band_ref = refs[:5]
    count = len(places)
    blocks, refs = refs[5 : 5 + count], refs[5 + count :]
    if first_call:
        fresh_ref, refs = refs[0], refs[1:]
    else:
        (total_in, top_in, norm_in), refs = refs[:3], refs[3:]
    if last_call:
        (kept_ref, given_ref), refs = refs[:2], refs[2:]
    total_ref, top_ref, norm_ref, score_ref = refs
    slot = order_ref[lax.axis_index("req")]
    old_len, new_len = old_ref[slot], new_ref[slot]
    rows = query_ref.shape[2]
    wide_old = cache_len - TILE + rows
    blk = lax.axis_index("blk")

    def attend(keys_values, begin, admit):
        size = keys_values.shape[0]
        top = top_ref[0]
        score_ref[:size, :] = jnp.dot(
            keys_values, query_ref[0], preferred_element_type=F32
        )
        for t in range(0, size, TILE):
            bias = band_ref[0, :, pl.ds(pl.multiple_of(begin - t, TILE), rows)]
            scores = score_ref[t : t + TILE, :] + bias
            scores = jnp.where(admit(t), scores, NEG_FILL)
            score_ref[t : t + TILE, :] = scores
            top = jnp.maximum(top, jnp.max(scores, axis=0, keepdims=True))
        weights = jnp.exp(score_ref[:size, :] - top)
        keep = jnp.exp(top_ref[0] - top)
        norm_ref[0] = norm_ref[0] * keep + jnp.sum(weights, axis=0, keepdims=True)
        term = lax.dot_general(
            keys_values, weights.astype(BF16), (((0,), (0,)), ((), ())),
            preferred_element_type=F32,
        )
        total_ref[0] = total_ref[0] * keep + term
        top_ref[0] = top

    if first_call:
        top_ref[...] = jnp.full(top_ref.shape, NEG_FILL, F32)
        norm_ref[...] = jnp.zeros(norm_ref.shape, F32)
        total_ref[...] = jnp.zeros(total_ref.shape, F32)

        def admit_fresh(t):
            keys = t + lax.broadcasted_iota(jnp.int32, (TILE, rows), 0)
            ids = lax.broadcasted_iota(jnp.int32, (TILE, rows), 1)
            return (keys <= ids) & (keys < new_len)

        attend(fresh_ref[...], wide_old + rows - TILE, admit_fresh)
    else:
        top_ref[...] = top_in[...]
        norm_ref[...] = norm_in[...]
        total_ref[...] = total_in[...]

    for block, place_of in zip(blocks, places):
        first = (blk ^ place_of) * block.shape[0]

        @pl.when(first < old_len)
        def _(block=block, first=first):
            def admit(t):
                keys = first + t + lax.broadcasted_iota(jnp.int32, (TILE, rows), 0)
                return keys < old_len

            attend(block[...], cache_len - TILE - first, admit)

    if last_call:
        total_ref[0, :HD, :] = total_ref[0, HD:, :] / norm_ref[0]
        half = rows // 2
        for out_ref, core in ((kept_ref, lax.rem(blk, 2)), (given_ref, 1 - lax.rem(blk, 2))):
            spot = pl.ds(pl.multiple_of(core * half, half), half)
            out_ref[0] = total_ref[0, :HD, spot].astype(BF16)


def self_attend(lens, query_t, band, blocks, places, cache_len, fresh=None, state=None, last_call=False):
    heads_dev, pair, rows = query_t.shape
    count, tokens = len(blocks), blocks[0].shape[0]
    first_call = state is None
    head_block = lambda *tail: pl.BlockSpec((1,) + tail, lambda h: (h, 0, 0))
    in_specs = [SMEM] * 3 + [
        head_block(pair, rows),
        head_block(TILE, band.shape[2]),
    ] + [pl.BlockSpec((tokens, pair), lambda h: (0, h))] * count
    held = [(pair, rows), (1, rows), (1, rows)]
    score = pltpu.VMEM((max(tokens, rows), rows), F32)
    if first_call:
        in_specs.append(pl.BlockSpec((rows, pair), lambda h: (0, h)))
        more = [fresh]
    else:
        in_specs += [head_block(*shape) for shape in held]
        more = list(state)
    if not last_call:
        out_specs = [head_block(*shape) for shape in held]
        out_shape = [jax.ShapeDtypeStruct((heads_dev,) + shape, F32) for shape in held]
        scratch = [score]
    else:
        out_specs = [head_block(HD, rows // 2)] * 2
        out_shape = [shaped((heads_dev, HD, rows // 2))] * 2
        scratch = [pltpu.VMEM((1,) + shape, F32) for shape in held] + [score]
    keys_all = count * tokens + (rows if first_call else 0)
    return pl.pallas_call(
        functools.partial(self_kernel, cache_len, places, first_call, last_call),
        grid=(heads_dev,),
        in_specs=in_specs,
        out_specs=out_specs,
        out_shape=out_shape,
        scratch_shapes=scratch,
        compiler_params=pltpu.CompilerParams(vmem_limit_bytes=16 << 20),
        cost_estimate=pl.CostEstimate(
            flops=4 * heads_dev * pair * rows * keys_all,
            bytes_accessed=2 * heads_dev * pair * keys_all + 4 * band.size,
            transcendentals=heads_dev * rows * keys_all,
        ),
    )(*lens, query_t, band, *blocks, *more)


def project_out(lefts, weights, skip, depth, owners, partial_ref):
    stride = weights[0].shape[0] // len(owners)
    width = weights[0].shape[1]
    for part, owner in enumerate(owners):
        total = 0.0
        for left, weight in zip(lefts, weights):
            block = weight[part * stride + skip : part * stride + skip + depth, :]
            total = total + lax.dot_general(
                left, block, (((0,), (0,)), ((), ())), preferred_element_type=F32
            )
        partial_ref[:, owner * width : (owner + 1) * width] = total.astype(BF16)


def tail_kernel(skip, *refs):
    parts, out = refs[:-1], refs[-1]
    size = out.shape[0] // len(parts)
    for k, part in enumerate(parts):
        at = skip[0] if k == 0 else skip[1]
        spot = (lax.axis_index("req") ^ k) * size
        out[pl.ds(pl.multiple_of(spot, size), size), :] = part[at : at + size, :]


def self_out_kernel(owners, *refs):
    kept, taken, w_own, w_other = refs[:4]
    outs, partial_ref = refs[4:-1], refs[-1]
    lefts = [kept[...], taken[...]]
    project_out(lefts, (w_own, w_other), 0, kept.shape[0], owners, partial_ref)
    chip = lax.axis_index("blk") // 2
    for k, out in enumerate(outs):
        size = out.shape[0]
        out[...] = partial_ref[pl.ds(pl.multiple_of((chip ^ k) * size, size), size), :]


def sum_rows(parts, residual_ref):
    total = residual_ref[...].astype(F32)
    moved = parts[0][...].astype(F32)
    for part in parts[1:]:
        moved = moved + part[...].astype(F32)
    return total + moved


def norm_rows(total, gain):
    mean_square = jnp.mean(total * total, axis=-1, keepdims=True)
    return (total * lax.rsqrt(mean_square + EPSILON) * gain).astype(BF16)


def query_kernel(owners, count, *refs):
    gain_ref, residual_ref, refs = refs[0], refs[1], refs[2:]
    parts, weights, (total_ref, *outs) = refs[:count], refs[count : count + 2], refs[count + 2 :]
    total = sum_rows(parts, residual_ref)
    total_ref[...] = total
    normed = norm_rows(total, gain_ref[1:2, :])
    depth = normed.shape[1] // len(owners)
    stride = weights[0].shape[0] // len(owners)
    width = outs[0].shape[1] // 2
    for pair in range(count // 2):
        found = []
        for w in weights:
            query = 0.0
            for part, owner in enumerate(owners):
                at = part * stride + pair * depth
                query = query + jnp.dot(
                    normed[:, owner * depth : (owner + 1) * depth],
                    w[at : at + depth, :],
                    preferred_element_type=F32,
                )
            found.append(query)
        for k in range(2):
            own = slice(k * width, (k + 1) * width)
            both = jnp.concatenate([query[:, own] for query in found], axis=1)
            outs[2 * pair + k][...] = both.astype(BF16)


def cross_out_kernel(owners, count, *refs):
    gain_ref, residual_ref, refs = refs[0], refs[1], refs[2:]
    blocks, weights, (total_ref, normed_ref) = (
        refs[:count], refs[count : count + 2], refs[count + 2 :],
    )
    width = blocks[0].shape[1] // 2
    stride = weights[0].shape[0] // len(owners)
    lanes = weights[0].shape[1]
    for part, owner in enumerate(owners):
        total = 0.0
        for i, w in enumerate(weights):
            left = [block[:, i * width : (i + 1) * width] for block in blocks]
            total = total + jnp.dot(
                jnp.concatenate(left, axis=1),
                w[part * stride : part * stride + count * width, :],
                preferred_element_type=F32,
            )
        cols = slice(owner * lanes, (owner + 1) * lanes)
        total_ref[:, cols] = residual_ref[:, cols] + total
    normed_ref[...] = norm_rows(total_ref[...], gain_ref[2:3, :])


def sum_kernel(*refs):
    residual_ref, parts, out_ref = refs[0], refs[1:-1], refs[-1]
    out_ref[...] = sum_rows(parts, residual_ref).astype(BF16)


def fill_rows(blocks, rows_ref):
    for k, block in enumerate(blocks):
        size = block.shape[0]
        rows_ref[k * size : (k + 1) * size, :] = block[...]


def hand_rows(outs, partial_ref):
    for k, out in enumerate(outs):
        size = out.shape[0]
        out[...] = partial_ref[k * size : (k + 1) * size, :]


def pair_kernel(owners, rows_ref, *refs):
    weights, outs = refs[:2], refs[2:]
    width = outs[0].shape[1]
    depth = rows_ref.shape[1] // len(owners)
    for core, weight in enumerate(weights):
        stride = weight.shape[0] // len(owners)
        for i in range(2):
            total = 0.0
            for part, owner in enumerate(owners):
                rows = rows_ref[:, owner * depth : (owner + 1) * depth]
                at = (part + 1) * stride - depth + i * (depth // 2)
                block = stacked(weight[at : at + depth // 2, :], width)
                total = total + jnp.dot(rows, block, preferred_element_type=F32)
            outs[2 * i + core][...] = total.astype(BF16)


def cross_kernel(count, heads_dev, order_ref, enc_ref, *refs):
    blocks, keys, values = refs[:count], refs[count : count + 2], refs[count + 2 : count + 4]
    outs, rows_ref = refs[count + 4 : -1], refs[-1]
    fill_rows(blocks, rows_ref)
    width = heads_dev * HD
    enc_len = enc_ref[order_ref[lax.axis_index("req")]]
    contexts = []
    for core, (key_ref, value_ref) in enumerate(zip(keys, values)):
        query = rows_ref[:, core * width : (core + 1) * width]
        head_of = lax.broadcasted_iota(jnp.int32, query.shape, 1) // HD
        for head in range(heads_dev):
            own_query = jnp.where(head_of == head, query, jnp.zeros_like(query))
            scores = lax.dot_general(
                key_ref[...], own_query, (((1,), (1,)), ((), ())), preferred_element_type=F32
            )
            admitted = lax.broadcasted_iota(jnp.int32, scores.shape, 0) < enc_len
            scores = jnp.where(admitted, scores, NEG_FILL)
            weights = jnp.exp(scores - jnp.max(scores, axis=0, keepdims=True))
            norm = jnp.sum(weights, axis=0, keepdims=True)
            context = lax.dot_general(
                value_ref[...], weights.astype(BF16), (((0,), (0,)), ((), ())),
                preferred_element_type=F32,
            )
            contexts.append(context[head * HD : (head + 1) * HD, :] / norm)
    context = jnp.concatenate(contexts, axis=0).T.astype(BF16)
    for k, out in enumerate(outs):
        size = out.shape[0]
        out[...] = context[k * size : (k + 1) * size, :]


def ffn_kernel(owners_a, owners_b, count, hidden_dev, *refs):
    blocks, weights_a, weights_b = refs[:count], refs[count : count + 2], refs[count + 2 : count + 4]
    outs, (rows_ref, partial_ref) = refs[count + 4 : -2], refs[-2:]
    fill_rows(blocks, rows_ref)
    depth = rows_ref.shape[1] // len(owners_a)
    stride_a = weights_a[0].shape[0] // len(owners_a)
    stride_b = weights_b[0].shape[0] // len(owners_b)
    hiddens = []
    for w_a, w_b in zip(weights_a, weights_b):
        totals = []
        for w, owners, stride, last in (
            (w_a, owners_a, stride_a, stride_a),
            (w_b, owners_b, stride_b, stride_b - hidden_dev),
        ):
            for block in range(last // depth):
                total = 0.0
                for part, owner in enumerate(owners):
                    at = part * stride + block * depth
                    total = total + jnp.dot(
                        rows_ref[:, owner * depth : (owner + 1) * depth],
                        w[at : at + depth, :],
                        preferred_element_type=F32,
                    )
                totals.append(total)
        both = jnp.concatenate(totals, axis=1)
        span = both.shape[1] // 2
        hidden = jax.nn.gelu(both[:, :span], approximate=True) * both[:, span:]
        hiddens.append(hidden[:, :hidden_dev].astype(BF16))
    lanes = weights_b[0].shape[1]
    for part, owner in enumerate(owners_b):
        total = 0.0
        for hidden, w in zip(hiddens, weights_b):
            at = (part + 1) * stride_b - hidden_dev
            total = total + jnp.dot(
                hidden, w[at : at + hidden_dev, :], preferred_element_type=F32
            )
        partial_ref[:, owner * lanes : (owner + 1) * lanes] = total.astype(BF16)
    hand_rows(outs, partial_ref)


def per_device(
    new_states,
    encoder_out,
    cache_in,
    slot_order,
    new_lengths,
    cache_lengths,
    enc_lengths,
    bucket_of,
    rel_bias,
    norm_gain,
    self_q,
    self_kv,
    self_out,
    cross_q,
    cross_kv,
    cross_out,
    ff_in,
    ff_out,
):
    req_count, blk_count = lax.axis_size("req"), lax.axis_size("blk")
    chips = blk_count // 2
    heads_dev = H // blk_count
    width_dev = heads_dev * HD
    rows, width = new_states.shape
    half, share = rows // 2, rows // blk_count
    depth, hidden_dev = self_q.shape[0], ff_in.shape[2]
    up_strides = [1 << i for i in range(req_count.bit_length() - 1)]
    down_strides = up_strides[::-1]
    down_owners = [part_owner(p, down_strides) for p in range(req_count)]

    lanes = 2 * width_dev
    tokens = cache_in.shape[1]
    *kept, given = cut_cache(cache_in, slot_order)
    band = make_band(
        bucket_of, rel_bias, slot_order, cache_lengths, heads_dev, tokens * blk_count, rows
    )
    near_req = [kept[0]] + [xor_send(kept[k], "req", k) for k in range(1, req_count)]
    cross = local_call(
        pack_cross_kernel,
        [after(cross_q, kept[0]), cross_out],
        [shaped((depth // 2 + width_dev, lanes))],
    )[0]
    for step in range(chips.bit_length() - 1):
        cross = place([cross, xor_send(cross, "blk", 2 << step)], lambda k: k)
        cross_first = cross if step == 0 else cross_first
    taken = xor_send(given, "blk", 1)
    skip = depth + depth // 2
    packed_in = [self_q, self_kv, cross_kv, ff_in, self_out, ff_out]
    packed_in[1], packed_in[2] = jnp.moveaxis(self_kv, 1, 0), jnp.moveaxis(cross_kv, 1, 0)
    packed_in[3] = ff_in.transpose(1, 2, 0)
    packed_in[0] = after(packed_in[0], kept[0])
    wide_cols = 2 * TILE * -(-hidden_dev // TILE)
    blocks_in = wide_cols // lanes
    blocks_a = -(-blocks_in // 2)
    first, rest_a, rest_b = local_call(
        pack_kernel,
        packed_in,
        [
            shaped((skip + width_dev, lanes)),
            shaped((depth + blocks_a * depth, lanes)),
            shaped(((blocks_in - blocks_a) * depth + hidden_dev, lanes)),
        ],
        scratch=[pltpu.VMEM((depth, wide_cols), BF16)],
    )

    all_depth = chips * (depth // 2)
    later_a, later_b = local_call(
        functools.partial(weave_kernel, chips),
        [cross, rest_a, rest_b],
        [
            shaped((all_depth + rest_a.shape[0], lanes)),
            shaped((chips * width_dev + rest_b.shape[0], lanes)),
        ],
    )

    joined = shaped((tokens + first.shape[0], taken.shape[1]))
    joined = local_call(
        join_kernel,
        [taken, first],
        [shaped((tokens, taken.shape[1]))] + [joined] * (req_count - 1),
    )
    near = list(turn([after(near_req[0], joined[0], cross_first), *near_req[1:]]))
    far_req = [joined[0]]
    far_req += [
        xor_send(after(joined[k], near[0]), "req", k) for k in range(1, req_count - 1)
    ]
    far_req.append(xor_send(after(joined[-1], near[0], cross), "req", req_count - 1))
    near[1] = after(near[1], far_req[1])
    near = chip_sends(near)
    far = turn([after(far_req[0], band, later_a, *near[1:]), *far_req[1:]])
    far = chip_sends(far)

    def token_order(i):
        here = lax.axis_index("blk")
        return 2 * ((here // 2) ^ (i % chips)) + (lax.rem(here, 2) ^ (i // chips))

    cache_own = place(near + far, token_order)

    w_self_out = local_call(
        functools.partial(tail_kernel, (skip, tokens + skip)),
        [first, *far_req[1:]],
        [shaped((req_count * width_dev, self_out.shape[1]))],
    )[0]
    w_self_out = (w_self_out, xor_send(w_self_out, "blk", 1))

    query_t, fresh, residual = local_call(
        functools.partial(project_kernel, tokens, heads_dev),
        [new_states, norm_gain, first, *far_req[1:]],
        [
            shaped((heads_dev, 2 * HD, rows)),
            shaped((rows, 2 * width_dev)),
            shaped((share, width)),
        ],
        scratch=[pltpu.VMEM((rows, width), BF16)],
        flops=6 * rows * width * width_dev,
    )
    lens = (slot_order, cache_lengths, new_lengths)
    near_places = [2 * k for k in range(chips)]
    far_places = [2 * k + 1 for k in range(chips)]
    cache_len = tokens * blk_count
    state = self_attend(
        lens,
        query_t,
        band,
        [far[0], *reordered(near)],
        [far_places[0], *reordered(near_places)],
        cache_len,
        fresh=fresh,
    )
    moved_a = xor_send(after(later_a, far[0]), "req", up_strides[0])
    moved_b = xor_send(after(later_b, far[0]), "req", down_strides[0])
    w_query, w_wide, w_cross, w_down = req_split(
        [after(later_a, state[0], *reordered(far)[1:]), later_b],
        [moved_a, moved_b],
        [up_strides[0], down_strides[0]],
        [all_depth + depth, chips * width_dev],
    )
    w_query, moved_a = gather_on(w_query, up_strides)
    w_cross, moved_b = gather_on(w_cross, down_strides)
    kept, given = self_attend(
        lens,
        query_t,
        band,
        reordered(far)[1:],
        reordered(far_places)[1:],
        cache_len,
        state=state,
        last_call=True,
    )
    kept, given = kept.reshape(width_dev, half), given.reshape(width_dev, half)

    parts_out = [shaped((share, width))] * chips
    partial_ref = pltpu.VMEM((half, width), BF16)
    parts = local_call(
        functools.partial(self_out_kernel, range(req_count)),
        [kept, xor_send(given, "blk", 1), *w_self_out],
        parts_out,
        scratch=[partial_ref],
        flops=4 * half * width * width_dev,
    )


    parts = chip_sends(parts)
    last = [up_strides[-1], down_strides[-1]]
    w_query, w_cross = req_stack_two(
        [after(w_query, *reordered(parts)[1:]), w_cross], [moved_a, moved_b], last
    )
    w_query = (w_query, xor_send(w_query, "blk", 1))
    w_cross = (w_cross, xor_send(w_cross, "blk", 1))
    residual = after(residual, w_cross[1])
    w_wide, moved_a = gather_on(after(w_wide, *reordered(parts)[1:]), up_strides)
    w_down, moved_b = gather_on(after(w_down, *reordered(parts)[1:]), down_strides)
    total, *queries = local_call(
        functools.partial(query_kernel, range(req_count), chips),
        [norm_gain, residual, *reordered(parts), *w_query],
        [shaped((share, width), F32)] + [shaped((share, lanes))] * chips,
        flops=2 * share * width * width,
    )
    residual = total
    enc_rows = encoder_out.shape[0]
    pairs = local_call(
        functools.partial(pair_kernel, range(req_count)),
        [encoder_out, *w_query],
        [shaped((enc_rows, width_dev))] * 4,
        flops=8 * enc_rows * width * width_dev,
    )
    contexts = local_call(
        functools.partial(cross_kernel, chips, heads_dev),
        [slot_order, enc_lengths, *reordered(chip_sends(queries)), *pairs],
        [shaped((share, lanes))] * chips,
        smem=2,
        scratch=[pltpu.VMEM((half, lanes), BF16)],
        flops=8 * half * width_dev * heads_dev * enc_rows,
        transcendentals=2 * heads_dev * half * enc_rows,
    )
    contexts = chip_sends(restored(contexts))

    residual, normed = local_call(
        functools.partial(cross_out_kernel, down_owners, chips),
        [norm_gain, residual, *contexts, *w_cross],
        [shaped((share, width), F32), shaped((share, width))],
        flops=2 * share * width * width,
    )
    blocks = chip_sends([normed] * chips)
    w_wide, w_down = req_stack_two([after(w_wide, normed), w_down], [moved_a, moved_b], last)
    w_wide = (w_wide, xor_send(w_wide, "blk", 1))
    w_down = (w_down, xor_send(w_down, "blk", 1))

    parts = local_call(
        functools.partial(ffn_kernel, range(req_count), down_owners, chips, hidden_dev),
        [*blocks, *w_wide, *w_down],
        parts_out,
        scratch=[partial_ref, partial_ref],
        flops=12 * half * width * hidden_dev,
        transcendentals=2 * half * hidden_dev,
    )
    final = local_call(
        sum_kernel,
        [residual, *reordered(chip_sends(parts))],
        [shaped((share, width))],
    )[0]

    same = chip_sends([after(final, cache_own)] * chips)
    both = same + [xor_send(part, "blk", 1) for part in same]

    def row_order(i):
        here = lax.axis_index("blk")
        core_at = lax.rem(here, 2) ^ (i // chips)
        return core_at * chips + ((here // 2) ^ (i % chips))

    layer_out = place(both, row_order)
    return (layer_out, cache_own[None])


def solution(mesh):
    in_specs = (
        P("req", None),
        P("req", None),
        P(None, "blk", "req"),
        P(),
        P(),
        P(),
        P(),
        P(),
        P(),
        P(),
        P("req", "blk"),
        P("req", None, "blk"),
        P("blk", "req"),
        P("req", "blk"),
        P("req", None, "blk"),
        P("blk", "req"),
        P("req", None, "blk"),
        P("blk", "req"),
    )
    out_specs = (P("req", None), P("req", None, "blk"))
    return jax.shard_map(
        per_device, mesh=mesh, in_specs=in_specs, out_specs=out_specs, check_vma=False
    )
```

```python
import functools

import jax
import jax.numpy as jnp
from jax import lax
from jax.experimental import pallas as pl
from jax.experimental.pallas import tpu as pltpu
from jax.sharding import PartitionSpec as P

H = 16
HD = 64
EPSILON = 1e-06
NEG_FILL = -1e30
TILE = 128
F32 = jnp.float32
BF16 = jnp.bfloat16


def xor_send(value, axis, step):
    size = lax.axis_size(axis)
    return lax.ppermute(value, axis, [(i, i ^ step) for i in range(size)])


def far_first(count):
    return [0, *range(count // 2, count), *range(1, count // 2)]


def chip_sends(parts):
    moved = [parts[0]] + [None] * (len(parts) - 1)
    for k in far_first(len(parts))[1:]:
        moved[k] = xor_send(parts[k], "blk", 2 * k)
    return moved


def reordered(parts):
    return [parts[k] for k in far_first(len(parts))]


def restored(parts):
    found = [None] * len(parts)
    for part, k in zip(parts, far_first(len(parts))):
        found[k] = part
    return found


VMEM = pl.BlockSpec(memory_space=pltpu.VMEM)
SMEM = pl.BlockSpec(memory_space=pltpu.SMEM)


def local_call(kernel, operands, outs, smem=0, scratch=(), flops=0, transcendentals=0):
    moved = sum(x.size * x.dtype.itemsize for x in list(operands) + list(outs))
    return pl.pallas_call(
        kernel,
        out_shape=list(outs),
        in_specs=[SMEM] * smem + [VMEM] * (len(operands) - smem),
        out_specs=[VMEM] * len(outs),
        scratch_shapes=list(scratch),
        compiler_params=pltpu.CompilerParams(vmem_limit_bytes=8 << 20),
        cost_estimate=pl.CostEstimate(
            flops=flops, bytes_accessed=moved, transcendentals=transcendentals
        ),
    )(*operands)


def shaped(shape, dtype=BF16):
    return jax.ShapeDtypeStruct(tuple(shape), dtype)


def after(value, *others):
    return lax.optimization_barrier((value,) + others)[0]


def place_kernel(order, *refs):
    parts, out = refs[:-1], refs[-1]
    for k, part in enumerate(parts):
        size = part.shape[0]
        out[pl.ds(pl.multiple_of(order(k) * size, size), size), :] = part[...]


def place(parts, order):
    rows, cols = parts[0].shape
    out = shaped((len(parts) * rows, cols))
    return local_call(functools.partial(place_kernel, order), parts, [out])[0]


def stack_order(stride):
    return lambda k: (lax.axis_index("req") // stride) % 2 ^ k


def req_stack(value, moved, stride):
    return place([value, moved], stack_order(stride))


def req_split(values, moved, strides, rows):
    ins, outs = [], []
    for value, other, size in zip(values, moved, rows):
        ins += [value, other]
        outs += [shaped((2 * n, value.shape[1])) for n in (size, value.shape[0] - size)]
    orders = [stack_order(stride) for stride in strides]
    return local_call(functools.partial(split_kernel, orders), ins, outs)


def double_place_kernel(orders, *refs):
    ins, outs = refs[: 2 * len(orders)], refs[2 * len(orders) :]
    for i, order in enumerate(orders):
        place_kernel(order, *ins[2 * i : 2 * i + 2], outs[i])


def req_stack_two(values, moved, strides):
    ins, outs = [], []
    for value, other in zip(values, moved):
        ins += [value, other]
        outs.append(shaped((2 * value.shape[0], value.shape[1])))
    orders = [stack_order(stride) for stride in strides]
    return local_call(functools.partial(double_place_kernel, orders), ins, outs)


def gather_on(value, strides):
    for stride in strides[1:-1]:
        value = req_stack(value, xor_send(value, "req", stride), stride)
    return value, xor_send(value, "req", strides[-1])


def part_owner(part, strides):
    owner = 0
    for i, stride in enumerate(strides):
        owner += stride * ((part >> i) & 1)
    return owner


def pack_projection(query, pair, out, at):
    depth = query.shape[0]
    value = pair[1]
    out[at : at + depth, :] = jnp.concatenate([query[...], pair[0]], axis=1)
    tail = jnp.concatenate([value[: depth // 2], value[depth // 2 :]], axis=1)
    out[at + depth : at + depth + depth // 2, :] = tail


def packed_projection(ref, at, depth, width):
    head = ref[at : at + depth, :]
    tail = ref[at + depth : at + depth + depth // 2, :]
    value = jnp.concatenate([tail[:, :width], tail[:, width:]], axis=0)
    return head[:, :width], head[:, width:], value


def beside(block, width):
    return jnp.concatenate([block[:width], block[width:]], axis=1)


def stacked(block, width):
    return jnp.concatenate([block[:, :width], block[:, width:]], axis=0)


def pack_cross_kernel(query, out, packed):
    depth = query.shape[0]
    packed[: depth // 2, :] = beside(query[...], depth // 2)
    packed[depth // 2 :, :] = out[...]


def pack_kernel(*refs):
    q1, kv1, kv2, ff, o1, o3, first, rest_a, rest_b, wide_ref = refs
    depth, lanes = q1.shape[0], first.shape[1]
    done = depth + depth // 2
    pack_projection(q1, kv1, first, 0)
    first[done:, :] = o1[...]
    rest_a[: depth // 2, :] = beside(kv2[0], depth // 2)
    rest_a[depth // 2 : depth, :] = beside(kv2[1], depth // 2)
    span = wide_ref.shape[1] // 2
    wide_ref[...] = jnp.zeros(wide_ref.shape, wide_ref.dtype)
    for i in range(2):
        block = ff[i].astype(F32).T.astype(BF16)
        wide_ref[:, i * span : i * span + block.shape[1]] = block
    blocks = [wide_ref[:, at : at + lanes] for at in range(0, wide_ref.shape[1], lanes)]
    count_a = rest_a.shape[0] // depth - 1
    for i, block in enumerate(blocks):
        out, at = (rest_a, i + 1) if i < count_a else (rest_b, i - count_a)
        out[at * depth : (at + 1) * depth, :] = block
    rest_b[rest_b.shape[0] - o3.shape[0] :, :] = o3[...]


def weave_kernel(count, all_parts, rest_a, rest_b, out_a, out_b):
    size, width = all_parts.shape[0] // count, all_parts.shape[1] // 2
    parts = [all_parts[k * size : (k + 1) * size, :] for k in range(count)]
    half_depth = size - width
    for k in range(0, count, 2):
        pair = [stacked(part[:half_depth, :], width) for part in parts[k : k + 2]]
        out_a[k * half_depth : (k + 2) * half_depth, :] = jnp.concatenate(pair, axis=1)
    for k, part in enumerate(parts):
        out_b[k * width : (k + 1) * width, :] = part[half_depth:, :]
    out_a[count * half_depth :, :] = rest_a[...]
    out_b[count * width :, :] = rest_b[...]


def split_kernel(orders, *refs):
    ins, outs = refs[: 2 * len(orders)], refs[2 * len(orders) :]
    for i, order in enumerate(orders):
        head, tail = outs[2 * i : 2 * i + 2]
        at = head.shape[0] // 2
        for k, part in enumerate(ins[2 * i : 2 * i + 2]):
            for out, rows in ((head, part[:at, :]), (tail, part[at:, :])):
                size = rows.shape[0]
                out[pl.ds(pl.multiple_of(order(k) * size, size), size), :] = rows


def join_kernel(taken, first, *outs):
    tokens = outs[0].shape[0]
    outs[0][...] = taken[:tokens, :]
    for k, out in enumerate(outs[1:], 1):
        out[:tokens, :] = taken[k * tokens : (k + 1) * tokens, :]
        out[tokens:, :] = first[...]


def project_kernel(tokens, heads_dev, states_ref, gain_ref, first, *refs):
    parts, (query_ref, fresh_ref, share_ref, normed_ref) = refs[:-4], refs[-4:]
    states = states_ref[...].astype(F32)
    mean_square = jnp.mean(states * states, axis=-1, keepdims=True)
    normed = states * lax.rsqrt(mean_square + EPSILON) * gain_ref[0:1, :]
    normed_ref[...] = normed.astype(BF16)
    size = share_ref.shape[0]
    blk = lax.axis_index("blk")
    spot = lax.rem(blk, 2) * (states.shape[0] // (2 * size)) + blk // 2
    share_ref[...] = states_ref[pl.ds(pl.multiple_of(spot * size, size), size), :]
    width = heads_dev * HD
    depth = normed_ref.shape[1] // (1 + len(parts))
    query, key, value = 0.0, 0.0, 0.0
    for k, part in enumerate([first, *parts]):
        at = 0 if k == 0 else tokens
        owner = lax.axis_index("req") ^ k
        rows = normed_ref[:, pl.ds(pl.multiple_of(owner * depth, depth), depth)]
        w_query, w_key, w_value = packed_projection(part, at, depth, width)
        query = query + lax.dot_general(
            w_query, rows, (((0,), (1,)), ((), ())), preferred_element_type=F32
        )
        key = key + jnp.dot(rows, w_key, preferred_element_type=F32)
        value = value + jnp.dot(rows, w_value, preferred_element_type=F32)
    pieces = []
    for head in range(heads_dev):
        own = slice(head * HD, (head + 1) * HD)
        query_ref[head, :HD, :] = query[own, :].astype(BF16)
        query_ref[head, HD:, :] = jnp.zeros((HD, query.shape[1]), BF16)
        pieces += [key[:, own], value[:, own]]
    fresh_ref[...] = jnp.concatenate(pieces, axis=1).astype(BF16)


def cut_kernel(order_ref, cache_ref, *outs):
    kept, given = outs[:-1], outs[-1]
    tokens, cols = kept[0].shape
    core = lax.rem(lax.axis_index("blk"), 2)
    own = pl.ds(pl.multiple_of(core * cols, cols), cols)
    other = pl.ds(pl.multiple_of((1 - core) * cols, cols), cols)
    for k, out in enumerate(kept):
        slot = order_ref[lax.axis_index("req") ^ k]
        out[...] = cache_ref[slot, :, own]
        given[k * tokens : (k + 1) * tokens, :] = cache_ref[slot, :, other]


def cut_cache(cache_in, slot_order):
    count, tokens, cols = cache_in.shape[0], cache_in.shape[1], cache_in.shape[2] // 2
    outs = [shaped((tokens, cols))] * count + [shaped((count * tokens, cols))]
    return local_call(cut_kernel, [slot_order, cache_in], outs, smem=1)


def turn_kernel(count, *refs):
    parts, outs = refs[:count], refs[count:]
    shift = lax.axis_index("req") ^ (lax.axis_index("blk") // 2)
    for case in range(count):

        @pl.when(shift == case)
        def _(case=case):
            for k in range(count):
                outs[k][...] = parts[k ^ case][: outs[k].shape[0], :]


def turn(parts):
    outs = [shaped(parts[0].shape)] * len(parts)
    return local_call(functools.partial(turn_kernel, len(parts)), parts, outs)


def band_kernel(heads_dev, cache_len, widths, order_ref, old_ref, bias_ref, bucket_ref, *refs):
    out_ref, line_ref, row_ref = refs
    head = lax.axis_index("blk") * heads_dev + pl.program_id(0)
    old_len = old_ref[order_ref[lax.axis_index("req")]]
    heads = lax.broadcasted_iota(jnp.int32, bias_ref.shape, 0)
    bias = jnp.sum(jnp.where(heads == head, bias_ref[...], 0.0), axis=0, keepdims=True)
    buckets = bucket_ref[...]
    copies, size = line_ref.shape
    line_ref[:, :cache_len] = jnp.broadcast_to(buckets[:, :1], (copies, cache_len))
    line_ref[:, cache_len:] = jnp.broadcast_to(buckets, (copies, size - cache_len))
    start = 0
    done = 0
    rows = (widths[1] + TILE) // 2
    for width, first in zip(widths, (old_len + 1, cache_len - rows + 1)):
        turned = pltpu.roll(line_ref[...], size - first, 1)[:, : width + TILE]
        row = jnp.zeros(turned.shape, F32)
        for bucket in range(bias_ref.shape[1]):
            row = jnp.where(turned == bucket, bias[:, bucket : bucket + 1], row)
        row_ref[:, start : start + width + TILE] = row
        for u in range(0, width, TILE):
            window = row_ref[0:1, start + u : start + u + 2 * TILE]
            wide = jnp.broadcast_to(window, (TILE, 2 * TILE))
            skewed = pltpu.roll(wide, TILE + 1, 1, stride=1, stride_axis=0)
            out_ref[0, :, done + u : done + u + TILE] = skewed[:, :TILE]
        start += width + TILE
        done += width


def make_band(bucket_of, rel_bias, slot_order, cache_lengths, heads_dev, cache_len, rows):
    widths = (cache_len - TILE + rows, 2 * rows - TILE)
    total = sum(widths)
    return pl.pallas_call(
        functools.partial(band_kernel, heads_dev, cache_len, widths),
        grid=(heads_dev,),
        out_shape=jax.ShapeDtypeStruct((heads_dev, TILE, total), F32),
        in_specs=[SMEM, SMEM, VMEM, VMEM],
        out_specs=pl.BlockSpec((1, TILE, total), lambda h: (h, 0, 0)),
        scratch_shapes=[
            pltpu.VMEM((8, cache_len + bucket_of.shape[0]), jnp.int32),
            pltpu.VMEM((8, total + 2 * TILE), F32),
        ],
        compiler_params=pltpu.CompilerParams(vmem_limit_bytes=12 << 20),
        cost_estimate=pl.CostEstimate(
            flops=8 * heads_dev * TILE * total,
            bytes_accessed=4 * heads_dev * TILE * total,
            transcendentals=0,
        ),
    )(slot_order, cache_lengths, rel_bias.T, bucket_of[None, :])


def self_kernel(cache_len, places, first_call, last_call, *refs):
    order_ref, old_ref, new_ref, query_ref, band_ref = refs[:5]
    count = len(places)
    blocks, refs = refs[5 : 5 + count], refs[5 + count :]
    if first_call:
        fresh_ref, refs = refs[0], refs[1:]
    else:
        (total_in, top_in, norm_in), refs = refs[:3], refs[3:]
    if last_call:
        (kept_ref, given_ref), refs = refs[:2], refs[2:]
    total_ref, top_ref, norm_ref, score_ref = refs
    slot = order_ref[lax.axis_index("req")]
    old_len, new_len = old_ref[slot], new_ref[slot]
    rows = query_ref.shape[2]
    wide_old = cache_len - TILE + rows
    blk = lax.axis_index("blk")

    def attend(keys_values, begin, admit):
        size = keys_values.shape[0]
        top = top_ref[0]
        score_ref[:size, :] = jnp.dot(
            keys_values, query_ref[0], preferred_element_type=F32
        )
        for t in range(0, size, TILE):
            bias = band_ref[0, :, pl.ds(pl.multiple_of(begin - t, TILE), rows)]
            scores = score_ref[t : t + TILE, :] + bias
            if admit is not None:
                scores = jnp.where(admit(t), scores, NEG_FILL)
            score_ref[t : t + TILE, :] = scores
            top = jnp.maximum(top, jnp.max(scores, axis=0, keepdims=True))
        weights = jnp.exp(score_ref[:size, :] - top)
        keep = jnp.exp(top_ref[0] - top)
        norm_ref[0] = norm_ref[0] * keep + jnp.sum(weights, axis=0, keepdims=True)
        term = lax.dot_general(
            keys_values, weights.astype(BF16), (((0,), (0,)), ((), ())),
            preferred_element_type=F32,
        )
        total_ref[0] = total_ref[0] * keep + term
        top_ref[0] = top

    if first_call:
        top_ref[...] = jnp.full(top_ref.shape, NEG_FILL, F32)
        norm_ref[...] = jnp.zeros(norm_ref.shape, F32)
        total_ref[...] = jnp.zeros(total_ref.shape, F32)

        def admit_fresh(t):
            keys = t + lax.broadcasted_iota(jnp.int32, (TILE, rows), 0)
            ids = lax.broadcasted_iota(jnp.int32, (TILE, rows), 1)
            return (keys <= ids) & (keys < new_len)

        attend(fresh_ref[...], wide_old + rows - TILE, admit_fresh)
    else:
        top_ref[...] = top_in[...]
        norm_ref[...] = norm_in[...]
        total_ref[...] = total_in[...]

    for block, place_of in zip(blocks, places):
        first = (blk ^ place_of) * block.shape[0]

        begin = cache_len - TILE - first
        whole = first + block.shape[0] <= old_len

        @pl.when(whole)
        def _(block=block, begin=begin):
            attend(block[...], begin, None)

        @pl.when((first < old_len) & jnp.logical_not(whole))
        def _(block=block, begin=begin, first=first):
            def admit(t):
                keys = first + t + lax.broadcasted_iota(jnp.int32, (TILE, rows), 0)
                return keys < old_len

            attend(block[...], begin, admit)

    if last_call:
        total_ref[0, :HD, :] = total_ref[0, HD:, :] / norm_ref[0]
        half = rows // 2
        for out_ref, core in ((kept_ref, lax.rem(blk, 2)), (given_ref, 1 - lax.rem(blk, 2))):
            spot = pl.ds(pl.multiple_of(core * half, half), half)
            out_ref[0] = total_ref[0, :HD, spot].astype(BF16)


def self_attend(lens, query_t, band, blocks, places, cache_len, fresh=None, state=None, last_call=False):
    heads_dev, pair, rows = query_t.shape
    count, tokens = len(blocks), blocks[0].shape[0]
    first_call = state is None
    head_block = lambda *tail: pl.BlockSpec((1,) + tail, lambda h: (h, 0, 0))
    in_specs = [SMEM] * 3 + [
        head_block(pair, rows),
        head_block(TILE, band.shape[2]),
    ] + [pl.BlockSpec((tokens, pair), lambda h: (0, h))] * count
    held = [(pair, rows), (1, rows), (1, rows)]
    score = pltpu.VMEM((max(tokens, rows), rows), F32)
    if first_call:
        in_specs.append(pl.BlockSpec((rows, pair), lambda h: (0, h)))
        more = [fresh]
    else:
        in_specs += [head_block(*shape) for shape in held]
        more = list(state)
    if not last_call:
        out_specs = [head_block(*shape) for shape in held]
        out_shape = [jax.ShapeDtypeStruct((heads_dev,) + shape, F32) for shape in held]
        scratch = [score]
    else:
        out_specs = [head_block(HD, rows // 2)] * 2
        out_shape = [shaped((heads_dev, HD, rows // 2))] * 2
        scratch = [pltpu.VMEM((1,) + shape, F32) for shape in held] + [score]
    keys_all = count * tokens + (rows if first_call else 0)
    return pl.pallas_call(
        functools.partial(self_kernel, cache_len, places, first_call, last_call),
        grid=(heads_dev,),
        in_specs=in_specs,
        out_specs=out_specs,
        out_shape=out_shape,
        scratch_shapes=scratch,
        compiler_params=pltpu.CompilerParams(vmem_limit_bytes=16 << 20),
        cost_estimate=pl.CostEstimate(
            flops=4 * heads_dev * pair * rows * keys_all,
            bytes_accessed=2 * heads_dev * pair * keys_all + 4 * band.size,
            transcendentals=heads_dev * rows * keys_all,
        ),
    )(*lens, query_t, band, *blocks, *more)


def project_out(lefts, weights, skip, depth, owners, partial_ref):
    stride = weights[0].shape[0] // len(owners)
    width = weights[0].shape[1]
    for part, owner in enumerate(owners):
        total = 0.0
        for left, weight in zip(lefts, weights):
            block = weight[part * stride + skip : part * stride + skip + depth, :]
            total = total + lax.dot_general(
                left, block, (((0,), (0,)), ((), ())), preferred_element_type=F32
            )
        partial_ref[:, owner * width : (owner + 1) * width] = total.astype(BF16)


def tail_kernel(skip, *refs):
    parts, out = refs[:-1], refs[-1]
    size = out.shape[0] // len(parts)
    for k, part in enumerate(parts):
        at = skip[0] if k == 0 else skip[1]
        spot = (lax.axis_index("req") ^ k) * size
        out[pl.ds(pl.multiple_of(spot, size), size), :] = part[at : at + size, :]


def self_out_kernel(owners, *refs):
    kept, taken, w_own, w_other = refs[:4]
    outs, partial_ref = refs[4:-1], refs[-1]
    lefts = [kept[...], taken[...]]
    project_out(lefts, (w_own, w_other), 0, kept.shape[0], owners, partial_ref)
    chip = lax.axis_index("blk") // 2
    for k, out in enumerate(outs):
        size = out.shape[0]
        out[...] = partial_ref[pl.ds(pl.multiple_of((chip ^ k) * size, size), size), :]


def sum_rows(parts, residual_ref):
    total = residual_ref[...].astype(F32)
    moved = parts[0][...].astype(F32)
    for part in parts[1:]:
        moved = moved + part[...].astype(F32)
    return total + moved


def norm_rows(total, gain):
    mean_square = jnp.mean(total * total, axis=-1, keepdims=True)
    return (total * lax.rsqrt(mean_square + EPSILON) * gain).astype(BF16)


def query_kernel(owners, count, *refs):
    gain_ref, residual_ref, refs = refs[0], refs[1], refs[2:]
    parts, weights, (total_ref, *outs) = refs[:count], refs[count : count + 2], refs[count + 2 :]
    total = sum_rows(parts, residual_ref)
    total_ref[...] = total
    normed = norm_rows(total, gain_ref[1:2, :])
    depth = normed.shape[1] // len(owners)
    stride = weights[0].shape[0] // len(owners)
    width = outs[0].shape[1] // 2
    for pair in range(count // 2):
        found = []
        for w in weights:
            query = 0.0
            for part, owner in enumerate(owners):
                at = part * stride + pair * depth
                query = query + jnp.dot(
                    normed[:, owner * depth : (owner + 1) * depth],
                    w[at : at + depth, :],
                    preferred_element_type=F32,
                )
            found.append(query)
        for k in range(2):
            own = slice(k * width, (k + 1) * width)
            both = jnp.concatenate([query[:, own] for query in found], axis=1)
            outs[2 * pair + k][...] = both.astype(BF16)


def cross_out_kernel(owners, count, *refs):
    gain_ref, residual_ref, refs = refs[0], refs[1], refs[2:]
    blocks, weights, (total_ref, normed_ref) = (
        refs[:count], refs[count : count + 2], refs[count + 2 :],
    )
    width = blocks[0].shape[1] // 2
    stride = weights[0].shape[0] // len(owners)
    lanes = weights[0].shape[1]
    for part, owner in enumerate(owners):
        total = 0.0
        for i, w in enumerate(weights):
            left = [block[:, i * width : (i + 1) * width] for block in blocks]
            total = total + jnp.dot(
                jnp.concatenate(left, axis=1),
                w[part * stride : part * stride + count * width, :],
                preferred_element_type=F32,
            )
        cols = slice(owner * lanes, (owner + 1) * lanes)
        total_ref[:, cols] = residual_ref[:, cols] + total
    normed_ref[...] = norm_rows(total_ref[...], gain_ref[2:3, :])


def sum_kernel(*refs):
    residual_ref, parts, out_ref = refs[0], refs[1:-1], refs[-1]
    out_ref[...] = sum_rows(parts, residual_ref).astype(BF16)


def fill_rows(blocks, rows_ref):
    for k, block in enumerate(blocks):
        size = block.shape[0]
        rows_ref[k * size : (k + 1) * size, :] = block[...]


def hand_rows(outs, partial_ref):
    for k, out in enumerate(outs):
        size = out.shape[0]
        out[...] = partial_ref[k * size : (k + 1) * size, :]


def pair_kernel(owners, rows_ref, *refs):
    weights, outs = refs[:2], refs[2:]
    width = outs[0].shape[1]
    depth = rows_ref.shape[1] // len(owners)
    for core, weight in enumerate(weights):
        stride = weight.shape[0] // len(owners)
        for i in range(2):
            total = 0.0
            for part, owner in enumerate(owners):
                rows = rows_ref[:, owner * depth : (owner + 1) * depth]
                at = (part + 1) * stride - depth + i * (depth // 2)
                block = stacked(weight[at : at + depth // 2, :], width)
                total = total + jnp.dot(rows, block, preferred_element_type=F32)
            outs[2 * i + core][...] = total.astype(BF16)


def cross_kernel(count, heads_dev, order_ref, enc_ref, *refs):
    blocks, keys, values = refs[:count], refs[count : count + 2], refs[count + 2 : count + 4]
    outs, rows_ref = refs[count + 4 : -1], refs[-1]
    fill_rows(blocks, rows_ref)
    width = heads_dev * HD
    enc_len = enc_ref[order_ref[lax.axis_index("req")]]
    contexts = []
    for core, (key_ref, value_ref) in enumerate(zip(keys, values)):
        query = rows_ref[:, core * width : (core + 1) * width]
        head_of = lax.broadcasted_iota(jnp.int32, query.shape, 1) // HD
        for head in range(heads_dev):
            own_query = jnp.where(head_of == head, query, jnp.zeros_like(query))
            scores = lax.dot_general(
                key_ref[...], own_query, (((1,), (1,)), ((), ())), preferred_element_type=F32
            )
            admitted = lax.broadcasted_iota(jnp.int32, scores.shape, 0) < enc_len
            scores = jnp.where(admitted, scores, NEG_FILL)
            weights = jnp.exp(scores - jnp.max(scores, axis=0, keepdims=True))
            norm = jnp.sum(weights, axis=0, keepdims=True)
            context = lax.dot_general(
                value_ref[...], weights.astype(BF16), (((0,), (0,)), ((), ())),
                preferred_element_type=F32,
            )
            contexts.append(context[head * HD : (head + 1) * HD, :] / norm)
    context = jnp.concatenate(contexts, axis=0).T.astype(BF16)
    for k, out in enumerate(outs):
        size = out.shape[0]
        out[...] = context[k * size : (k + 1) * size, :]


def ffn_kernel(owners_a, owners_b, count, hidden_dev, *refs):
    blocks, weights_a, weights_b = refs[:count], refs[count : count + 2], refs[count + 2 : count + 4]
    outs, (rows_ref, partial_ref) = refs[count + 4 : -2], refs[-2:]
    fill_rows(blocks, rows_ref)
    depth = rows_ref.shape[1] // len(owners_a)
    stride_a = weights_a[0].shape[0] // len(owners_a)
    stride_b = weights_b[0].shape[0] // len(owners_b)
    hiddens = []
    for w_a, w_b in zip(weights_a, weights_b):
        totals = []
        for w, owners, stride, last in (
            (w_a, owners_a, stride_a, stride_a),
            (w_b, owners_b, stride_b, stride_b - hidden_dev),
        ):
            for block in range(last // depth):
                total = 0.0
                for part, owner in enumerate(owners):
                    at = part * stride + block * depth
                    total = total + jnp.dot(
                        rows_ref[:, owner * depth : (owner + 1) * depth],
                        w[at : at + depth, :],
                        preferred_element_type=F32,
                    )
                totals.append(total)
        both = jnp.concatenate(totals, axis=1)
        span = both.shape[1] // 2
        hidden = jax.nn.gelu(both[:, :span], approximate=True) * both[:, span:]
        hiddens.append(hidden[:, :hidden_dev].astype(BF16))
    lanes = weights_b[0].shape[1]
    for part, owner in enumerate(owners_b):
        total = 0.0
        for hidden, w in zip(hiddens, weights_b):
            at = (part + 1) * stride_b - hidden_dev
            total = total + jnp.dot(
                hidden, w[at : at + hidden_dev, :], preferred_element_type=F32
            )
        partial_ref[:, owner * lanes : (owner + 1) * lanes] = total.astype(BF16)
    hand_rows(outs, partial_ref)


def per_device(
    new_states,
    encoder_out,
    cache_in,
    slot_order,
    new_lengths,
    cache_lengths,
    enc_lengths,
    bucket_of,
    rel_bias,
    norm_gain,
    self_q,
    self_kv,
    self_out,
    cross_q,
    cross_kv,
    cross_out,
    ff_in,
    ff_out,
):
    req_count, blk_count = lax.axis_size("req"), lax.axis_size("blk")
    chips = blk_count // 2
    heads_dev = H // blk_count
    width_dev = heads_dev * HD
    rows, width = new_states.shape
    half, share = rows // 2, rows // blk_count
    depth, hidden_dev = self_q.shape[0], ff_in.shape[2]
    up_strides = [1 << i for i in range(req_count.bit_length() - 1)]
    down_strides = up_strides[::-1]
    down_owners = [part_owner(p, down_strides) for p in range(req_count)]

    lanes = 2 * width_dev
    tokens = cache_in.shape[1]
    *kept, given = cut_cache(cache_in, slot_order)
    band = make_band(
        bucket_of, rel_bias, slot_order, cache_lengths, heads_dev, tokens * blk_count, rows
    )
    near_req = [kept[0]] + [xor_send(kept[k], "req", k) for k in range(1, req_count)]
    cross = local_call(
        pack_cross_kernel,
        [after(cross_q, kept[0]), cross_out],
        [shaped((depth // 2 + width_dev, lanes))],
    )[0]
    for step in range(chips.bit_length() - 1):
        cross = place([cross, xor_send(cross, "blk", 2 << step)], lambda k: k)
        cross_first = cross if step == 0 else cross_first
    taken = xor_send(given, "blk", 1)
    skip = depth + depth // 2
    packed_in = [self_q, self_kv, cross_kv, ff_in, self_out, ff_out]
    packed_in[1], packed_in[2] = jnp.moveaxis(self_kv, 1, 0), jnp.moveaxis(cross_kv, 1, 0)
    packed_in[3] = ff_in.transpose(1, 2, 0)
    packed_in[0] = after(packed_in[0], kept[0])
    wide_cols = 2 * TILE * -(-hidden_dev // TILE)
    blocks_in = wide_cols // lanes
    blocks_a = -(-blocks_in // 2)
    first, rest_a, rest_b = local_call(
        pack_kernel,
        packed_in,
        [
            shaped((skip + width_dev, lanes)),
            shaped((depth + blocks_a * depth, lanes)),
            shaped(((blocks_in - blocks_a) * depth + hidden_dev, lanes)),
        ],
        scratch=[pltpu.VMEM((depth, wide_cols), BF16)],
    )

    all_depth = chips * (depth // 2)
    later_a, later_b = local_call(
        functools.partial(weave_kernel, chips),
        [cross, rest_a, rest_b],
        [
            shaped((all_depth + rest_a.shape[0], lanes)),
            shaped((chips * width_dev + rest_b.shape[0], lanes)),
        ],
    )

    joined = shaped((tokens + first.shape[0], taken.shape[1]))
    joined = local_call(
        join_kernel,
        [taken, first],
        [shaped((tokens, taken.shape[1]))] + [joined] * (req_count - 1),
    )
    near = list(turn([after(near_req[0], joined[0], cross_first), *near_req[1:]]))
    far_req = [joined[0]]
    far_req += [
        xor_send(after(joined[k], near[0]), "req", k) for k in range(1, req_count - 1)
    ]
    far_req.append(xor_send(after(joined[-1], near[0], cross), "req", req_count - 1))
    near[1] = after(near[1], far_req[1])
    near = chip_sends(near)
    far = turn([after(far_req[0], band, later_a, *near[1:]), *far_req[1:]])
    far = chip_sends(far)

    def token_order(i):
        here = lax.axis_index("blk")
        return 2 * ((here // 2) ^ (i % chips)) + (lax.rem(here, 2) ^ (i // chips))

    cache_own = place(near + far, token_order)

    w_self_out = local_call(
        functools.partial(tail_kernel, (skip, tokens + skip)),
        [first, *far_req[1:]],
        [shaped((req_count * width_dev, self_out.shape[1]))],
    )[0]
    w_self_out = (w_self_out, xor_send(w_self_out, "blk", 1))

    query_t, fresh, residual = local_call(
        functools.partial(project_kernel, tokens, heads_dev),
        [new_states, norm_gain, first, *far_req[1:]],
        [
            shaped((heads_dev, 2 * HD, rows)),
            shaped((rows, 2 * width_dev)),
            shaped((share, width)),
        ],
        scratch=[pltpu.VMEM((rows, width), BF16)],
        flops=6 * rows * width * width_dev,
    )
    lens = (slot_order, cache_lengths, new_lengths)
    near_places = [2 * k for k in range(chips)]
    far_places = [2 * k + 1 for k in range(chips)]
    cache_len = tokens * blk_count
    state = self_attend(
        lens,
        query_t,
        band,
        [far[0], *reordered(near)],
        [far_places[0], *reordered(near_places)],
        cache_len,
        fresh=fresh,
    )
    moved_a = xor_send(after(later_a, far[0]), "req", up_strides[0])
    moved_b = xor_send(after(later_b, far[0]), "req", down_strides[0])
    w_query, w_wide, w_cross, w_down = req_split(
        [after(later_a, state[0], *reordered(far)[1:]), later_b],
        [moved_a, moved_b],
        [up_strides[0], down_strides[0]],
        [all_depth + depth, chips * width_dev],
    )
    w_query, moved_a = gather_on(w_query, up_strides)
    w_cross, moved_b = gather_on(w_cross, down_strides)
    kept, given = self_attend(
        lens,
        query_t,
        band,
        reordered(far)[1:],
        reordered(far_places)[1:],
        cache_len,
        state=state,
        last_call=True,
    )
    kept, given = kept.reshape(width_dev, half), given.reshape(width_dev, half)

    parts_out = [shaped((share, width))] * chips
    partial_ref = pltpu.VMEM((half, width), BF16)
    parts = local_call(
        functools.partial(self_out_kernel, range(req_count)),
        [kept, xor_send(given, "blk", 1), *w_self_out],
        parts_out,
        scratch=[partial_ref],
        flops=4 * half * width * width_dev,
    )


    parts = chip_sends(parts)
    last = [up_strides[-1], down_strides[-1]]
    w_query, w_cross = req_stack_two(
        [after(w_query, *reordered(parts)[1:]), w_cross], [moved_a, moved_b], last
    )
    w_query = (w_query, xor_send(w_query, "blk", 1))
    w_cross = (w_cross, xor_send(w_cross, "blk", 1))
    residual = after(residual, w_cross[1])
    w_wide, moved_a = gather_on(after(w_wide, *reordered(parts)[1:]), up_strides)
    w_down, moved_b = gather_on(after(w_down, *reordered(parts)[1:]), down_strides)
    total, *queries = local_call(
        functools.partial(query_kernel, range(req_count), chips),
        [norm_gain, residual, *reordered(parts), *w_query],
        [shaped((share, width), F32)] + [shaped((share, lanes))] * chips,
        flops=2 * share * width * width,
    )
    residual = total
    enc_rows = encoder_out.shape[0]
    pairs = local_call(
        functools.partial(pair_kernel, range(req_count)),
        [encoder_out, *w_query],
        [shaped((enc_rows, width_dev))] * 4,
        flops=8 * enc_rows * width * width_dev,
    )
    contexts = local_call(
        functools.partial(cross_kernel, chips, heads_dev),
        [slot_order, enc_lengths, *reordered(chip_sends(queries)), *pairs],
        [shaped((share, lanes))] * chips,
        smem=2,
        scratch=[pltpu.VMEM((half, lanes), BF16)],
        flops=8 * half * width_dev * heads_dev * enc_rows,
        transcendentals=2 * heads_dev * half * enc_rows,
    )
    contexts = chip_sends(restored(contexts))

    residual, normed = local_call(
        functools.partial(cross_out_kernel, down_owners, chips),
        [norm_gain, residual, *contexts, *w_cross],
        [shaped((share, width), F32), shaped((share, width))],
        flops=2 * share * width * width,
    )
    blocks = chip_sends([normed] * chips)
    w_wide, w_down = req_stack_two([after(w_wide, normed), w_down], [moved_a, moved_b], last)
    w_wide = (w_wide, xor_send(w_wide, "blk", 1))
    w_down = (w_down, xor_send(w_down, "blk", 1))

    parts = local_call(
        functools.partial(ffn_kernel, range(req_count), down_owners, chips, hidden_dev),
        [*blocks, *w_wide, *w_down],
        parts_out,
        scratch=[partial_ref, partial_ref],
        flops=12 * half * width * hidden_dev,
        transcendentals=2 * half * hidden_dev,
    )
    final = local_call(
        sum_kernel,
        [residual, *reordered(chip_sends(parts))],
        [shaped((share, width))],
    )[0]

    same = chip_sends([after(final, cache_own)] * chips)
    both = same + [xor_send(part, "blk", 1) for part in same]

    def row_order(i):
        here = lax.axis_index("blk")
        core_at = lax.rem(here, 2) ^ (i // chips)
        return core_at * chips + ((here // 2) ^ (i % chips))

    layer_out = place(both, row_order)
    return (layer_out, cache_own[None])


def solution(mesh):
    in_specs = (
        P("req", None),
        P("req", None),
        P(None, "blk", "req"),
        P(),
        P(),
        P(),
        P(),
        P(),
        P(),
        P(),
        P("req", "blk"),
        P("req", None, "blk"),
        P("blk", "req"),
        P("req", "blk"),
        P("req", None, "blk"),
        P("blk", "req"),
        P("req", None, "blk"),
        P("blk", "req"),
    )
    out_specs = (P("req", None), P("req", None, "blk"))
    return jax.shard_map(
        per_device, mesh=mesh, in_specs=in_specs, out_specs=out_specs, check_vma=False
    )
```
